32 devices in a mesh: pipe: 4 (over y, x), ctx: 4 (over z), tp: 2 (over core).
Axes of the slice: x: 2, y: 2, z: 4, core: 2. Of those that a mesh axis runs over, the one named last changes fastest.
Arguments:
- q_self: bfloat16 [4, 1024, 4096], P('pipe', 'ctx', 'tp'), may hold values from -5 to 5
- kv_self: bfloat16 [4, 1024, 2, 512], P('pipe', 'ctx', None, 'tp'), may hold values from -5 to 5
- q_cross: bfloat16 [4, 1024, 4096], P('pipe', 'ctx', 'tp'), may hold values from -5 to 5
- kv_cross: bfloat16 [4, 2, 1024, 2, 512], P(None, None, ('pipe', 'ctx'), None, 'tp'), may hold values from -5 to 5
- sample_lengths: int32 [4, 8], P('pipe'), may hold values from 1 to 640, 1024 in all within a row
- sample_image: int32 [4, 8], P('pipe'), may hold values from 0 to 1
Outputs:
- self_out: bfloat16 [4, 1024, 4096], P('pipe', 'ctx', 'tp')
- cross_out: bfloat16 [4, 1024, 4096], P('pipe', 'ctx', 'tp')
The draws below stay inside these ranges and needn't reach their ends.
Inputs may be any that keep to these rules, and one draw needn't show every extreme that they name: `sample_lengths`: each micro-batch's lengths sum to 1024; the longest sample of each micro-batch has exactly 640 positions.
All inputs are finite; a program needn't handle non-finite values.
Results may differ from the reference program's by a relative error of at most 0.0047.
Values may be sent and summed in bfloat16 or wider, within the bound.
No kernel may reach another device: no remote copies, remote signals or barrier semaphores. Data moves between devices by JAX's collectives and lax.ppermute only.
A program may use at most 128 MiB of HBM per device.

```python
import math
import jax
import jax.numpy as jnp
import numpy as np
from jax import lax

HD = 128
QH = 32
KVH = 4
IMAGES = 2
PATCH = 1024
SAMPLES = 8
LEN = 1024
MOST = 640
N_PIPE = 4


def drawn_normal(key, shape, salt):
    seeded = jax.random.fold_in(key, salt)
    return jnp.clip(jax.random.normal(jax.random.fold_in(seeded, 1), shape, jnp.float32), -4.0, 4.0)


def draw_q_self(key, part):
    return drawn_normal(key, (N_PIPE, LEN, QH * HD), 7).astype(jnp.bfloat16)


def draw_q_cross(key, part):
    return drawn_normal(key, (N_PIPE, LEN, QH * HD), 11).astype(jnp.bfloat16)


def draw_kv_self(key, part):
    shape = (N_PIPE, LEN, 2, KVH * HD)
    return drawn_normal(key, shape, 13).astype(jnp.bfloat16)


def draw_kv_cross(key, part):
    shape = (N_PIPE, IMAGES, PATCH, 2, KVH * HD)
    return drawn_normal(key, shape, 17).astype(jnp.bfloat16)


def place_ends(entries, rng, smallest, high):
    extent = entries.shape
    index_at = [jax.random.randint(jax.random.fold_in(rng, axis), (), 0, extent[axis]) for axis in range(len(extent))]
    entries = entries.at[tuple(index_at)].set(smallest)
    longest = extent.index(max(extent))
    index_at[longest] = (index_at[longest] + 1) % extent[longest]
    return entries.at[tuple(index_at)].set(high)


def profile(count, total, most, lean):
    loads = [(1 << 20) // math.isqrt(standing ** lean) + 1 for standing in range(2, count + 1)]
    rest, holding = total - most - (count - 1), [1] * (count - 1)
    while rest > 0:
        candidates = [i for i in range(count - 1) if holding[i] < most]
        mass, left = sum([loads[i] for i in candidates]), rest
        for i in candidates:
            more = min(most - holding[i], max(1, left * loads[i] // mass), rest)
            holding[i] = holding[i] + more
            rest = rest - more
    return np.array([most] + holding)


def uneven_parts(key, number_of, total, most, skew):
    if number_of == 2:
        one = jax.random.randint(key, (), max(1, total - most), min(most, total - 1) + 1)
        return jnp.stack([one, total - one])
    tallies = jnp.asarray(profile(number_of, total, most, skew), jnp.int32)
    couples = (number_of - 1) // 2
    source_of, taker = tallies[1:1 + 2 * couples:2], tallies[2:2 + 2 * couples:2]
    room = jnp.minimum(source_of - 1, most - taker)
    passed = jax.random.randint(jax.random.fold_in(key, 1), (couples,), 0, 1 << 20) % (room + 1)
    tallies = tallies.at[1:1 + 2 * couples:2].set(source_of - passed).at[2:2 + 2 * couples:2].set(taker + passed)
    return tallies[jax.random.permutation(jax.random.fold_in(key, 2), number_of)]


def setup_inputs(seed: int = 0) -> dict:
    key_list = jax.random.split(jax.random.key(seed), 7)
    return {
        "q_self": draw_q_self(jax.random.fold_in(key_list[6], 71), 0),
        "kv_self": draw_kv_self(jax.random.fold_in(key_list[6], 71), 0),
        "q_cross": draw_q_cross(jax.random.fold_in(key_list[6], 71), 0),
        "kv_cross": draw_kv_cross(jax.random.fold_in(key_list[6], 71), 0),
        "sample_lengths": jax.vmap(lambda own: uneven_parts(own, SAMPLES, LEN, MOST, 2))(jax.random.split(key_list[4], N_PIPE)).reshape((N_PIPE, SAMPLES)).astype(jnp.int32),
        "sample_image": place_ends(jax.random.randint(key_list[5], (N_PIPE, SAMPLES), 0, IMAGES), jax.random.fold_in(key_list[5], 1), 0, IMAGES - 1).astype(jnp.int32),
    }


def sample_of(sample_ends, positions):
    return lax.optimization_barrier(jnp.sum((positions[:, None] >= sample_ends[None, :]).astype(jnp.int32), axis=1)).astype(jnp.int32)

def heads_first(matrix, head_count):
    return matrix.astype(jnp.float32).reshape(matrix.shape[0], head_count, HD).transpose(1, 0, 2)

def masked_attention(queries, key_rows, value_rows, permitted, score_scale):

    def one_head(operands):
        query, key_head, value_head = operands
        scores = jnp.dot(query, key_head.T, precision=lax.Precision.HIGHEST) * score_scale
        scores = jnp.where(permitted, scores, -jnp.inf)
        row_max = lax.optimization_barrier(jnp.max(scores, axis=1, keepdims=True))
        weights = jnp.exp(scores - row_max)
        weight_sum = lax.optimization_barrier(jnp.sum(weights, axis=1, keepdims=True))
        rounded = lax.optimization_barrier(weights.astype(jnp.bfloat16)).astype(jnp.float32)
        return jnp.dot(rounded, value_head, precision=lax.Precision.HIGHEST) / weight_sum
    return lax.map(one_head, (queries, key_rows, value_rows))

def reference(q_self, kv_self, q_cross, kv_cross, sample_lengths, sample_image):
    score_scale = 1.0 / math.sqrt(HD)
    group = QH // KVH
    positions = jnp.arange(LEN, dtype=jnp.int32)
    patch_image = (jnp.arange(IMAGES * PATCH, dtype=jnp.int32) // PATCH).astype(jnp.int32)
    self_parts = []
    cross_parts = []
    for segment_index in range(N_PIPE):
        sample_ends = jnp.cumsum(sample_lengths[segment_index]).astype(jnp.int32)
        own_samples = sample_of(sample_ends, positions)
        matches = own_samples[:, None] == jnp.arange(SAMPLES, dtype=jnp.int32)[None, :]
        token_image = lax.optimization_barrier(jnp.sum(jnp.where(matches, sample_image[segment_index][None, :], 0), axis=1)).astype(jnp.int32)
        permitted = (positions[None, :] <= positions[:, None]) & (own_samples[None, :] == own_samples[:, None])
        queries = heads_first(q_self[segment_index], QH)
        key_rows = jnp.repeat(heads_first(kv_self[segment_index, :, 0], KVH), group, axis=0)
        value_rows = jnp.repeat(heads_first(kv_self[segment_index, :, 1], KVH), group, axis=0)
        mixed = masked_attention(queries, key_rows, value_rows, permitted, score_scale)
        self_parts.append(mixed.transpose(1, 0, 2).reshape(LEN, QH * HD).astype(jnp.bfloat16))
        image_rows = kv_cross[segment_index].reshape(IMAGES * PATCH, 2, KVH * HD)
        cross_permitted = token_image[:, None] == patch_image[None, :]
        queries = heads_first(q_cross[segment_index], QH)
        key_rows = jnp.repeat(heads_first(image_rows[:, 0], KVH), group, axis=0)
        value_rows = jnp.repeat(heads_first(image_rows[:, 1], KVH), group, axis=0)
        mixed = masked_attention(queries, key_rows, value_rows, cross_permitted, score_scale)
        cross_parts.append(mixed.transpose(1, 0, 2).reshape(LEN, QH * HD).astype(jnp.bfloat16))
    return (jnp.stack(self_parts), jnp.stack(cross_parts))
```

```python
import functools
import math

import jax
import jax.numpy as jnp
from jax import lax
from jax.experimental import pallas as pl
from jax.experimental.pallas import tpu as pltpu
from jax.sharding import PartitionSpec as P

HD = 128
TILE = 32
LOW = -1e30
EXP_SCALE = math.log2(math.e) / math.sqrt(HD)
NT = (((1,), (1,)), ((), ()))


def sample_bounds(lengths_ref, count):
    starts, ends, total = [], [], jnp.int32(0)
    for j in range(count):
        starts.append(total)
        total = total + lengths_ref[0, j]
        ends.append(total)
    return starts, ends


def stack_heads(q_ref, g, group):
    first = g * group
    return jnp.concatenate(
        [q_ref[:, (first + h) * HD : (first + h + 1) * HD] for h in range(group)], axis=0
    )


def write_heads(out_ref, rows, g, group):
    for h in range(group):
        at = (g * group + h) * HD
        out_ref[:, at : at + HD] = rows[h * TILE : (h + 1) * TILE].astype(out_ref.dtype)


def absorb(state, scores, values):
    top, total, mixed = state
    new_top = top
    for s in scores:
        new_top = jnp.maximum(new_top, jnp.max(s, axis=1, keepdims=True))
    decay = jnp.exp2((top - new_top) * EXP_SCALE)
    total = total * decay
    mixed = mixed * decay
    for s, v in zip(scores, values):
        w = jnp.exp2((s - new_top) * EXP_SCALE)
        total = total + jnp.sum(w, axis=1, keepdims=True)
        mixed = mixed + jnp.dot(w.astype(jnp.bfloat16), v, preferred_element_type=jnp.float32)
    return new_top, total, mixed


def self_kernel(lengths_ref, place_ref, q_ref, *refs, kv_heads, group, spans, rows_here, samples):
    pieces, out_ref = refs[: len(spans)], refs[len(spans)]
    top_ref, total_ref, mixed_ref = refs[len(spans) + 1 :]
    base = place_ref[0] * rows_here
    first = base + pl.program_id(0) * TILE
    starts, ends = sample_bounds(lengths_ref, samples)
    lowest = jnp.int32(0)
    for e in ends:
        lowest = jnp.where(e <= first, e, lowest)
    height = group * TILE
    row_t = first + (lax.broadcasted_iota(jnp.int32, (height, 1), 0) & (TILE - 1))
    row_start = jnp.zeros((height, 1), jnp.int32)
    for e in ends:
        row_start = jnp.where(e <= row_t, e, row_start)

    top_ref[...] = jnp.full_like(top_ref, LOW)
    total_ref[...] = jnp.zeros_like(total_ref)
    mixed_ref[...] = jnp.zeros_like(mixed_ref)

    for number, (back, count) in enumerate(spans):
        piece_end = base - (back - 1) * rows_here
        piece_start = piece_end - count

        def work(piece_ref=pieces[number], piece_start=piece_start, count=count):
            key_t = piece_start + lax.broadcasted_iota(jnp.int32, (1, count), 1)
            allowed = (key_t >= row_start) & (key_t <= row_t)
            for g in range(kv_heads):
                q = stack_heads(q_ref, g, group)
                k = piece_ref[:, g * HD : (g + 1) * HD]
                v = piece_ref[:, (kv_heads + g) * HD : (kv_heads + g + 1) * HD]
                s = lax.dot_general(q, k, NT, preferred_element_type=jnp.float32)
                s = jnp.where(allowed, s, LOW)
                top, total, mixed = top_ref[g], total_ref[g], mixed_ref[g]
                new_top = jnp.maximum(top, jnp.max(s, axis=1, keepdims=True))
                decay = jnp.exp2((top - new_top) * EXP_SCALE)
                w = jnp.where(allowed, jnp.exp2((s - new_top) * EXP_SCALE), 0.0)
                top_ref[g] = new_top
                total_ref[g] = total * decay + jnp.sum(w, axis=1, keepdims=True)
                mixed_ref[g] = mixed * decay + jnp.dot(
                    w.astype(jnp.bfloat16), v, preferred_element_type=jnp.float32
                )

        if back == 0:
            work()
        else:
            pl.when((piece_start >= 0) & (lowest < piece_end))(work)

    for g in range(kv_heads):
        write_heads(out_ref, mixed_ref[g] / total_ref[g], g, group)


def cross_kernel(
    lengths_ref, images_ref, place_ref, q_ref, *refs,
    kv_heads, group, choices, rows_here, samples, image_count, begin, end,
):
    refs = list(refs)
    take = lambda n: [refs.pop(0) for _ in range(n)]
    sources = [take(c) for c in choices]
    if not begin:
        stat_in, mixed_in = take(2)
    if end:
        (out_ref,) = take(1)
    else:
        stat_out, mixed_out = take(2)
    top_ref, total_ref, mixed_ref = take(3)
    chosen = refs
    step = pl.program_id(0)
    pieces = []
    for source in sources:
        if len(source) == 1:
            pieces.append(source[0])
            continue
        slot = chosen.pop(0)
        pieces.append(slot)
        inner = place_ref[1] == 1

        @pl.when((step == 0) & inner)
        def _(slot=slot, ref=source[0]):
            slot[...] = ref[...]

        @pl.when((step == 0) & jnp.logical_not(inner))
        def _(slot=slot, ref=source[1]):
            slot[...] = ref[...]

    first = place_ref[0] * rows_here + step * TILE
    starts, ends = sample_bounds(lengths_ref, samples)
    height = group * TILE
    row_t = first + (lax.broadcasted_iota(jnp.int32, (height, 1), 0) & (TILE - 1))
    row_image = jnp.zeros((height, 1), jnp.int32)
    for j in range(samples):
        row_image = jnp.where(row_t >= starts[j], images_ref[0, j], row_image)

    lane = lax.broadcasted_iota(jnp.int32, (height, HD), 1)
    if begin:
        top_ref[...] = jnp.full_like(top_ref, LOW)
        total_ref[...] = jnp.zeros_like(total_ref)
        mixed_ref[...] = jnp.zeros_like(mixed_ref)
    else:
        for g in range(kv_heads):
            stat = stat_in[0, g]
            top_ref[g] = stat[:, 0:1]
            total_ref[g] = stat[:, HD // 2 : HD // 2 + 1]
            mixed_ref[g] = mixed_in[0, g]

    for image in range(image_count):
        wanted = jnp.bool_(False)
        for j in range(samples):
            meets = (starts[j] < first + TILE) & (ends[j] > first) & (ends[j] > starts[j])
            wanted = wanted | (meets & (images_ref[0, j] == image))

        @pl.when(wanted)
        def _(image=image):
            mine = row_image == image
            for g in range(kv_heads):
                q = stack_heads(q_ref, g, group)
                scores, values = [], []
                for piece in pieces:
                    k = piece[image, :, g * HD : (g + 1) * HD]
                    values.append(piece[image, :, (kv_heads + g) * HD : (kv_heads + g + 1) * HD])
                    scores.append(lax.dot_general(q, k, NT, preferred_element_type=jnp.float32))
                old = top_ref[g], total_ref[g], mixed_ref[g]
                new = absorb(old, scores, values)
                top_ref[g] = jnp.where(mine, new[0], old[0])
                total_ref[g] = jnp.where(mine, new[1], old[1])
                mixed_ref[g] = jnp.where(mine, new[2], old[2])

    for g in range(kv_heads):
        if end:
            write_heads(out_ref, mixed_ref[g] / total_ref[g], g, group)
        else:
            stat_out[0, g] = jnp.where(lane < HD // 2, top_ref[g], total_ref[g])
            mixed_out[0, g] = mixed_ref[g]


def whole(shape):
    return pl.BlockSpec(shape, lambda i: (0,) * len(shape))


def smem():
    return pl.BlockSpec(memory_space=pltpu.SMEM)


def self_attention(lengths, place, q, pieces, spans, kv_heads, group):
    rows, width = q.shape
    height = group * TILE
    keys = sum(count for _, count in spans)
    return pl.pallas_call(
        functools.partial(
            self_kernel, kv_heads=kv_heads, group=group, spans=spans, rows_here=rows,
            samples=lengths.shape[1],
        ),
        out_shape=jax.ShapeDtypeStruct((rows, width), q.dtype),
        grid=(rows // TILE,),
        in_specs=[smem(), smem(), pl.BlockSpec((TILE, width), lambda i: (i, 0))]
        + [whole(p.shape) for p in pieces],
        out_specs=pl.BlockSpec((TILE, width), lambda i: (i, 0)),
        scratch_shapes=[
            pltpu.VMEM((kv_heads, height, 1), jnp.float32),
            pltpu.VMEM((kv_heads, height, 1), jnp.float32),
            pltpu.VMEM((kv_heads, height, HD), jnp.float32),
        ],
        compiler_params=pltpu.CompilerParams(vmem_limit_bytes=32 << 20),
        cost_estimate=pl.CostEstimate(
            flops=4 * rows * width * keys, bytes_accessed=4 * rows * width,
            transcendentals=rows * (width // HD) * keys,
        ),
    )(lengths, place, q, *pieces)


def cross_attention(lengths, images, place, q, sources, state, end, kv_heads, group):
    rows, width = q.shape
    height = group * TILE
    begin = state is None
    state = () if begin else state
    state_shape = (rows // TILE, kv_heads, height, HD)
    state_spec = pl.BlockSpec((1, kv_heads, height, HD), lambda i: (i, 0, 0, 0))
    q_spec = pl.BlockSpec((TILE, width), lambda i: (i, 0))
    if end:
        out_shape, out_specs = jax.ShapeDtypeStruct((rows, width), q.dtype), q_spec
    else:
        out_shape = [jax.ShapeDtypeStruct(state_shape, jnp.float32)] * 2
        out_specs = [state_spec] * 2
    operands = [piece for source in sources for piece in source]
    image_count = operands[0].shape[0]
    keys = sum(source[0].shape[1] for source in sources)
    return pl.pallas_call(
        functools.partial(
            cross_kernel, kv_heads=kv_heads, group=group,
            choices=tuple(len(source) for source in sources), rows_here=rows,
            samples=lengths.shape[1], image_count=image_count, begin=begin, end=end,
        ),
        out_shape=out_shape,
        grid=(rows // TILE,),
        in_specs=[smem(), smem(), smem(), q_spec]
        + [whole(p.shape) for p in operands] + [state_spec] * len(state),
        out_specs=out_specs,
        scratch_shapes=[
            pltpu.VMEM((kv_heads, height, 1), jnp.float32),
            pltpu.VMEM((kv_heads, height, 1), jnp.float32),
            pltpu.VMEM((kv_heads, height, HD), jnp.float32),
        ]
        + [pltpu.VMEM(source[0].shape, source[0].dtype) for source in sources if len(source) > 1],
        compiler_params=pltpu.CompilerParams(vmem_limit_bytes=32 << 20),
        cost_estimate=pl.CostEstimate(
            flops=4 * rows * width * keys, bytes_accessed=4 * rows * width,
            transcendentals=rows * (width // HD) * keys,
        ),
    )(lengths, images, place, q, *operands, *state)


def per_device(q_self, kv_self, q_cross, kv_cross, sample_lengths, sample_image, *, n_pipe, n_ctx):
    rows = q_self.shape[1]
    kv_heads = kv_self.shape[3] // HD
    group = q_self.shape[2] // HD // kv_heads
    z = lax.axis_index("ctx")
    pipe = lax.axis_index("pipe")
    inner = ((z == 1) | (z == 2)).astype(jnp.int32)
    place = jnp.stack([z, inner]).astype(jnp.int32)

    shares = [lax.dynamic_index_in_dim(kv_cross, pipe, 0, keepdims=False)]
    for k in range(1, n_pipe):
        outgoing = lax.dynamic_index_in_dim(kv_cross, pipe ^ k, 0, keepdims=False)
        shares.append(lax.ppermute(outgoing, "pipe", [(p, p ^ k) for p in range(n_pipe)]))

    longest = rows * n_ctx * 5 // 8
    own = kv_self[0].reshape(rows, -1)
    pieces, spans, left, step = [own], [(0, rows)], longest - 1, 0
    while left > 0 and step < n_ctx - 1:
        step += 1
        count = min(rows, -(-left // 128) * 128)
        sent = pieces[-1][rows - count :]
        pairs = [(c, c + 1) for c in range(step - 1, n_ctx - 1)]
        pieces.append(lax.ppermute(sent, "ctx", pairs))
        spans.append((step, count))
        left -= rows

    own_block = jnp.concatenate(shares, axis=1)
    own_block = own_block.reshape(own_block.shape[0], own_block.shape[1], -1)

    self_out = self_attention(
        sample_lengths, place, q_self[0], pieces, tuple(spans), kv_heads, group
    )

    cross = functools.partial(
        cross_attention, sample_lengths, sample_image, place, q_cross[0],
        kv_heads=kv_heads, group=group,
    )
    if n_ctx == 4:
        pair = lax.ppermute(own_block, "ctx", [(0, 1), (1, 0), (2, 3), (3, 2)])
        near = lax.ppermute(own_block, "ctx", [(1, 2), (2, 1)])
        far = lax.ppermute(own_block, "ctx", [(0, 2), (3, 1)])
        near_on = lax.ppermute(near, "ctx", [(1, 0), (2, 3)])
        far_on = lax.ppermute(far, "ctx", [(1, 0), (2, 3)])
        state = cross([[own_block], [pair]], None, False)
        state = cross([[near, near_on]], state, False)
        cross_out = cross([[far, far_on]], state, True)
    else:
        cross_out = cross([[lax.all_gather(own_block, "ctx", axis=1, tiled=True)]], None, True)
    return self_out[None], cross_out[None]


def solution(mesh):
    in_specs = (
        P("pipe", "ctx", "tp"),
        P("pipe", "ctx", None, "tp"),
        P("pipe", "ctx", "tp"),
        P(None, None, ("pipe", "ctx"), None, "tp"),
        P("pipe", None),
        P("pipe", None),
    )
    out_specs = (P("pipe", "ctx", "tp"), P("pipe", "ctx", "tp"))
    body = functools.partial(
        per_device, n_pipe=mesh.shape["pipe"], n_ctx=mesh.shape["ctx"]
    )
    return jax.shard_map(
        body, mesh=mesh, in_specs=in_specs, out_specs=out_specs, check_vma=False
    )
```

```python
import functools
import math

import jax
import jax.numpy as jnp
from jax import lax
from jax.experimental import pallas as pl
from jax.experimental.pallas import tpu as pltpu
from jax.sharding import PartitionSpec as P

HD = 128
TILE = 32
LOW = -1e30
EXP_SCALE = math.log2(math.e) / math.sqrt(HD)
NT = (((1,), (1,)), ((), ()))
NN = (((1,), (0,)), ((), ()))


def sample_bounds(lengths_ref, count):
    starts, ends, total = [], [], jnp.int32(0)
    for j in range(count):
        starts.append(total)
        total = total + lengths_ref[0, j]
        ends.append(total)
    return starts, ends


def stacked_queries(q_ref, tile, g, group):
    first = g * group
    rows = pl.ds(tile * TILE, TILE)
    return jnp.concatenate(
        [q_ref[rows, (first + h) * HD : (first + h + 1) * HD] for h in range(group)], axis=0
    )


def write_heads(out_ref, mixed, total, tile, g, group):
    rows = (mixed * (1.0 / total)).T.astype(out_ref.dtype)
    for h in range(group):
        at = (g * group + h) * HD
        out_ref[pl.ds(tile * TILE, TILE), at : at + HD] = rows[h * TILE : (h + 1) * TILE]


def scores_of(keys, q):
    return lax.dot_general(keys, q, NT, preferred_element_type=jnp.float32)


def absorb(state, scores, values):
    top, total, mixed = state
    new_top = top
    for s in scores:
        new_top = jnp.maximum(new_top, jnp.max(s, axis=0, keepdims=True))
    decay = jnp.exp2((top - new_top) * EXP_SCALE)
    total = total * decay
    mixed = mixed * decay
    for s, v in zip(scores, values):
        w = jnp.exp2((s - new_top) * EXP_SCALE)
        total = total + jnp.sum(w, axis=0, keepdims=True)
        mixed = mixed + lax.dot_general(
            v, w.astype(jnp.bfloat16), NN, preferred_element_type=jnp.float32
        )
    return new_top, total, mixed


def empty(height):
    return (
        jnp.full((1, height), LOW, jnp.float32),
        jnp.zeros((1, height), jnp.float32),
        jnp.zeros((HD, height), jnp.float32),
    )


def row_positions(first, height):
    return first + (lax.broadcasted_iota(jnp.int32, (1, height), 1) & (TILE - 1))


def self_kernel(lengths_ref, place_ref, q_ref, *refs, kv_heads, group, spans, samples):
    pieces, out_ref, stat_ref, mixed_ref = refs[: len(spans)], *refs[len(spans) : len(spans) + 3]
    flipped = refs[len(spans) + 3 :]
    rows_here = q_ref.shape[0]
    height = group * TILE
    base = place_ref[0] * rows_here
    starts, ends = sample_bounds(lengths_ref, samples)

    def lowest_of(t):
        low = jnp.int32(0)
        for e in ends:
            low = jnp.where(e <= t, e, low)
        return low

    def reached(number, low):
        back, count = spans[number]
        piece_end = base - (back - 1) * rows_here
        return (piece_end - count >= 0) & (low < piece_end)

    def flip(number):
        for g in range(kv_heads):
            v = pieces[number][:, (kv_heads + g) * HD : (kv_heads + g + 1) * HD]
            flipped[number][g] = v.T

    flip(0)
    low_here = lowest_of(base)
    for number in range(1, len(spans)):
        pl.when(reached(number, low_here))(functools.partial(flip, number))

    @pl.loop(0, rows_here // TILE)
    def _(tile):
        first = base + tile * TILE
        low = lowest_of(first)
        row_t = row_positions(first, height)
        row_start = jnp.zeros((1, height), jnp.int32)
        for e in ends:
            row_start = jnp.where(e <= row_t, e, row_start)

        def work(number, begin):
            back, count = spans[number]
            piece_start = base - (back - 1) * rows_here - count
            key_t = piece_start + lax.broadcasted_iota(jnp.int32, (count, 1), 0)
            allowed = key_t >= row_start
            if back == 0:
                allowed = allowed & (key_t <= row_t)
            for g in range(kv_heads):
                q = stacked_queries(q_ref, tile, g, group)
                s = scores_of(pieces[number][:, g * HD : (g + 1) * HD], q)
                s = jnp.where(allowed, s, LOW)
                if begin:
                    state = empty(height)
                else:
                    state = stat_ref[g, 0:1, :], stat_ref[g, 1:2, :], mixed_ref[g]
                top, total, mixed = absorb(state, [s], [flipped[number][g]])
                stat_ref[g, 0:1, :] = top
                stat_ref[g, 1:2, :] = total
                mixed_ref[g] = mixed

        work(0, True)
        for number in range(1, len(spans)):
            pl.when(reached(number, low))(functools.partial(work, number, False))
        for g in range(kv_heads):
            write_heads(out_ref, mixed_ref[g], stat_ref[g, 1:2, :], tile, g, group)


def cross_kernel(
    lengths_ref, images_ref, place_ref, q_ref, *refs, kv_heads, group, choices, samples, begin, end
):
    refs = list(refs)
    take = lambda n: [refs.pop(0) for _ in range(n)]
    sources = [take(c) for c in choices]
    stat_in, mixed_in = (None, None) if begin else take(2)
    out_ref = take(1)[0] if end else None
    stat_ref, mixed_ref = take(2)
    keys_ref, flipped_ref = take(2)
    rows_here = q_ref.shape[0]
    height = group * TILE
    base = place_ref[0] * rows_here
    starts, ends = sample_bounds(lengths_ref, samples)
    image_count, _, span, _ = keys_ref.shape

    def lay(ref, at):
        parts, _, each, _ = ref.shape
        for image in range(image_count):
            for g in range(kv_heads):
                k = ref[:, image, :, g * HD : (g + 1) * HD].reshape(parts * each, HD)
                v = ref[:, image, :, (kv_heads + g) * HD : (kv_heads + g + 1) * HD]
                keys_ref[image, g, at : at + parts * each] = k
                flipped_ref[image, g, :, at : at + parts * each] = v.reshape(parts * each, HD).T

    at = 0
    for source in sources:
        if len(source) == 1:
            lay(source[0], at)
        else:
            inner = place_ref[1] == 1
            pl.when(inner)(functools.partial(lay, source[0], at))
            pl.when(jnp.logical_not(inner))(functools.partial(lay, source[1], at))
        at += source[0].shape[0] * source[0].shape[2]

    @pl.loop(0, rows_here // TILE)
    def _(tile):
        slot = 0 if end else tile
        first = base + tile * TILE
        row_t = row_positions(first, height)
        row_image = jnp.zeros((1, height), jnp.int32)
        leading = jnp.int32(0)
        for j in range(samples):
            row_image = jnp.where(row_t >= starts[j], images_ref[0, j], row_image)
            leading = jnp.where(first >= starts[j], images_ref[0, j], leading)

        def work(image, read_stat, read_mixed, at):
            mine = row_image == image
            for g in range(kv_heads):
                q = stacked_queries(q_ref, tile, g, group)
                s = scores_of(keys_ref[image, g], q)
                if read_stat is None:
                    old = empty(height)
                else:
                    old = read_stat[at, g, 0:1, :], read_stat[at, g, 1:2, :], read_mixed[at, g]
                new = absorb(old, [s], [flipped_ref[image, g]])
                top, total, mixed = [jnp.where(mine, n, o) for n, o in zip(new, old)]
                stat_ref[slot, g, 0:1, :] = top
                stat_ref[slot, g, 1:2, :] = total
                mixed_ref[slot, g] = mixed

        work(leading, stat_in, mixed_in, tile)
        for image in range(image_count):
            wanted = jnp.bool_(False)
            for j in range(samples):
                meets = (starts[j] < first + TILE) & (ends[j] > first)
                wanted = wanted | (meets & (images_ref[0, j] == image))
            pl.when(wanted & (leading != image))(
                functools.partial(work, image, stat_ref, mixed_ref, slot)
            )
        if end:
            for g in range(kv_heads):
                write_heads(out_ref, mixed_ref[0, g], stat_ref[0, g, 1:2, :], tile, g, group)


def smem():
    return pl.BlockSpec(memory_space=pltpu.SMEM)


def vmem():
    return pl.BlockSpec(memory_space=pltpu.VMEM)


def cost(rows, width, keys):
    return pl.CostEstimate(
        flops=8 * rows * width * keys, bytes_accessed=4 * rows * width,
        transcendentals=rows * (width // HD) * keys,
    )


def self_attention(lengths, place, q, pieces, spans, kv_heads, group):
    rows, width = q.shape
    height = group * TILE
    return pl.pallas_call(
        functools.partial(
            self_kernel, kv_heads=kv_heads, group=group, spans=spans, samples=lengths.shape[1]
        ),
        out_shape=jax.ShapeDtypeStruct((rows, width), q.dtype),
        in_specs=[smem(), smem(), vmem()] + [vmem() for p in pieces],
        out_specs=vmem(),
        scratch_shapes=[
            pltpu.VMEM((kv_heads, 8, height), jnp.float32),
            pltpu.VMEM((kv_heads, HD, height), jnp.float32),
        ]
        + [pltpu.VMEM((kv_heads, HD, count), q.dtype) for _, count in spans],
        compiler_params=pltpu.CompilerParams(vmem_limit_bytes=24 << 20),
        cost_estimate=cost(rows, width, sum(count for _, count in spans)),
    )(lengths, place, q, *pieces)


def cross_attention(lengths, images, place, q, sources, state, end, kv_heads, group):
    rows, width = q.shape
    height = group * TILE
    begin = state is None
    state = () if begin else state
    tiles = 1 if end else rows // TILE
    stat_shape, mixed_shape = (tiles, kv_heads, 8, height), (tiles, kv_heads, HD, height)
    state_scratch = []
    if end:
        out_shape = jax.ShapeDtypeStruct((rows, width), q.dtype)
        state_scratch = [pltpu.VMEM(s, jnp.float32) for s in (stat_shape, mixed_shape)]
    else:
        out_shape = [jax.ShapeDtypeStruct(s, jnp.float32) for s in (stat_shape, mixed_shape)]
    operands = [piece for source in sources for piece in source]
    image_count = operands[0].shape[1]
    keys = sum(source[0].shape[0] * source[0].shape[2] for source in sources)
    return pl.pallas_call(
        functools.partial(
            cross_kernel, kv_heads=kv_heads, group=group,
            choices=tuple(len(source) for source in sources),
            samples=lengths.shape[1], begin=begin, end=end,
        ),
        out_shape=out_shape,
        in_specs=[smem(), smem(), smem(), vmem()] + [vmem() for p in (*operands, *state)],
        out_specs=vmem() if end else [vmem(), vmem()],
        scratch_shapes=state_scratch
        + [
            pltpu.VMEM((image_count, kv_heads, keys, HD), q.dtype),
            pltpu.VMEM((image_count, kv_heads, HD, keys), q.dtype),
        ],
        compiler_params=pltpu.CompilerParams(vmem_limit_bytes=24 << 20),
        cost_estimate=cost(rows, width, keys),
    )(lengths, images, place, q, *operands, *state)


def per_device(q_self, kv_self, q_cross, kv_cross, sample_lengths, sample_image, *, n_pipe, n_ctx):
    rows = q_self.shape[1]
    kv_heads = kv_self.shape[3] // HD
    group = q_self.shape[2] // HD // kv_heads
    z = lax.axis_index("ctx")
    inner = ((z == 1) | (z == 2)).astype(jnp.int32)
    place = jnp.stack([z, inner]).astype(jnp.int32)

    own = kv_self[0].reshape(rows, -1)
    shift = lambda piece, step: lax.ppermute(
        piece, "ctx", [(c, c + 1) for c in range(step - 1, n_ctx - 1)]
    )
    passed = shift(own, 1)
    arrived = lax.all_to_all(kv_cross, "pipe", split_axis=0, concat_axis=0, tiled=True)
    arrived, passed = lax.optimization_barrier((arrived, passed))
    own_block = arrived.reshape(*arrived.shape[:3], -1)

    longest = rows * n_ctx * 5 // 8
    pieces, spans, left, step = [own, passed], [(0, rows), (1, rows)], longest - 1 - rows, 1
    while left > 0 and step < n_ctx - 1:
        step += 1
        count = min(rows, -(-left // 128) * 128)
        pieces.append(shift(pieces[-1][rows - count :], step))
        spans.append((step, count))
        left -= rows

    self_out = self_attention(
        sample_lengths, place, q_self[0], pieces, tuple(spans), kv_heads, group
    )

    cross = functools.partial(
        cross_attention, sample_lengths, sample_image, place, q_cross[0],
        kv_heads=kv_heads, group=group,
    )
    if n_ctx == 4:
        near = lax.ppermute(own_block, "ctx", [(1, 2), (2, 1)])
        far = lax.ppermute(own_block, "ctx", [(0, 2), (3, 1)])
        pair = lax.ppermute(own_block, "ctx", [(0, 1), (1, 0), (2, 3), (3, 2)])
        near_on = lax.ppermute(near, "ctx", [(1, 0), (2, 3)])
        far_on = lax.ppermute(far, "ctx", [(1, 0), (2, 3)])
        state = cross([[own_block], [pair]], None, False)
        state = cross([[near, near_on]], state, False)
        cross_out = cross([[far, far_on]], state, True)
    else:
        gathered = lax.all_gather(own_block, "ctx", axis=2, tiled=True)
        cross_out = cross([[gathered]], None, True)
    return self_out[None], cross_out[None]


def solution(mesh):
    in_specs = (
        P("pipe", "ctx", "tp"),
        P("pipe", "ctx", None, "tp"),
        P("pipe", "ctx", "tp"),
        P(None, None, ("pipe", "ctx"), None, "tp"),
        P("pipe", None),
        P("pipe", None),
    )
    out_specs = (P("pipe", "ctx", "tp"), P("pipe", "ctx", "tp"))
    body = functools.partial(
        per_device, n_pipe=mesh.shape["pipe"], n_ctx=mesh.shape["ctx"]
    )
    return jax.shard_map(
        body, mesh=mesh, in_specs=in_specs, out_specs=out_specs, check_vma=False
    )
```

```python
import functools
import math

import jax
import jax.numpy as jnp
from jax import lax
from jax.experimental import pallas as pl
from jax.experimental.pallas import tpu as pltpu
from jax.sharding import PartitionSpec as P

HD = 128
TILE = 32
TOGETHER = 4
LOW = -1e30
EXP_SCALE = math.log2(math.e) / math.sqrt(HD)
NT = (((1,), (1,)), ((), ()))
NN = (((1,), (0,)), ((), ()))


def sample_bounds(lengths_ref, count):
    starts, ends, total = [], [], jnp.int32(0)
    for j in range(count):
        starts.append(total)
        total = total + lengths_ref[0, j]
        ends.append(total)
    return starts, ends


def stacked_queries(q_ref, tile, g, group):
    first = g * group
    rows = pl.ds(tile * TILE, TILE)
    return jnp.concatenate(
        [q_ref[rows, (first + h) * HD : (first + h + 1) * HD] for h in range(group)], axis=0
    )


def write_heads(out_ref, mixed, total, tile, g, group):
    rows = (mixed * (1.0 / total)).T.astype(out_ref.dtype)
    for h in range(group):
        at = (g * group + h) * HD
        out_ref[pl.ds(tile * TILE, TILE), at : at + HD] = rows[h * TILE : (h + 1) * TILE]


def scores_of(keys, q):
    return lax.dot_general(keys, q, NT, preferred_element_type=jnp.float32)


def absorb(state, s, v):
    if state is None:
        new_top = jnp.max(s, axis=0, keepdims=True)
    else:
        top, total, mixed = state
        new_top = jnp.maximum(top, jnp.max(s, axis=0, keepdims=True))
    w = jnp.exp2((s - new_top) * EXP_SCALE)
    added = jnp.sum(w, axis=0, keepdims=True)
    product = lax.dot_general(v, w.astype(jnp.bfloat16), NN, preferred_element_type=jnp.float32)
    if state is None:
        return new_top, added, product
    decay = jnp.exp2((top - new_top) * EXP_SCALE)
    return new_top, total * decay + added, mixed * decay + product


def staggered(units, score, finish):
    waiting = None
    for unit in units:
        s = score(*unit)
        if waiting is not None:
            finish(*waiting)
        waiting = (*unit, s)
    finish(*waiting)


def row_positions(first, height):
    return first + (lax.broadcasted_iota(jnp.int32, (1, height), 1) & (TILE - 1))


def lay(keys_at, flipped_at, ref, rows, kv_heads, g):
    keys_at[...] = ref[rows, g * HD : (g + 1) * HD]
    flipped_at[...] = ref[rows, (kv_heads + g) * HD : (kv_heads + g + 1) * HD].T


def self_kernel(lengths_ref, place_ref, q_ref, *refs, kv_heads, group, spans, parts, samples):
    sources = {part[1] for part in parts}
    pieces = refs[: len(sources)]
    out_ref, stat_ref, mixed_ref, keys_ref, flipped_ref = refs[len(sources) :]
    rows_here = q_ref.shape[0]
    tiles = rows_here // TILE
    height = group * TILE
    base = place_ref[0] * rows_here
    _, ends = sample_bounds(lengths_ref, samples)
    ats = [sum(count for _, count in spans[:n]) for n in range(len(spans))]

    lows = []
    for tile in range(tiles):
        low = jnp.int32(0)
        for e in ends:
            low = jnp.where(e <= base + tile * TILE, e, low)
        lows.append(low)

    def limits(number):
        back, count = spans[number]
        end = base - (back - 1) * rows_here
        return end - count, end

    def reached(number):
        start, end = limits(number)
        many = jnp.int32(0)
        for low in lows:
            many = many + (low < end).astype(jnp.int32)
        return jnp.where(start >= 0, many, 0)

    counts = [reached(number) for number in range(1, len(spans))]
    for number, source, at, offset, count, only in parts:

        def fill(number=number, source=source, at=at, offset=offset, count=count):
            here = slice(ats[number] + offset, ats[number] + offset + count)
            for g in range(kv_heads):
                lay(
                    keys_ref.at[g, here], flipped_ref.at[g, :, here], pieces[source],
                    slice(at, at + count), kv_heads, g,
                )

        if number == 0:
            fill()
        else:
            asked = counts[number - 1] > 0
            if only is not None:
                asked = asked & (place_ref[0] == only)
            pl.when(asked)(fill)

    def starts_of(first):
        row_t = row_positions(first, height)
        row_start = jnp.zeros((1, height), jnp.int32)
        for e in ends:
            row_start = jnp.where(e <= row_t, e, row_start)
        return row_start, row_t

    def keep(tile, g, state):
        stat_ref[tile, g, 0:1, :] = state[0]
        stat_ref[tile, g, 1:2, :] = state[1]
        mixed_ref[tile, g] = state[2]

    def own_count(tile):
        return min(rows_here, -(-(tile + 1) * TILE // HD) * HD)

    def own_scores(tile, g):
        q = stacked_queries(q_ref, tile, g, group)
        return scores_of(keys_ref[g, : own_count(tile)], q)

    def own_finish(tile, g, s):
        row_start, row_t = starts_of(base + tile * TILE)
        key_t = base + lax.broadcasted_iota(jnp.int32, (own_count(tile), 1), 0)
        s = jnp.where((key_t >= row_start) & (key_t <= row_t), s, LOW)
        keep(tile, g, absorb(None, s, flipped_ref[g, :, : own_count(tile)]))

    staggered(
        [(tile, g) for tile in range(tiles) for g in range(kv_heads)], own_scores, own_finish
    )

    together = math.gcd(tiles, TOGETHER)
    for number in range(1, len(spans)):
        start, _ = limits(number)
        at, count = ats[number], spans[number][1]

        @pl.loop(0, (counts[number - 1] + together - 1) // together)
        def _(turn, start=start, at=at, count=count):
            def scores(n, g):
                q = stacked_queries(q_ref, turn * together + n, g, group)
                return scores_of(keys_ref[g, at : at + count], q)

            def finish(n, g, s):
                tile = turn * together + n
                row_start, _ = starts_of(base + tile * TILE)
                key_t = start + lax.broadcasted_iota(jnp.int32, (count, 1), 0)
                s = jnp.where(key_t >= row_start, s, LOW)
                old = stat_ref[tile, g, 0:1, :], stat_ref[tile, g, 1:2, :], mixed_ref[tile, g]
                keep(tile, g, absorb(old, s, flipped_ref[g, :, at : at + count]))

            staggered(
                [(n, g) for n in range(together) for g in range(kv_heads)], scores, finish
            )

    for tile in range(tiles):
        for g in range(kv_heads):
            write_heads(out_ref, mixed_ref[tile, g], stat_ref[tile, g, 1:2, :], tile, g, group)


def cross_kernel(
    lengths_ref, images_ref, place_ref, q_ref, *refs, kv_heads, group, sources, samples, begin, end
):
    refs = list(refs)
    take = lambda n: [refs.pop(0) for _ in range(n)]
    pieces = [take(len(source)) for source in sources]
    stat_in, mixed_in = (None, None) if begin else take(2)
    out_ref = take(1)[0] if end else None
    stat_ref, mixed_ref, keys_ref, flipped_ref = take(4)
    rows_here = q_ref.shape[0]
    tiles = rows_here // TILE
    height = group * TILE
    base = place_ref[0] * rows_here
    starts, _ = sample_bounds(lengths_ref, samples)
    image_count = keys_ref.shape[0]

    def fill(ref, at, row, parts, each):
        for part in range(parts):
            for image in range(image_count):
                rows = slice(row + (part * image_count + image) * each, None)
                rows = slice(rows.start, rows.start + each)
                here = slice(at + part * each, at + (part + 1) * each)
                for g in range(kv_heads):
                    keys_ref[image, g, here] = ref[rows, g * HD : (g + 1) * HD]
        for image in range(image_count):
            for g in range(kv_heads):
                column = (kv_heads + g) * HD
                values = [
                    ref[pl.ds(row + (part * image_count + image) * each, each), column : column + HD]
                    for part in range(parts)
                ]
                whole = jnp.concatenate(values, axis=0)
                flipped_ref[image, g, :, at : at + parts * each] = whole.T

    at = 0
    for source, given in zip(sources, pieces):
        for number, ((row, parts, each), ref) in enumerate(zip(source, given)):
            put = functools.partial(fill, ref, at, row, parts, each)
            if len(source) == 1:
                put()
            else:
                pl.when(place_ref[1] == 1 - number)(put)
        at += source[0][1] * source[0][2]

    def images_of(tile):
        first = base + tile * TILE
        row_t = row_positions(first, height)
        row_image = jnp.zeros((1, height), jnp.int32)
        leading = jnp.int32(0)
        for j in range(samples):
            row_image = jnp.where(row_t >= starts[j], images_ref[0, j], row_image)
            leading = jnp.where(first >= starts[j], images_ref[0, j], leading)
        return row_image, leading

    def keep(tile, g, state):
        stat_ref[tile, g, 0:1, :] = state[0]
        stat_ref[tile, g, 1:2, :] = state[1]
        mixed_ref[tile, g] = state[2]

    def chosen(mine, new, old):
        if old is None:
            old = LOW, 0.0, 0.0
        return [jnp.where(mine, n, o) for n, o in zip(new, old)]

    marks = [images_of(tile) for tile in range(tiles)]

    def scores(tile, g):
        return scores_of(keys_ref[marks[tile][1], g], stacked_queries(q_ref, tile, g, group))

    def finish(tile, g, s):
        row_image, leading = marks[tile]
        old = None
        if not begin:
            old = stat_in[tile, g, 0:1, :], stat_in[tile, g, 1:2, :], mixed_in[tile, g]
        new = absorb(old, s, flipped_ref[leading, g])
        keep(tile, g, chosen(row_image == leading, new, old))

    staggered([(tile, g) for tile in range(tiles) for g in range(kv_heads)], scores, finish)

    @pl.loop(0, tiles)
    def _(tile):
        first = base + tile * TILE
        leading, others = jnp.int32(0), [jnp.bool_(False)] * image_count
        for j in range(samples):
            leading = jnp.where(first >= starts[j], images_ref[0, j], leading)
        for j in range(samples):
            inside = (starts[j] > first) & (starts[j] < first + TILE)
            for image in range(image_count):
                others[image] = others[image] | (inside & (images_ref[0, j] == image))
        for image in range(image_count):

            @pl.when(others[image] & (leading != image))
            def _(image=image):
                row_image, _ = images_of(tile)
                olds = [
                    (stat_ref[tile, g, 0:1, :], stat_ref[tile, g, 1:2, :], mixed_ref[tile, g])
                    for g in range(kv_heads)
                ]
                ss = [
                    scores_of(keys_ref[image, g], stacked_queries(q_ref, tile, g, group))
                    for g in range(kv_heads)
                ]
                for g in range(kv_heads):
                    new = absorb(olds[g], ss[g], flipped_ref[image, g])
                    keep(tile, g, chosen(row_image == image, new, olds[g]))

    if end:
        for tile in range(tiles):
            for g in range(kv_heads):
                write_heads(out_ref, mixed_ref[tile, g], stat_ref[tile, g, 1:2, :], tile, g, group)


def smem():
    return pl.BlockSpec(memory_space=pltpu.SMEM)


def vmem():
    return pl.BlockSpec(memory_space=pltpu.VMEM)


def cost(rows, width, keys):
    return pl.CostEstimate(
        flops=8 * rows * width * keys, bytes_accessed=4 * rows * width,
        transcendentals=rows * (width // HD) * keys,
    )


def state_shapes(rows, kv_heads, group):
    tiles, height = rows // TILE, group * TILE
    return (tiles, kv_heads, 8, height), (tiles, kv_heads, HD, height)


def self_attention(lengths, place, q, pieces, spans, parts, kv_heads, group):
    rows, width = q.shape
    keys = sum(count for _, count in spans)
    return pl.pallas_call(
        functools.partial(
            self_kernel, kv_heads=kv_heads, group=group, spans=spans, parts=parts,
            samples=lengths.shape[1],
        ),
        out_shape=jax.ShapeDtypeStruct((rows, width), q.dtype),
        in_specs=[smem(), smem(), vmem()] + [vmem() for p in pieces],
        out_specs=vmem(),
        scratch_shapes=[pltpu.VMEM(s, jnp.float32) for s in state_shapes(rows, kv_heads, group)]
        + [
            pltpu.VMEM((kv_heads, keys, HD), q.dtype),
            pltpu.VMEM((kv_heads, HD, keys), q.dtype),
        ],
        compiler_params=pltpu.CompilerParams(vmem_limit_bytes=28 << 20),
        cost_estimate=cost(rows, width, keys),
    )(lengths, place, q, *pieces)


def cross_attention(lengths, images, place, q, sources, state, end, kv_heads, group, image_count):
    rows, width = q.shape
    begin = state is None
    state = () if begin else state
    shapes = state_shapes(rows, kv_heads, group)
    state_scratch = []
    if end:
        out_shape = jax.ShapeDtypeStruct((rows, width), q.dtype)
        state_scratch = [pltpu.VMEM(s, jnp.float32) for s in shapes]
    else:
        out_shape = [jax.ShapeDtypeStruct(s, jnp.float32) for s in shapes]
    operands = [piece[0] for source in sources for piece in source]
    keys = sum(source[0][2] * source[0][3] for source in sources)
    return pl.pallas_call(
        functools.partial(
            cross_kernel, kv_heads=kv_heads, group=group,
            sources=tuple(tuple(piece[1:] for piece in source) for source in sources),
            samples=lengths.shape[1], begin=begin, end=end,
        ),
        out_shape=out_shape,
        in_specs=[smem(), smem(), smem(), vmem()] + [vmem() for p in (*operands, *state)],
        out_specs=vmem() if end else [vmem(), vmem()],
        scratch_shapes=state_scratch
        + [
            pltpu.VMEM((image_count, kv_heads, keys, HD), q.dtype),
            pltpu.VMEM((image_count, kv_heads, HD, keys), q.dtype),
        ],
        compiler_params=pltpu.CompilerParams(vmem_limit_bytes=28 << 20),
        cost_estimate=cost(rows, width, keys),
    )(lengths, images, place, q, *operands, *state)


def per_device(q_self, kv_self, q_cross, kv_cross, sample_lengths, sample_image, *, n_pipe, n_ctx):
    rows = q_self.shape[1]
    kv_heads = kv_self.shape[3] // HD
    group = q_self.shape[2] // HD // kv_heads
    image_count, each = kv_cross.shape[1:3]
    z = lax.axis_index("ctx")
    inner = ((z == 1) | (z == 2)).astype(jnp.int32)
    place = jnp.stack([z, inner]).astype(jnp.int32)

    own = kv_self[0].reshape(rows, -1)
    shift = lambda piece, step: lax.ppermute(
        piece, "ctx", [(c, c + 1) for c in range(step - 1, n_ctx - 1)]
    )
    passed = shift(own, 1)
    arrived = lax.all_to_all(kv_cross, "pipe", split_axis=0, concat_axis=0, tiled=True)
    arrived, passed = lax.optimization_barrier((arrived, passed))
    own_rows = arrived.reshape(-1, own.shape[1])
    cross_rows = own_rows.shape[0]
    longest = rows * n_ctx * 5 // 8

    attend_self = functools.partial(
        self_attention, sample_lengths, place, q_self[0], kv_heads=kv_heads, group=group
    )
    attend_cross = functools.partial(
        cross_attention, sample_lengths, sample_image, place, q_cross[0],
        kv_heads=kv_heads, group=group, image_count=image_count,
    )
    if n_ctx == 4:
        half = rows // 2
        block = jnp.concatenate([passed[half:], own_rows, passed[:half]], axis=0)
        at = lambda array, row: (array, row, n_pipe, each)
        near = lax.ppermute(block, "ctx", [(1, 2), (2, 1)])
        pair = lax.ppermute(block, "ctx", [(0, 1), (1, 0), (2, 3), (3, 2)])
        state = attend_cross([[at(own_rows, 0)]], None, False)
        near, pair, state = lax.optimization_barrier((near, pair, state))
        far = lax.ppermute(pair[half : half + cross_rows], "ctx", [(1, 2), (2, 1)])
        near_on = lax.ppermute(near[: half + cross_rows], "ctx", [(1, 0), (2, 3)])
        state = attend_cross([[at(pair, half)]], state, False)
        far, near_on, state = lax.optimization_barrier((far, near_on, state))
        far_on = lax.ppermute(far, "ctx", [(1, 0), (2, 3)])
        state = attend_cross([[at(near, half), at(near_on, half)]], state, False)
        low = half + cross_rows
        spans = ((0, rows), (1, rows), (2, rows), (3, half))
        parts = (
            (0, 0, 0, 0, rows, None),
            (1, 1, 0, 0, rows, None),
            (2, 2, low, 0, half, 2),
            (2, 2, 0, half, half, 2),
            (2, 3, low, 0, half, 3),
            (2, 3, 0, half, half, 3),
            (3, 4, 0, 0, half, 3),
        )
        self_out = attend_self([own, passed, near, pair, near_on], spans, parts)
        cross_out = attend_cross([[at(far, 0), at(far_on, 0)]], state, True)
    else:
        pieces, spans, left, step = [own, passed], [(0, rows), (1, rows)], longest - 1 - rows, 1
        while left > 0 and step < n_ctx - 1:
            step += 1
            count = min(rows, -(-left // HD) * HD)
            pieces.append(shift(pieces[-1][rows - count :], step))
            spans.append((step, count))
            left -= rows
        parts = tuple((n, n, 0, 0, count, None) for n, (_, count) in enumerate(spans))
        self_out = attend_self(pieces, tuple(spans), parts)
        gathered = lax.all_gather(own_rows, "ctx", axis=0, tiled=True)
        cross_out = attend_cross([[(gathered, 0, n_ctx * n_pipe, each)]], None, True)
    return self_out[None], cross_out[None]


def solution(mesh):
    in_specs = (
        P("pipe", "ctx", "tp"),
        P("pipe", "ctx", None, "tp"),
        P("pipe", "ctx", "tp"),
        P(None, None, ("pipe", "ctx"), None, "tp"),
        P("pipe", None),
        P("pipe", None),
    )
    out_specs = (P("pipe", "ctx", "tp"), P("pipe", "ctx", "tp"))
    body = functools.partial(
        per_device, n_pipe=mesh.shape["pipe"], n_ctx=mesh.shape["ctx"]
    )
    return jax.shard_map(
        body, mesh=mesh, in_specs=in_specs, out_specs=out_specs, check_vma=False
    )
```

```python
import functools
import math

import jax
import jax.numpy as jnp
from jax import lax
from jax.experimental import pallas as pl
from jax.experimental.pallas import tpu as pltpu
from jax.sharding import PartitionSpec as P

HD = 128
TILE = 32
TOGETHER = 4
LOW = -1e30
EXP_SCALE = math.log2(math.e) / math.sqrt(HD)
NT = (((1,), (1,)), ((), ()))
NN = (((1,), (0,)), ((), ()))


def sample_bounds(lengths_ref, count):
    starts, ends, total = [], [], jnp.int32(0)
    for j in range(count):
        starts.append(total)
        total = total + lengths_ref[0, j]
        ends.append(total)
    return starts, ends


def stacked_queries(q_ref, tile, g, group):
    first = g * group
    rows = pl.ds(tile * TILE, TILE)
    return jnp.concatenate(
        [q_ref[rows, (first + h) * HD : (first + h + 1) * HD] for h in range(group)], axis=0
    )


def write_heads(out_ref, mixed, total, tile, g, group):
    rows = (mixed * (1.0 / total)).T.astype(out_ref.dtype)
    for h in range(group):
        at = (g * group + h) * HD
        out_ref[pl.ds(tile * TILE, TILE), at : at + HD] = rows[h * TILE : (h + 1) * TILE]


def scores_of(keys, q):
    return lax.dot_general(keys, q, NT, preferred_element_type=jnp.float32)


def absorb(state, s, v):
    if state is None:
        new_top = jnp.max(s, axis=0, keepdims=True)
    else:
        top, total, mixed = state
        new_top = jnp.maximum(top, jnp.max(s, axis=0, keepdims=True))
    w = jnp.exp2((s - new_top) * EXP_SCALE)
    added = jnp.sum(w, axis=0, keepdims=True)
    product = lax.dot_general(v, w.astype(jnp.bfloat16), NN, preferred_element_type=jnp.float32)
    if state is None:
        return new_top, added, product
    decay = jnp.exp2((top - new_top) * EXP_SCALE)
    return new_top, total * decay + added, mixed * decay + product


def staggered(units, score, finish):
    waiting = None
    for unit in units:
        s = score(*unit)
        if waiting is not None:
            finish(*waiting)
        waiting = (*unit, s)
    finish(*waiting)


def row_positions(first, height):
    return first + (lax.broadcasted_iota(jnp.int32, (1, height), 1) & (TILE - 1))


def lay(keys_at, flipped_at, ref, rows, kv_heads, g):
    keys_at[...] = ref[rows, g * HD : (g + 1) * HD]
    flipped_at[...] = ref[rows, (kv_heads + g) * HD : (kv_heads + g + 1) * HD].T


def self_kernel(
    lengths_ref, place_ref, q_ref, *refs, kv_heads, group, spans, parts, samples, begin, end
):
    refs = list(refs)
    take = lambda n: [refs.pop(0) for _ in range(n)]
    pieces = take(len({part[1] for part in parts}))
    stat_in, mixed_in = (None, None) if begin else take(2)
    out_ref = take(1)[0] if end else None
    stat_ref, mixed_ref, keys_ref, flipped_ref = take(4)
    rows_here = q_ref.shape[0]
    tiles = rows_here // TILE
    height = group * TILE
    base = place_ref[0] * rows_here
    _, ends = sample_bounds(lengths_ref, samples)
    ats = [sum(count for _, count in spans[:n]) for n in range(len(spans))]

    lows = []
    for tile in range(tiles):
        low = jnp.int32(0)
        for e in ends:
            low = jnp.where(e <= base + tile * TILE, e, low)
        lows.append(low)

    def limits(number):
        back, count = spans[number]
        past = base - (back - 1) * rows_here
        return past - count, past

    def reached(number):
        start, past = limits(number)
        many = jnp.int32(0)
        for low in lows:
            many = many + (low < past).astype(jnp.int32)
        return jnp.where(start >= 0, many, 0)

    counts = [reached(number) for number in range(len(spans))]
    for number, source, at, offset, count, only in parts:

        def fill(number=number, source=source, at=at, offset=offset, count=count):
            here = slice(ats[number] + offset, ats[number] + offset + count)
            for g in range(kv_heads):
                lay(
                    keys_ref.at[g, here], flipped_ref.at[g, :, here], pieces[source],
                    slice(at, at + count), kv_heads, g,
                )

        if spans[number][0] == 0:
            fill()
        else:
            asked = counts[number] > 0
            if only is not None:
                asked = asked & (place_ref[0] == only)
            pl.when(asked)(fill)

    def starts_of(first):
        row_t = row_positions(first, height)
        row_start = jnp.zeros((1, height), jnp.int32)
        for e in ends:
            row_start = jnp.where(e <= row_t, e, row_start)
        return row_start, row_t

    def keep(tile, g, state):
        stat_ref[tile, g, 0:1, :] = state[0]
        stat_ref[tile, g, 1:2, :] = state[1]
        mixed_ref[tile, g] = state[2]

    def own_count(tile):
        return min(rows_here, -(-(tile + 1) * TILE // HD) * HD)

    def own_scores(tile, g):
        q = stacked_queries(q_ref, tile, g, group)
        return scores_of(keys_ref[g, : own_count(tile)], q)

    def own_finish(tile, g, s):
        row_start, row_t = starts_of(base + tile * TILE)
        key_t = base + lax.broadcasted_iota(jnp.int32, (own_count(tile), 1), 0)
        s = jnp.where((key_t >= row_start) & (key_t <= row_t), s, LOW)
        keep(tile, g, absorb(None, s, flipped_ref[g, :, : own_count(tile)]))

    if begin:
        staggered(
            [(tile, g) for tile in range(tiles) for g in range(kv_heads)], own_scores, own_finish
        )
    else:
        stat_ref[...] = stat_in[...]
        mixed_ref[...] = mixed_in[...]

    together = math.gcd(tiles, TOGETHER)
    for number in range(1 if begin else 0, len(spans)):
        start, _ = limits(number)
        at, count = ats[number], spans[number][1]

        @pl.loop(0, (counts[number] + together - 1) // together)
        def _(turn, start=start, at=at, count=count):
            def scores(n, g):
                q = stacked_queries(q_ref, turn * together + n, g, group)
                return scores_of(keys_ref[g, at : at + count], q)

            def finish(n, g, s):
                tile = turn * together + n
                row_start, _ = starts_of(base + tile * TILE)
                key_t = start + lax.broadcasted_iota(jnp.int32, (count, 1), 0)
                s = jnp.where(key_t >= row_start, s, LOW)
                old = stat_ref[tile, g, 0:1, :], stat_ref[tile, g, 1:2, :], mixed_ref[tile, g]
                keep(tile, g, absorb(old, s, flipped_ref[g, :, at : at + count]))

            staggered(
                [(n, g) for n in range(together) for g in range(kv_heads)], scores, finish
            )

    for tile in range(tiles if end else 0):
        for g in range(kv_heads):
            write_heads(out_ref, mixed_ref[tile, g], stat_ref[tile, g, 1:2, :], tile, g, group)


def cross_kernel(
    lengths_ref, images_ref, place_ref, q_ref, *refs, kv_heads, group, sources, samples, begin, end
):
    refs = list(refs)
    take = lambda n: [refs.pop(0) for _ in range(n)]
    pieces = [take(len(source)) for source in sources]
    stat_in, mixed_in = (None, None) if begin else take(2)
    out_ref = take(1)[0] if end else None
    stat_ref, mixed_ref, keys_ref, flipped_ref = take(4)
    rows_here = q_ref.shape[0]
    tiles = rows_here // TILE
    height = group * TILE
    base = place_ref[0] * rows_here
    starts, _ = sample_bounds(lengths_ref, samples)
    image_count = keys_ref.shape[0]

    def fill(ref, at, row, parts, each):
        for part in range(parts):
            for image in range(image_count):
                rows = slice(row + (part * image_count + image) * each, None)
                rows = slice(rows.start, rows.start + each)
                here = slice(at + part * each, at + (part + 1) * each)
                for g in range(kv_heads):
                    keys_ref[image, g, here] = ref[rows, g * HD : (g + 1) * HD]
        for image in range(image_count):
            for g in range(kv_heads):
                column = (kv_heads + g) * HD
                values = [
                    ref[pl.ds(row + (part * image_count + image) * each, each), column : column + HD]
                    for part in range(parts)
                ]
                whole = jnp.concatenate(values, axis=0)
                flipped_ref[image, g, :, at : at + parts * each] = whole.T

    at = 0
    for source, given in zip(sources, pieces):
        for number, ((row, parts, each), ref) in enumerate(zip(source, given)):
            put = functools.partial(fill, ref, at, row, parts, each)
            if len(source) == 1:
                put()
            else:
                pl.when(place_ref[1] == 1 - number)(put)
        at += source[0][1] * source[0][2]

    def images_of(tile):
        first = base + tile * TILE
        row_t = row_positions(first, height)
        row_image = jnp.zeros((1, height), jnp.int32)
        leading = jnp.int32(0)
        for j in range(samples):
            row_image = jnp.where(row_t >= starts[j], images_ref[0, j], row_image)
            leading = jnp.where(first >= starts[j], images_ref[0, j], leading)
        return row_image, leading

    def keep(tile, g, state):
        stat_ref[tile, g, 0:1, :] = state[0]
        stat_ref[tile, g, 1:2, :] = state[1]
        mixed_ref[tile, g] = state[2]

    def chosen(mine, new, old):
        if old is None:
            old = LOW, 0.0, 0.0
        return [jnp.where(mine, n, o) for n, o in zip(new, old)]

    marks = [images_of(tile) for tile in range(tiles)]

    def scores(tile, g):
        return scores_of(keys_ref[marks[tile][1], g], stacked_queries(q_ref, tile, g, group))

    def finish(tile, g, s):
        row_image, leading = marks[tile]
        old = None
        if not begin:
            old = stat_in[tile, g, 0:1, :], stat_in[tile, g, 1:2, :], mixed_in[tile, g]
        new = absorb(old, s, flipped_ref[leading, g])
        keep(tile, g, chosen(row_image == leading, new, old))

    staggered([(tile, g) for tile in range(tiles) for g in range(kv_heads)], scores, finish)

    @pl.loop(0, tiles)
    def _(tile):
        first = base + tile * TILE
        leading, others = jnp.int32(0), [jnp.bool_(False)] * image_count
        for j in range(samples):
            leading = jnp.where(first >= starts[j], images_ref[0, j], leading)
        for j in range(samples):
            inside = (starts[j] > first) & (starts[j] < first + TILE)
            for image in range(image_count):
                others[image] = others[image] | (inside & (images_ref[0, j] == image))
        for image in range(image_count):

            @pl.when(others[image] & (leading != image))
            def _(image=image):
                row_image, _ = images_of(tile)
                olds = [
                    (stat_ref[tile, g, 0:1, :], stat_ref[tile, g, 1:2, :], mixed_ref[tile, g])
                    for g in range(kv_heads)
                ]
                ss = [
                    scores_of(keys_ref[image, g], stacked_queries(q_ref, tile, g, group))
                    for g in range(kv_heads)
                ]
                for g in range(kv_heads):
                    new = absorb(olds[g], ss[g], flipped_ref[image, g])
                    keep(tile, g, chosen(row_image == image, new, olds[g]))

    if end:
        for tile in range(tiles):
            for g in range(kv_heads):
                write_heads(out_ref, mixed_ref[tile, g], stat_ref[tile, g, 1:2, :], tile, g, group)


def smem():
    return pl.BlockSpec(memory_space=pltpu.SMEM)


def vmem():
    return pl.BlockSpec(memory_space=pltpu.VMEM)


def cost(rows, width, keys):
    return pl.CostEstimate(
        flops=8 * rows * width * keys, bytes_accessed=4 * rows * width,
        transcendentals=rows * (width // HD) * keys,
    )


def state_shapes(rows, kv_heads, group):
    tiles, height = rows // TILE, group * TILE
    return (tiles, kv_heads, 8, height), (tiles, kv_heads, HD, height)


def state_call(kernel, operands, rows, width, keys, shapes, scratch, end, dtype):
    scalars = sum(x.dtype == jnp.int32 for x in operands)
    state_scratch = []
    if end:
        out_shape = jax.ShapeDtypeStruct((rows, width), dtype)
        state_scratch = [pltpu.VMEM(s, jnp.float32) for s in shapes]
    else:
        out_shape = [jax.ShapeDtypeStruct(s, jnp.float32) for s in shapes]
    return pl.pallas_call(
        kernel,
        out_shape=out_shape,
        in_specs=[smem()] * scalars + [vmem()] * (len(operands) - scalars),
        out_specs=vmem() if end else [vmem(), vmem()],
        scratch_shapes=state_scratch + scratch,
        compiler_params=pltpu.CompilerParams(vmem_limit_bytes=28 << 20),
        cost_estimate=cost(rows, width, keys),
    )(*operands)


def self_attention(lengths, place, q, pieces, spans, parts, state, end, kv_heads, group):
    rows, width = q.shape
    keys = sum(count for _, count in spans)
    begin = state is None
    kernel = functools.partial(
        self_kernel, kv_heads=kv_heads, group=group, spans=spans, parts=parts,
        samples=lengths.shape[1], begin=begin, end=end,
    )
    scratch = [
        pltpu.VMEM((kv_heads, keys, HD), q.dtype), pltpu.VMEM((kv_heads, HD, keys), q.dtype)
    ]
    operands = (lengths, place, q, *pieces, *(() if begin else state))
    shapes = state_shapes(rows, kv_heads, group)
    return state_call(kernel, operands, rows, width, keys, shapes, scratch, end, q.dtype)


def cross_attention(lengths, images, place, q, sources, state, end, kv_heads, group, image_count):
    rows, width = q.shape
    begin = state is None
    kernel = functools.partial(
        cross_kernel, kv_heads=kv_heads, group=group,
        sources=tuple(tuple(piece[1:] for piece in source) for source in sources),
        samples=lengths.shape[1], begin=begin, end=end,
    )
    pieces = [piece[0] for source in sources for piece in source]
    keys = sum(source[0][2] * source[0][3] for source in sources)
    scratch = [
        pltpu.VMEM((image_count, kv_heads, keys, HD), q.dtype),
        pltpu.VMEM((image_count, kv_heads, HD, keys), q.dtype),
    ]
    operands = (lengths, images, place, q, *pieces, *(() if begin else state))
    shapes = state_shapes(rows, kv_heads, group)
    return state_call(kernel, operands, rows, width, keys, shapes, scratch, end, q.dtype)


def cross_ending(lengths, images, place, q, sources, state, rest, head, kv_heads, group, image_count):
    rows, width = q.shape
    share = width // kv_heads
    keys = sources[0][2] * sources[0][3]
    kernel = functools.partial(
        cross_kernel, kv_heads=1, group=group,
        sources=(tuple(piece[1:] for piece in sources),),
        samples=lengths.shape[1], begin=False, end=True,
    )
    pieces = [piece[0] for piece in sources]
    shapes = state_shapes(rows, 1, group)
    first = lambda shape: pl.BlockSpec(shape, lambda i: (0, head) + (0,) * (len(shape) - 2))
    body = lambda *refs: kernel(*refs)
    operands = [lengths, images, place, q, *pieces, *state]
    in_specs = [smem()] * 3 + [first((rows, share))] + [vmem()] * len(pieces)
    in_specs += [first(shape) for shape in shapes]
    aliases = {}
    if rest is not None:
        body = lambda *refs: kernel(*refs[: len(operands) - 1], *refs[len(operands) :])
        aliases = {len(operands): 0}
        operands.append(rest)
        in_specs.append(pl.BlockSpec(memory_space=pl.ANY))
    return pl.pallas_call(
        body,
        out_shape=jax.ShapeDtypeStruct((rows, width), q.dtype),
        grid=(1,),
        in_specs=in_specs,
        out_specs=first((rows, share)),
        scratch_shapes=[pltpu.VMEM(s, jnp.float32) for s in shapes]
        + [
            pltpu.VMEM((image_count, 1, keys, HD), q.dtype),
            pltpu.VMEM((image_count, 1, HD, keys), q.dtype),
        ],
        input_output_aliases=aliases,
        compiler_params=pltpu.CompilerParams(vmem_limit_bytes=28 << 20),
        cost_estimate=cost(rows, share, keys),
    )(*operands)


def per_device(q_self, kv_self, q_cross, kv_cross, sample_lengths, sample_image, *, n_pipe, n_ctx):
    rows = q_self.shape[1]
    kv_heads = kv_self.shape[3] // HD
    group = q_self.shape[2] // HD // kv_heads
    image_count, each = kv_cross.shape[1:3]
    z = lax.axis_index("ctx")
    inner = ((z == 1) | (z == 2)).astype(jnp.int32)
    place = jnp.stack([z, inner]).astype(jnp.int32)

    shift = lambda piece, step: lax.ppermute(
        piece, "ctx", [(c, c + 1) for c in range(step - 1, n_ctx - 1)]
    )
    passed = shift(kv_self[0], 1)
    arrived = lax.all_to_all(kv_cross, "pipe", split_axis=0, concat_axis=0, tiled=True)
    arrived, passed = lax.optimization_barrier((arrived, passed))
    own = kv_self[0].reshape(rows, -1)
    passed = passed.reshape(rows, -1)
    own_rows = arrived.reshape(-1, own.shape[1])
    cross_rows = own_rows.shape[0]
    longest = rows * n_ctx * 5 // 8

    attend_self = functools.partial(
        self_attention, sample_lengths, place, q_self[0], kv_heads=kv_heads, group=group
    )
    attend_cross = functools.partial(
        cross_attention, sample_lengths, sample_image, place, q_cross[0],
        kv_heads=kv_heads, group=group, image_count=image_count,
    )
    if n_ctx == 4:
        half = rows // 2
        block = jnp.concatenate([passed[half:], own_rows, passed[:half]], axis=0)
        at = lambda array, row: (array, row, n_pipe, each)
        near = lax.ppermute(block, "ctx", [(1, 2), (2, 1)])
        pair = lax.ppermute(block, "ctx", [(0, 1), (1, 0), (2, 3), (3, 2)])
        early = ((0, rows), (1, rows))
        parts = ((0, 0, 0, 0, rows, None), (1, 1, 0, 0, rows, None))
        state = attend_cross([[at(own_rows, 0)]], None, False)
        self_state = attend_self([own, passed], early, parts, None, False)
        near, pair, state, self_state = lax.optimization_barrier((near, pair, state, self_state))
        columns = lambda j: pair[half : half + cross_rows, j * HD : (j + 1) * HD]
        far = [
            lax.ppermute(
                jnp.concatenate([columns(g), columns(kv_heads + g)], axis=1),
                "ctx", [(1, 2), (2, 1)],
            )
            for g in range(kv_heads)
        ]
        near_on = lax.ppermute(near[: half + cross_rows], "ctx", [(1, 0), (2, 3)])
        state = attend_cross([[at(pair, half)]], state, False)
        far[0], state = lax.optimization_barrier((far[0], state))
        low = half + cross_rows
        parts = (
            (0, 0, low, 0, half, 2),
            (0, 0, 0, half, half, 2),
            (0, 1, low, 0, half, 3),
            (0, 1, 0, half, half, 3),
        )
        self_state = attend_self([near, pair], ((2, rows),), parts, self_state, False)
        far[-1], self_state = lax.optimization_barrier((far[-1], self_state))
        far_on = [lax.ppermute(part, "ctx", [(1, 0), (2, 3)]) for part in far]
        state = attend_cross([[at(near, half), at(near_on, half)]], state, False)
        parts = ((0, 0, 0, 0, half, 3),)
        self_out = attend_self([near_on], ((3, half),), parts, self_state, True)
        cross_out = None
        for g in range(kv_heads):
            cross_out = cross_ending(
                sample_lengths, sample_image, place, q_cross[0],
                [at(far[g], 0), at(far_on[g], 0)], state, cross_out, g,
                kv_heads, group, image_count,
            )
    else:
        pieces, spans, left, step = [own, passed], [(0, rows), (1, rows)], longest - 1 - rows, 1
        while left > 0 and step < n_ctx - 1:
            step += 1
            count = min(rows, -(-left // HD) * HD)
            pieces.append(shift(pieces[-1][rows - count :], step))
            spans.append((step, count))
            left -= rows
        parts = tuple((n, n, 0, 0, count, None) for n, (_, count) in enumerate(spans))
        self_out = attend_self(pieces, tuple(spans), parts, None, True)
        gathered = lax.all_gather(own_rows, "ctx", axis=0, tiled=True)
        cross_out = attend_cross([[(gathered, 0, n_ctx * n_pipe, each)]], None, True)
    return self_out[None], cross_out[None]


def solution(mesh):
    in_specs = (
        P("pipe", "ctx", "tp"),
        P("pipe", "ctx", None, "tp"),
        P("pipe", "ctx", "tp"),
        P(None, None, ("pipe", "ctx"), None, "tp"),
        P("pipe", None),
        P("pipe", None),
    )
    out_specs = (P("pipe", "ctx", "tp"), P("pipe", "ctx", "tp"))
    body = functools.partial(
        per_device, n_pipe=mesh.shape["pipe"], n_ctx=mesh.shape["ctx"]
    )
    return jax.shard_map(
        body, mesh=mesh, in_specs=in_specs, out_specs=out_specs, check_vma=False
    )
```

```python
import functools
import math

import jax
import jax.numpy as jnp
from jax import lax
from jax.experimental import pallas as pl
from jax.experimental.pallas import tpu as pltpu
from jax.sharding import PartitionSpec as P

HD = 128
TILE = 32
TOGETHER = 4
LOW = -1e30
EXP_SCALE = math.log2(math.e) / math.sqrt(HD)
NT = (((1,), (1,)), ((), ()))
NN = (((1,), (0,)), ((), ()))


def mark_kernel(
    lengths_ref, images_ref, place_ref, marks_ref, row_start_ref, row_image_ref, *, samples, images
):
    tiles, _, height = row_start_ref.shape
    starts, total = [], jnp.int32(0)
    for j in range(samples):
        starts.append(total)
        total = total + lengths_ref[0, j]
    base = place_ref[0] * tiles * TILE
    for tile in range(tiles):
        first = base + tile * TILE
        row_t = first + (lax.broadcasted_iota(jnp.int32, (1, height), 1) & (TILE - 1))
        row_start = jnp.zeros((1, height), jnp.int32)
        row_image = jnp.zeros((1, height), jnp.int32)
        leading, low = jnp.int32(0), jnp.int32(0)
        met = [jnp.int32(0)] * images
        for j in range(samples):
            image = images_ref[0, j]
            row_start = jnp.where(row_t >= starts[j], starts[j], row_start)
            row_image = jnp.where(row_t >= starts[j], image, row_image)
            low = jnp.where(first >= starts[j], starts[j], low)
            leading = jnp.where(first >= starts[j], image, leading)
            inside = (starts[j] > first) & (starts[j] < first + TILE)
            met = [jnp.where(inside & (image == i), 1, m) for i, m in enumerate(met)]
        row_start_ref[tile] = row_start
        row_image_ref[tile] = row_image
        marks_ref[tile, 0] = low
        marks_ref[tile, 1] = leading
        for i in range(images):
            marks_ref[tile, 2 + i] = jnp.where(leading == i, 0, met[i])


def stacked_queries(q_ref, tile, g, group):
    first = g * group
    rows = pl.ds(tile * TILE, TILE)
    return jnp.concatenate(
        [q_ref[rows, (first + h) * HD : (first + h + 1) * HD] for h in range(group)], axis=0
    )


def write_heads(out_ref, mixed, total, tile, g, group):
    rows = (mixed * (1.0 / total)).T.astype(out_ref.dtype)
    for h in range(group):
        at = (g * group + h) * HD
        out_ref[pl.ds(tile * TILE, TILE), at : at + HD] = rows[h * TILE : (h + 1) * TILE]


def scores_of(keys, q):
    return lax.dot_general(keys, q, NT, preferred_element_type=jnp.float32)


def absorb(state, s, v):
    if state is None:
        new_top = jnp.max(s, axis=0, keepdims=True)
    else:
        top, total, mixed = state
        new_top = jnp.maximum(top, jnp.max(s, axis=0, keepdims=True))
    w = jnp.exp2((s - new_top) * EXP_SCALE)
    added = jnp.sum(w, axis=0, keepdims=True)
    product = lax.dot_general(v, w.astype(jnp.bfloat16), NN, preferred_element_type=jnp.float32)
    if state is None:
        return new_top, added, product
    decay = jnp.exp2((top - new_top) * EXP_SCALE)
    return new_top, total * decay + added, mixed * decay + product


def staggered(units, score, finish):
    waiting = None
    for unit in units:
        s = score(*unit)
        if waiting is not None:
            finish(*waiting)
        waiting = (*unit, s)
    finish(*waiting)


def lay(keys_at, flipped_at, ref, rows, kv_heads, g):
    keys_at[...] = ref[rows, g * HD : (g + 1) * HD]
    flipped_at[...] = ref[rows, (kv_heads + g) * HD : (kv_heads + g + 1) * HD].T


def self_kernel(
    marks_ref, place_ref, row_start_ref, q_ref, *refs, kv_heads, group, spans, parts, begin, end
):
    refs = list(refs)
    take = lambda n: [refs.pop(0) for _ in range(n)]
    pieces = take(len({part[1] for part in parts}))
    stat_in, mixed_in = (None, None) if begin else take(2)
    out_ref = take(1)[0] if end else None
    stat_ref, mixed_ref, keys_ref, flipped_ref = take(4)
    rows_here = q_ref.shape[0]
    tiles = rows_here // TILE
    height = group * TILE
    base = place_ref[0] * rows_here
    ats = [sum(count for _, count in spans[:n]) for n in range(len(spans))]

    lows = [marks_ref[tile, 0] for tile in range(tiles)]

    def limits(number):
        back, count = spans[number]
        past = base - (back - 1) * rows_here
        return past - count, past

    def reached(number):
        start, past = limits(number)
        many = jnp.int32(0)
        for low in lows:
            many = many + (low < past).astype(jnp.int32)
        return jnp.where(start >= 0, many, 0)

    counts = [reached(number) for number in range(len(spans))]
    for number, source, at, offset, count, only in parts:

        def fill(number=number, source=source, at=at, offset=offset, count=count):
            here = slice(ats[number] + offset, ats[number] + offset + count)
            for g in range(kv_heads):
                lay(
                    keys_ref.at[g, here], flipped_ref.at[g, :, here], pieces[source],
                    slice(at, at + count), kv_heads, g,
                )

        if spans[number][0] == 0:
            fill()
        else:
            asked = counts[number] > 0
            if only is not None:
                asked = asked & (place_ref[0] == only)
            pl.when(asked)(fill)

    def keep(tile, g, state):
        stat_ref[tile, g, 0:1, :] = state[0]
        stat_ref[tile, g, 1:2, :] = state[1]
        mixed_ref[tile, g] = state[2]

    def own_count(tile):
        return min(rows_here, -(-(tile + 1) * TILE // HD) * HD)

    def own_scores(tile, g):
        q = stacked_queries(q_ref, tile, g, group)
        return scores_of(keys_ref[g, : own_count(tile)], q)

    def own_finish(tile, g, s):
        row_start = row_start_ref[tile]
        row_t = base + tile * TILE
        row_t = row_t + (lax.broadcasted_iota(jnp.int32, (1, height), 1) & (TILE - 1))
        key_t = base + lax.broadcasted_iota(jnp.int32, (own_count(tile), 1), 0)
        s = jnp.where((key_t >= row_start) & (key_t <= row_t), s, LOW)
        keep(tile, g, absorb(None, s, flipped_ref[g, :, : own_count(tile)]))

    if begin:
        staggered(
            [(tile, g) for tile in range(tiles) for g in range(kv_heads)], own_scores, own_finish
        )
    else:
        stat_ref[...] = stat_in[...]
        mixed_ref[...] = mixed_in[...]

    together = math.gcd(tiles, TOGETHER)
    for number in range(1 if begin else 0, len(spans)):
        start, _ = limits(number)
        at, count = ats[number], spans[number][1]

        @pl.loop(0, (counts[number] + together - 1) // together)
        def _(turn, start=start, at=at, count=count):
            def scores(n, g):
                q = stacked_queries(q_ref, turn * together + n, g, group)
                return scores_of(keys_ref[g, at : at + count], q)

            def finish(n, g, s):
                tile = turn * together + n
                row_start = row_start_ref[tile]
                key_t = start + lax.broadcasted_iota(jnp.int32, (count, 1), 0)
                s = jnp.where(key_t >= row_start, s, LOW)
                old = stat_ref[tile, g, 0:1, :], stat_ref[tile, g, 1:2, :], mixed_ref[tile, g]
                keep(tile, g, absorb(old, s, flipped_ref[g, :, at : at + count]))

            staggered(
                [(n, g) for n in range(together) for g in range(kv_heads)], scores, finish
            )

    for tile in range(tiles if end else 0):
        for g in range(kv_heads):
            write_heads(out_ref, mixed_ref[tile, g], stat_ref[tile, g, 1:2, :], tile, g, group)


def cross_kernel(
    marks_ref, place_ref, row_image_ref, q_ref, *refs, kv_heads, group, heads, sources, begin, end
):
    refs = list(refs)
    take = lambda n: [refs.pop(0) for _ in range(n)]
    pieces = [take(len(source)) for source in sources]
    stat_in, mixed_in = (None, None) if begin else take(2)
    rest_ref = take(1)[0] if end and heads[0] > 0 else None
    out_ref = take(1)[0] if end else None
    stat_ref, mixed_ref, keys_ref, flipped_ref = take(4)
    tiles = q_ref.shape[0] // TILE
    image_count = keys_ref.shape[0]

    def fill(ref, at, parts, each):
        held = ref.shape[1] // HD // 2
        for n, g in enumerate(heads):
            k_at = (g if held == kv_heads else n) * HD
            v_at = k_at + held * HD
            for image in range(image_count):
                values = []
                for part in range(parts):
                    row = (part * image_count + image) * each
                    here = slice(at + part * each, at + (part + 1) * each)
                    keys_ref[image, n, here] = ref[row : row + each, k_at : k_at + HD]
                    values.append(ref[row : row + each, v_at : v_at + HD])
                whole = jnp.concatenate(values, axis=0)
                flipped_ref[image, n, :, at : at + parts * each] = whole.T

    at = 0
    for source, given in zip(sources, pieces):
        for number, ((parts, each), ref) in enumerate(zip(source, given)):
            put = functools.partial(fill, ref, at, parts, each)
            if len(source) == 1:
                put()
            else:
                pl.when(place_ref[1] == 1 - number)(put)
        at += source[0][0] * source[0][1]

    def keep(tile, n, state):
        stat_ref[tile, n, 0:1, :] = state[0]
        stat_ref[tile, n, 1:2, :] = state[1]
        mixed_ref[tile, n] = state[2]

    def chosen(mine, new, old):
        if old is None:
            old = LOW, 0.0, 0.0
        return [jnp.where(mine, n, o) for n, o in zip(new, old)]

    def scores(tile, n):
        q = stacked_queries(q_ref, tile, heads[n], group)
        return scores_of(keys_ref[marks_ref[tile, 1], n], q)

    def finish(tile, n, s):
        leading = marks_ref[tile, 1]
        old, g = None, heads[n]
        if not begin:
            old = stat_in[tile, g, 0:1, :], stat_in[tile, g, 1:2, :], mixed_in[tile, g]
        new = absorb(old, s, flipped_ref[leading, n])
        keep(tile, n, chosen(row_image_ref[tile] == leading, new, old))

    order = range(len(heads))
    staggered([(tile, n) for tile in range(tiles) for n in order], scores, finish)

    @pl.loop(0, tiles)
    def _(tile):
        for image in range(image_count):

            @pl.when(marks_ref[tile, 2 + image] == 1)
            def _(image=image):
                mine = row_image_ref[tile] == image
                olds = [
                    (stat_ref[tile, n, 0:1, :], stat_ref[tile, n, 1:2, :], mixed_ref[tile, n])
                    for n in order
                ]
                ss = [
                    scores_of(keys_ref[image, n], stacked_queries(q_ref, tile, heads[n], group))
                    for n in order
                ]
                for n in order:
                    new = absorb(olds[n], ss[n], flipped_ref[image, n])
                    keep(tile, n, chosen(mine, new, olds[n]))

    if rest_ref is not None:
        out_ref[:, : rest_ref.shape[1]] = rest_ref[...]
    for tile in range(tiles if end else 0):
        for n in order:
            write_heads(
                out_ref, mixed_ref[tile, n], stat_ref[tile, n, 1:2, :], tile, heads[n], group
            )


def smem():
    return pl.BlockSpec(memory_space=pltpu.SMEM)


def vmem():
    return pl.BlockSpec(memory_space=pltpu.VMEM)


def cost(rows, width, keys):
    return pl.CostEstimate(
        flops=8 * rows * width * keys, bytes_accessed=4 * rows * width,
        transcendentals=rows * (width // HD) * keys,
    )


def state_shapes(rows, kv_heads, group):
    tiles, height = rows // TILE, group * TILE
    return (tiles, kv_heads, 8, height), (tiles, kv_heads, HD, height)


def state_call(kernel, operands, rows, width, keys, shapes, scratch, end, dtype):
    state_scratch = []
    if end:
        out_shape = jax.ShapeDtypeStruct((rows, width), dtype)
        state_scratch = [pltpu.VMEM(s, jnp.float32) for s in shapes]
    else:
        out_shape = [jax.ShapeDtypeStruct(s, jnp.float32) for s in shapes]
    return pl.pallas_call(
        kernel,
        out_shape=out_shape,
        in_specs=[smem()] * 2 + [vmem()] * (len(operands) - 2),
        out_specs=vmem() if end else [vmem(), vmem()],
        scratch_shapes=state_scratch + scratch,
        compiler_params=pltpu.CompilerParams(vmem_limit_bytes=28 << 20),
        cost_estimate=cost(rows, width, keys),
    )(*operands)


def marks_of(lengths, images, place, rows, group, image_count):
    tiles, height = rows // TILE, group * TILE
    row_shape = jax.ShapeDtypeStruct((tiles, 1, height), jnp.int32)
    return pl.pallas_call(
        functools.partial(mark_kernel, samples=lengths.shape[1], images=image_count),
        out_shape=[jax.ShapeDtypeStruct((tiles, 2 + image_count), jnp.int32), row_shape, row_shape],
        in_specs=[smem()] * 3,
        out_specs=[smem(), vmem(), vmem()],
    )(lengths, images, place)


def self_attention(marks, place, row_start, q, pieces, spans, parts, state, end, kv_heads, group):
    rows, width = q.shape
    keys = sum(count for _, count in spans)
    begin = state is None
    kernel = functools.partial(
        self_kernel, kv_heads=kv_heads, group=group, spans=spans, parts=parts,
        begin=begin, end=end,
    )
    scratch = [
        pltpu.VMEM((kv_heads, keys, HD), q.dtype), pltpu.VMEM((kv_heads, HD, keys), q.dtype)
    ]
    operands = (marks, place, row_start, q, *pieces, *(() if begin else state))
    shapes = state_shapes(rows, kv_heads, group)
    return state_call(kernel, operands, rows, width, keys, shapes, scratch, end, q.dtype)


def cross_attention(
    marks, place, row_image, q, sources, state, end, kv_heads, group, image_count,
    heads=None, rest=None,
):
    heads = tuple(range(kv_heads)) if heads is None else heads
    rows, width = q.shape
    begin = state is None
    kernel = functools.partial(
        cross_kernel, kv_heads=kv_heads, group=group, heads=heads,
        sources=tuple(tuple(piece[1:] for piece in source) for source in sources),
        begin=begin, end=end,
    )
    pieces = [piece[0] for source in sources for piece in source]
    keys = sum(source[0][1] * source[0][2] for source in sources)
    scratch = [
        pltpu.VMEM((image_count, len(heads), keys, HD), q.dtype),
        pltpu.VMEM((image_count, len(heads), HD, keys), q.dtype),
    ]
    operands = (marks, place, row_image, q, *pieces, *(() if begin else state))
    if rest is not None:
        operands += (rest,)
    shapes = state_shapes(rows, len(heads), group)
    width = (heads[-1] + 1) * group * HD
    return state_call(kernel, operands, rows, width, keys, shapes, scratch, end, q.dtype)


def per_device(q_self, kv_self, q_cross, kv_cross, sample_lengths, sample_image, *, n_pipe, n_ctx):
    rows = q_self.shape[1]
    kv_heads = kv_self.shape[3] // HD
    group = q_self.shape[2] // HD // kv_heads
    image_count, each = kv_cross.shape[1:3]
    z = lax.axis_index("ctx")
    inner = ((z == 1) | (z == 2)).astype(jnp.int32)
    place = jnp.stack([z, inner]).astype(jnp.int32)

    shift = lambda piece, step: lax.ppermute(
        piece, "ctx", [(c, c + 1) for c in range(step - 1, n_ctx - 1)]
    )
    passed = shift(kv_self[0], 1)
    arrived = lax.all_to_all(kv_cross, "pipe", split_axis=0, concat_axis=0, tiled=True)
    own = kv_self[0].reshape(rows, -1)

    marks, row_start, row_image = marks_of(
        sample_lengths, sample_image, place, rows, group, image_count
    )
    attend_self = functools.partial(
        self_attention, marks, place, row_start, q_self[0], kv_heads=kv_heads, group=group
    )
    attend_cross = functools.partial(
        cross_attention, marks, place, row_image, q_cross[0],
        kv_heads=kv_heads, group=group, image_count=image_count,
    )
    if n_ctx == 4:
        at = lambda array: (array, n_pipe, each)
        self_state = attend_self([own], ((0, rows),), ((0, 0, 0, 0, rows, None),), None, False)
        arrived, passed, self_state = lax.optimization_barrier((arrived, passed, self_state))
        own_rows = arrived.reshape(-1, own.shape[1])

        near = lax.ppermute(own_rows, "ctx", [(1, 2), (2, 1)])
        pair = lax.ppermute(own_rows, "ctx", [(0, 1), (1, 0), (2, 3), (3, 2)])
        state = attend_cross([[at(own_rows)]], None, False)
        passed, state = lax.optimization_barrier((passed, state))
        half = rows // 2
        two_back = lax.ppermute(passed, "ctx", [(1, 2), (2, 3)]).reshape(rows, -1)
        three_back = lax.ppermute(passed[half:], "ctx", [(1, 3)]).reshape(half, -1)
        self_state = attend_self(
            [passed.reshape(rows, -1)], ((1, rows),), ((0, 0, 0, 0, rows, None),), self_state, False
        )
        near, pair, self_state = lax.optimization_barrier((near, pair, self_state))

        near_on = lax.ppermute(near, "ctx", [(1, 0), (2, 3)])
        columns = lambda j: pair[:, j * HD : (j + 1) * HD]
        far = [
            lax.ppermute(
                jnp.concatenate([columns(g), columns(kv_heads + g)], axis=1),
                "ctx", [(1, 2), (2, 1)],
            )
            for g in range(kv_heads)
        ]
        state = attend_cross([[at(pair)]], state, False)
        far[0], state = lax.optimization_barrier((far[0], state))
        self_out = attend_self(
            [two_back, three_back], ((2, rows), (3, half)),
            ((0, 0, 0, 0, rows, None), (1, 1, 0, 0, half, 3)), self_state, True,
        )
        far[-1], self_out = lax.optimization_barrier((far[-1], self_out))
        far_on = [lax.ppermute(part, "ctx", [(1, 0), (2, 3)]) for part in far]
        state = attend_cross([[at(near), at(near_on)]], state, False)
        cross_out = None
        for g in range(kv_heads):
            cross_out = attend_cross(
                [[at(far[g]), at(far_on[g])]], state, True, heads=(g,), rest=cross_out
            )
    else:
        longest = rows * n_ctx * 5 // 8
        pieces, spans = [own, passed.reshape(rows, -1)], [(0, rows), (1, rows)]
        left, step = longest - 1 - rows, 1
        while left > 0 and step < n_ctx - 1:
            step += 1
            count = min(rows, -(-left // HD) * HD)
            pieces.append(shift(pieces[-1][rows - count :], step))
            spans.append((step, count))
            left -= rows
        parts = tuple((n, n, 0, 0, count, None) for n, (_, count) in enumerate(spans))
        self_out = attend_self(pieces, tuple(spans), parts, None, True)
        own_rows = arrived.reshape(-1, own.shape[1])
        gathered = lax.all_gather(own_rows, "ctx", axis=0, tiled=True)
        cross_out = attend_cross([[(gathered, n_ctx * n_pipe, each)]], None, True)
    return self_out[None], cross_out[None]


def solution(mesh):
    in_specs = (
        P("pipe", "ctx", "tp"),
        P("pipe", "ctx", None, "tp"),
        P("pipe", "ctx", "tp"),
        P(None, None, ("pipe", "ctx"), None, "tp"),
        P("pipe", None),
        P("pipe", None),
    )
    out_specs = (P("pipe", "ctx", "tp"), P("pipe", "ctx", "tp"))
    body = functools.partial(
        per_device, n_pipe=mesh.shape["pipe"], n_ctx=mesh.shape["ctx"]
    )
    return jax.shard_map(
        body, mesh=mesh, in_specs=in_specs, out_specs=out_specs, check_vma=False
    )
```

```python
import functools
import math

import jax
import jax.numpy as jnp
from jax import lax
from jax.experimental import pallas as pl
from jax.experimental.pallas import tpu as pltpu
from jax.sharding import PartitionSpec as P

HD = 128
TILE = 32
TOGETHER = 4
LOW = -1e30
EXP_SCALE = math.log2(math.e) / math.sqrt(HD)
NT = (((1,), (1,)), ((), ()))
NN = (((1,), (0,)), ((), ()))


def sample_bounds(lengths_ref, count):
    starts, ends, total = [], [], jnp.int32(0)
    for j in range(count):
        starts.append(total)
        total = total + lengths_ref[0, j]
        ends.append(total)
    return starts, ends


def stacked_queries(q_ref, tile, g, group):
    first = g * group
    rows = pl.ds(tile * TILE, TILE)
    return jnp.concatenate(
        [q_ref[rows, (first + h) * HD : (first + h + 1) * HD] for h in range(group)], axis=0
    )


def write_heads(out_ref, mixed, total, tile, g, group):
    rows = (mixed * (1.0 / total)).T.astype(out_ref.dtype)
    for h in range(group):
        at = (g * group + h) * HD
        out_ref[pl.ds(tile * TILE, TILE), at : at + HD] = rows[h * TILE : (h + 1) * TILE]


def scores_of(keys, q):
    return lax.dot_general(keys, q, NT, preferred_element_type=jnp.float32)


def absorb(state, s, v):
    if state is None:
        new_top = jnp.max(s, axis=0, keepdims=True)
    else:
        top, total, mixed = state
        new_top = jnp.maximum(top, jnp.max(s, axis=0, keepdims=True))
    w = jnp.exp2((s - new_top) * EXP_SCALE)
    added = jnp.sum(w, axis=0, keepdims=True)
    product = lax.dot_general(v, w.astype(jnp.bfloat16), NN, preferred_element_type=jnp.float32)
    if state is None:
        return new_top, added, product
    decay = jnp.exp2((top - new_top) * EXP_SCALE)
    return new_top, total * decay + added, mixed * decay + product


def staggered(units, score, finish):
    waiting = None
    for unit in units:
        s = score(*unit)
        if waiting is not None:
            finish(*waiting)
        waiting = (*unit, s)
    finish(*waiting)


def row_positions(first, height):
    return first + (lax.broadcasted_iota(jnp.int32, (1, height), 1) & (TILE - 1))


def lay(keys_at, flipped_at, ref, rows, kv_heads, g):
    keys_at[...] = ref[rows, g * HD : (g + 1) * HD]
    flipped_at[...] = ref[rows, (kv_heads + g) * HD : (kv_heads + g + 1) * HD].T


def self_kernel(
    lengths_ref, place_ref, q_ref, *refs, kv_heads, group, spans, parts, samples, begin, end
):
    refs = list(refs)
    take = lambda n: [refs.pop(0) for _ in range(n)]
    pieces = take(len({part[1] for part in parts}))
    stat_in, mixed_in = (None, None) if begin else take(2)
    out_ref = take(1)[0] if end else None
    stat_ref, mixed_ref, keys_ref, flipped_ref = take(4)
    rows_here = q_ref.shape[0]
    tiles = rows_here // TILE
    height = group * TILE
    base = place_ref[0] * rows_here
    _, ends = sample_bounds(lengths_ref, samples)
    ats = [sum(count for _, count in spans[:n]) for n in range(len(spans))]

    lows = []
    for tile in range(tiles):
        low = jnp.int32(0)
        for e in ends:
            low = jnp.where(e <= base + tile * TILE, e, low)
        lows.append(low)

    def limits(number):
        back, count = spans[number]
        past = base - (back - 1) * rows_here
        return past - count, past

    def reached(number):
        start, past = limits(number)
        many = jnp.int32(0)
        for low in lows:
            many = many + (low < past).astype(jnp.int32)
        return jnp.where(start >= 0, many, 0)

    counts = [reached(number) for number in range(len(spans))]
    for number, source, at, offset, count, only in parts:

        def fill(number=number, source=source, at=at, offset=offset, count=count):
            here = slice(ats[number] + offset, ats[number] + offset + count)
            for g in range(kv_heads):
                lay(
                    keys_ref.at[g, here], flipped_ref.at[g, :, here], pieces[source],
                    slice(at, at + count), kv_heads, g,
                )

        if spans[number][0] == 0:
            fill()
        else:
            asked = counts[number] > 0
            if only is not None:
                asked = asked & (place_ref[0] == only)
            pl.when(asked)(fill)

    def starts_of(first):
        row_t = row_positions(first, height)
        row_start = jnp.zeros((1, height), jnp.int32)
        for e in ends:
            row_start = jnp.where(e <= row_t, e, row_start)
        return row_start, row_t

    def keep(tile, g, state):
        stat_ref[tile, g, 0:1, :] = state[0]
        stat_ref[tile, g, 1:2, :] = state[1]
        mixed_ref[tile, g] = state[2]

    def own_count(tile):
        return min(rows_here, -(-(tile + 1) * TILE // HD) * HD)

    def own_scores(tile, g):
        q = stacked_queries(q_ref, tile, g, group)
        return scores_of(keys_ref[g, : own_count(tile)], q)

    def own_finish(tile, g, s):
        row_start, row_t = starts_of(base + tile * TILE)
        key_t = base + lax.broadcasted_iota(jnp.int32, (own_count(tile), 1), 0)
        s = jnp.where((key_t >= row_start) & (key_t <= row_t), s, LOW)
        keep(tile, g, absorb(None, s, flipped_ref[g, :, : own_count(tile)]))

    if begin:
        staggered(
            [(tile, g) for tile in range(tiles) for g in range(kv_heads)], own_scores, own_finish
        )
    else:
        stat_ref[...] = stat_in[...]
        mixed_ref[...] = mixed_in[...]

    together = math.gcd(tiles, TOGETHER)
    for number in range(1 if begin else 0, len(spans)):
        start, _ = limits(number)
        at, count = ats[number], spans[number][1]

        @pl.loop(0, (counts[number] + together - 1) // together)
        def _(turn, start=start, at=at, count=count):
            def scores(n, g):
                q = stacked_queries(q_ref, turn * together + n, g, group)
                return scores_of(keys_ref[g, at : at + count], q)

            def finish(n, g, s):
                tile = turn * together + n
                row_start, _ = starts_of(base + tile * TILE)
                key_t = start + lax.broadcasted_iota(jnp.int32, (count, 1), 0)
                s = jnp.where(key_t >= row_start, s, LOW)
                old = stat_ref[tile, g, 0:1, :], stat_ref[tile, g, 1:2, :], mixed_ref[tile, g]
                keep(tile, g, absorb(old, s, flipped_ref[g, :, at : at + count]))

            staggered(
                [(n, g) for n in range(together) for g in range(kv_heads)], scores, finish
            )

    for tile in range(tiles if end else 0):
        for g in range(kv_heads):
            write_heads(out_ref, mixed_ref[tile, g], stat_ref[tile, g, 1:2, :], tile, g, group)


def cross_kernel(
    lengths_ref, images_ref, place_ref, q_ref, *refs, kv_heads, group, sources, samples, begin, end, heads
):
    refs = list(refs)
    take = lambda n: [refs.pop(0) for _ in range(n)]
    pieces = [take(len(source)) for source in sources]
    stat_in, mixed_in = (None, None) if begin else take(2)
    if end and heads[0] > 0:
        take(1)
    out_ref = take(1)[0] if end else None
    stat_ref, mixed_ref, keys_ref, flipped_ref = take(4)
    rows_ref, copied = take(2) if end else (None, None)
    rows_here = q_ref.shape[0]
    tiles = rows_here // TILE
    height = group * TILE
    base = place_ref[0] * rows_here
    starts, _ = sample_bounds(lengths_ref, samples)
    image_count = keys_ref.shape[0]

    def fill(ref, at, row, parts, each):
        held = ref.shape[1] // HD // 2
        for n, g in enumerate(heads):
            k_at = (g if held == kv_heads else n) * HD
            v_at = k_at + held * HD
            for image in range(image_count):
                values = []
                for part in range(parts):
                    first = row + (part * image_count + image) * each
                    here = slice(at + part * each, at + (part + 1) * each)
                    keys_ref[image, n, here] = ref[first : first + each, k_at : k_at + HD]
                    values.append(ref[first : first + each, v_at : v_at + HD])
                whole = jnp.concatenate(values, axis=0)
                flipped_ref[image, n, :, at : at + parts * each] = whole.T

    at = 0
    for source, given in zip(sources, pieces):
        for number, ((row, parts, each), ref) in enumerate(zip(source, given)):
            put = functools.partial(fill, ref, at, row, parts, each)
            if len(source) == 1:
                put()
            else:
                pl.when(place_ref[1] == 1 - number)(put)
        at += source[0][1] * source[0][2]

    def images_of(tile):
        first = base + tile * TILE
        row_t = row_positions(first, height)
        row_image = jnp.zeros((1, height), jnp.int32)
        leading = jnp.int32(0)
        for j in range(samples):
            row_image = jnp.where(row_t >= starts[j], images_ref[0, j], row_image)
            leading = jnp.where(first >= starts[j], images_ref[0, j], leading)
        return row_image, leading

    def keep(tile, g, state):
        stat_ref[tile, g, 0:1, :] = state[0]
        stat_ref[tile, g, 1:2, :] = state[1]
        mixed_ref[tile, g] = state[2]

    def chosen(mine, new, old):
        if old is None:
            old = LOW, 0.0, 0.0
        return [jnp.where(mine, n, o) for n, o in zip(new, old)]

    marks = [images_of(tile) for tile in range(tiles)]
    order = range(len(heads))

    def scores(tile, n):
        return scores_of(
            keys_ref[marks[tile][1], n], stacked_queries(q_ref, tile, heads[n], group)
        )

    def finish(tile, n, s):
        row_image, leading = marks[tile]
        old, g = None, heads[n]
        if not begin:
            old = stat_in[tile, g, 0:1, :], stat_in[tile, g, 1:2, :], mixed_in[tile, g]
        new = absorb(old, s, flipped_ref[leading, n])
        keep(tile, n, chosen(row_image == leading, new, old))

    staggered([(tile, n) for tile in range(tiles) for n in order], scores, finish)

    @pl.loop(0, tiles)
    def _(tile):
        first = base + tile * TILE
        leading, others = jnp.int32(0), [jnp.bool_(False)] * image_count
        for j in range(samples):
            leading = jnp.where(first >= starts[j], images_ref[0, j], leading)
        for j in range(samples):
            inside = (starts[j] > first) & (starts[j] < first + TILE)
            for image in range(image_count):
                others[image] = others[image] | (inside & (images_ref[0, j] == image))
        for image in range(image_count):

            @pl.when(others[image] & (leading != image))
            def _(image=image):
                row_image, _ = images_of(tile)
                olds = [
                    (stat_ref[tile, n, 0:1, :], stat_ref[tile, n, 1:2, :], mixed_ref[tile, n])
                    for n in order
                ]
                ss = [
                    scores_of(keys_ref[image, n], stacked_queries(q_ref, tile, heads[n], group))
                    for n in order
                ]
                for n in order:
                    new = absorb(olds[n], ss[n], flipped_ref[image, n])
                    keep(tile, n, chosen(row_image == image, new, olds[n]))

    if not end:
        return
    share = len(heads) * group * HD
    pace = 2
    copies = []
    for tile in range(tiles):
        for n in order:
            write_heads(rows_ref, mixed_ref[tile, n], stat_ref[tile, n, 1:2, :], tile, n, group)
        if (tile + 1) % pace == 0 or tile + 1 == tiles:
            done = slice(len(copies) * pace * TILE, (tile + 1) * TILE)
            copy = pltpu.make_async_copy(
                rows_ref.at[done],
                out_ref.at[done, heads[0] * group * HD : heads[0] * group * HD + share],
                copied.at[len(copies)],
            )
            copy.start()
            copies.append(copy)
    for copy in copies:
        copy.wait()


def smem():
    return pl.BlockSpec(memory_space=pltpu.SMEM)


def vmem():
    return pl.BlockSpec(memory_space=pltpu.VMEM)


def cost(rows, width, keys):
    return pl.CostEstimate(
        flops=8 * rows * width * keys, bytes_accessed=4 * rows * width,
        transcendentals=rows * (width // HD) * keys,
    )


def join_kernel(passed_ref, rows_ref, out_ref):
    half = passed_ref.shape[0] // 2
    count = rows_ref.shape[0]
    out_ref[:half] = passed_ref[half:]
    out_ref[half : half + count] = rows_ref[...]
    out_ref[half + count :] = passed_ref[:half]


def joined(passed, own_rows):
    total, width = passed.shape[0] + own_rows.shape[0], passed.shape[1]
    return pl.pallas_call(
        join_kernel,
        out_shape=jax.ShapeDtypeStruct((total, width), passed.dtype),
        in_specs=[vmem(), vmem()],
        out_specs=vmem(),
        cost_estimate=pl.CostEstimate(
            flops=0, bytes_accessed=4 * total * width, transcendentals=0
        ),
    )(passed, own_rows)


def state_shapes(rows, kv_heads, group):
    tiles, height = rows // TILE, group * TILE
    return (tiles, kv_heads, 8, height), (tiles, kv_heads, HD, height)


def state_call(
    kernel, operands, rows, width, keys, shapes, scratch, end, dtype, placed=False, rest=None
):
    scalars = sum(x.dtype == jnp.int32 for x in operands)
    state_scratch = []
    if end:
        out_shape = jax.ShapeDtypeStruct((rows, width), dtype)
        state_scratch = [pltpu.VMEM(s, jnp.float32) for s in shapes]
    else:
        out_shape = [jax.ShapeDtypeStruct(s, jnp.float32) for s in shapes]
    anywhere = pl.BlockSpec(memory_space=pl.ANY)
    in_specs = [smem()] * scalars + [vmem()] * (len(operands) - scalars)
    aliases = {}
    if rest is not None:
        aliases = {len(operands): 0}
        operands, in_specs = (*operands, rest), in_specs + [anywhere]
    return pl.pallas_call(
        kernel,
        out_shape=out_shape,
        in_specs=in_specs,
        out_specs=(anywhere if placed else vmem()) if end else [vmem(), vmem()],
        scratch_shapes=state_scratch + scratch,
        input_output_aliases=aliases,
        compiler_params=pltpu.CompilerParams(vmem_limit_bytes=28 << 20),
        cost_estimate=cost(rows, width, keys),
    )(*operands)


def self_attention(lengths, place, q, pieces, spans, parts, state, end, kv_heads, group):
    rows, width = q.shape
    keys = sum(count for _, count in spans)
    begin = state is None
    kernel = functools.partial(
        self_kernel, kv_heads=kv_heads, group=group, spans=spans, parts=parts,
        samples=lengths.shape[1], begin=begin, end=end,
    )
    scratch = [
        pltpu.VMEM((kv_heads, keys, HD), q.dtype), pltpu.VMEM((kv_heads, HD, keys), q.dtype)
    ]
    operands = (lengths, place, q, *pieces, *(() if begin else state))
    shapes = state_shapes(rows, kv_heads, group)
    return state_call(kernel, operands, rows, width, keys, shapes, scratch, end, q.dtype)


def cross_attention(
    lengths, images, place, q, sources, state, end, kv_heads, group, image_count,
    heads=None, rest=None,
):
    heads = tuple(range(kv_heads)) if heads is None else heads
    rows, width = q.shape
    begin = state is None
    kernel = functools.partial(
        cross_kernel, kv_heads=kv_heads, group=group, heads=heads,
        sources=tuple(tuple(piece[1:] for piece in source) for source in sources),
        samples=lengths.shape[1], begin=begin, end=end,
    )
    pieces = [piece[0] for source in sources for piece in source]
    keys = sum(source[0][2] * source[0][3] for source in sources)
    scratch = [
        pltpu.VMEM((image_count, len(heads), keys, HD), q.dtype),
        pltpu.VMEM((image_count, len(heads), HD, keys), q.dtype),
    ]
    if end:
        scratch += [
            pltpu.VMEM((rows, len(heads) * group * HD), q.dtype),
            pltpu.SemaphoreType.DMA((rows // TILE,)),
        ]
    operands = (lengths, images, place, q, *pieces, *(() if begin else state))
    shapes = state_shapes(rows, len(heads), group)
    return state_call(
        kernel, operands, rows, width, keys, shapes, scratch, end, q.dtype, True, rest
    )


def per_device(q_self, kv_self, q_cross, kv_cross, sample_lengths, sample_image, *, n_pipe, n_ctx):
    rows = q_self.shape[1]
    kv_heads = kv_self.shape[3] // HD
    group = q_self.shape[2] // HD // kv_heads
    image_count, each = kv_cross.shape[1:3]
    z = lax.axis_index("ctx")
    inner = ((z == 1) | (z == 2)).astype(jnp.int32)
    place = jnp.stack([z, inner]).astype(jnp.int32)

    shift = lambda piece, step: lax.ppermute(
        piece, "ctx", [(c, c + 1) for c in range(step - 1, n_ctx - 1)]
    )
    passed = shift(kv_self[0], 1)
    arrived = lax.all_to_all(kv_cross, "pipe", split_axis=0, concat_axis=0, tiled=True)
    arrived, passed = lax.optimization_barrier((arrived, passed))
    own = kv_self[0].reshape(rows, -1)
    passed = passed.reshape(rows, -1)
    own_rows = arrived.reshape(-1, own.shape[1])
    cross_rows = own_rows.shape[0]
    longest = rows * n_ctx * 5 // 8

    attend_self = functools.partial(
        self_attention, sample_lengths, place, q_self[0], kv_heads=kv_heads, group=group
    )
    attend_cross = functools.partial(
        cross_attention, sample_lengths, sample_image, place, q_cross[0],
        kv_heads=kv_heads, group=group, image_count=image_count,
    )
    if n_ctx == 4:
        half = rows // 2
        block = joined(passed, own_rows)
        at = lambda array, row: (array, row, n_pipe, each)
        near = lax.ppermute(block, "ctx", [(1, 2), (2, 1)])
        pair = lax.ppermute(block, "ctx", [(0, 1), (1, 0), (2, 3), (3, 2)])
        early = ((0, rows), (1, rows))
        parts = ((0, 0, 0, 0, rows, None), (1, 1, 0, 0, rows, None))
        state = attend_cross([[at(own_rows, 0)]], None, False)
        self_state = attend_self([own, passed], early, parts, None, False)
        near, state = lax.optimization_barrier((near, state))
        pair, self_state = lax.optimization_barrier((pair, self_state))
        columns = lambda j: pair[half : half + cross_rows, j * HD : (j + 1) * HD]
        far = [
            lax.ppermute(
                jnp.concatenate([columns(g), columns(kv_heads + g)], axis=1),
                "ctx", [(1, 2), (2, 1)],
            )
            for g in range(kv_heads)
        ]
        near_on = lax.ppermute(near[: half + cross_rows], "ctx", [(1, 0), (2, 3)])
        state = attend_cross([[at(pair, half)]], state, False)
        far[0], state = lax.optimization_barrier((far[0], state))
        low = half + cross_rows
        parts = (
            (0, 0, low, 0, half, 2),
            (0, 0, 0, half, half, 2),
            (0, 1, low, 0, half, 3),
            (0, 1, 0, half, half, 3),
        )
        self_state = attend_self([near, pair], ((2, rows),), parts, self_state, False)
        far[-1], self_state = lax.optimization_barrier((far[-1], self_state))
        far_on = [lax.ppermute(part, "ctx", [(1, 0), (2, 3)]) for part in far]
        state = attend_cross([[at(near, half), at(near_on, half)]], state, False)
        parts = ((0, 0, 0, 0, half, 3),)
        self_out = attend_self([near_on], ((3, half),), parts, self_state, True)
        cross_out = None
        for g in range(kv_heads):
            cross_out = attend_cross(
                [[at(far[g], 0), at(far_on[g], 0)]], state, True, heads=(g,), rest=cross_out
            )
    else:
        pieces, spans, left, step = [own, passed], [(0, rows), (1, rows)], longest - 1 - rows, 1
        while left > 0 and step < n_ctx - 1:
            step += 1
            count = min(rows, -(-left // HD) * HD)
            pieces.append(shift(pieces[-1][rows - count :], step))
            spans.append((step, count))
            left -= rows
        parts = tuple((n, n, 0, 0, count, None) for n, (_, count) in enumerate(spans))
        self_out = attend_self(pieces, tuple(spans), parts, None, True)
        gathered = lax.all_gather(own_rows, "ctx", axis=0, tiled=True)
        cross_out = attend_cross([[(gathered, 0, n_ctx * n_pipe, each)]], None, True)
    return self_out[None], cross_out[None]


def solution(mesh):
    in_specs = (
        P("pipe", "ctx", "tp"),
        P("pipe", "ctx", None, "tp"),
        P("pipe", "ctx", "tp"),
        P(None, None, ("pipe", "ctx"), None, "tp"),
        P("pipe", None),
        P("pipe", None),
    )
    out_specs = (P("pipe", "ctx", "tp"), P("pipe", "ctx", "tp"))
    body = functools.partial(
        per_device, n_pipe=mesh.shape["pipe"], n_ctx=mesh.shape["ctx"]
    )
    return jax.shard_map(
        body, mesh=mesh, in_specs=in_specs, out_specs=out_specs, check_vma=False
    )
```

```python
import functools
import math

import jax
import jax.numpy as jnp
from jax import lax
from jax.experimental import pallas as pl
from jax.experimental.pallas import tpu as pltpu
from jax.sharding import PartitionSpec as P

HD = 128
TILE = 32
TOGETHER = 4
LOW = -1e30
EXP_SCALE = math.log2(math.e) / math.sqrt(HD)
NT = (((1,), (1,)), ((), ()))
NN = (((1,), (0,)), ((), ()))


def sample_bounds(lengths_ref, count):
    starts, ends, total = [], [], jnp.int32(0)
    for j in range(count):
        starts.append(total)
        total = total + lengths_ref[0, j]
        ends.append(total)
    return starts, ends


def stacked_queries(q_ref, tile, g, group):
    first = g * group
    rows = pl.ds(tile * TILE, TILE)
    return jnp.concatenate(
        [q_ref[rows, (first + h) * HD : (first + h + 1) * HD] for h in range(group)], axis=0
    )


def write_heads(out_ref, mixed, total, tile, g, group):
    rows = (mixed * (1.0 / total)).T.astype(out_ref.dtype)
    for h in range(group):
        at = (g * group + h) * HD
        out_ref[pl.ds(tile * TILE, TILE), at : at + HD] = rows[h * TILE : (h + 1) * TILE]


def scores_of(keys, q):
    return lax.dot_general(keys, q, NT, preferred_element_type=jnp.float32)


def absorb(state, s, v):
    if state is None:
        new_top = jnp.max(s, axis=0, keepdims=True)
    else:
        top, total, mixed = state
        new_top = jnp.maximum(top, jnp.max(s, axis=0, keepdims=True))
    w = jnp.exp2((s - new_top) * EXP_SCALE)
    added = jnp.sum(w, axis=0, keepdims=True)
    product = lax.dot_general(v, w.astype(jnp.bfloat16), NN, preferred_element_type=jnp.float32)
    if state is None:
        return new_top, added, product
    decay = jnp.exp2((top - new_top) * EXP_SCALE)
    return new_top, total * decay + added, mixed * decay + product


def staggered(units, score, finish):
    waiting = None
    for unit in units:
        s = score(*unit)
        if waiting is not None:
            finish(*waiting)
        waiting = (*unit, s)
    finish(*waiting)


def row_positions(first, height):
    return first + (lax.broadcasted_iota(jnp.int32, (1, height), 1) & (TILE - 1))


def lay(keys_at, flipped_at, ref, rows, kv_heads, g):
    keys_at[...] = ref[rows, g * HD : (g + 1) * HD]
    flipped_at[...] = ref[rows, (kv_heads + g) * HD : (kv_heads + g + 1) * HD].T


def self_kernel(
    lengths_ref, place_ref, q_ref, *refs, kv_heads, group, spans, parts, samples, begin, end
):
    refs = list(refs)
    take = lambda n: [refs.pop(0) for _ in range(n)]
    pieces = take(len({part[1] for part in parts}))
    stat_in, mixed_in = (None, None) if begin else take(2)
    out_ref = take(1)[0] if end else None
    stat_ref, mixed_ref, keys_ref, flipped_ref = take(4)
    rows_here = q_ref.shape[0]
    tiles = rows_here // TILE
    height = group * TILE
    base = place_ref[0] * rows_here
    _, ends = sample_bounds(lengths_ref, samples)
    ats = [sum(count for _, count in spans[:n]) for n in range(len(spans))]

    lows = []
    for tile in range(tiles):
        low = jnp.int32(0)
        for e in ends:
            low = jnp.where(e <= base + tile * TILE, e, low)
        lows.append(low)

    def limits(number):
        back, count = spans[number]
        past = base - (back - 1) * rows_here
        return past - count, past

    def reached(number):
        start, past = limits(number)
        many = jnp.int32(0)
        for low in lows:
            many = many + (low < past).astype(jnp.int32)
        return jnp.where(start >= 0, many, 0)

    counts = [reached(number) for number in range(len(spans))]
    for number, source, at, offset, count, only in parts:

        def fill(number=number, source=source, at=at, offset=offset, count=count):
            here = slice(ats[number] + offset, ats[number] + offset + count)
            for g in range(kv_heads):
                lay(
                    keys_ref.at[g, here], flipped_ref.at[g, :, here], pieces[source],
                    slice(at, at + count), kv_heads, g,
                )

        if spans[number][0] == 0:
            fill()
        else:
            asked = counts[number] > 0
            if only is not None:
                asked = asked & (place_ref[0] == only)
            pl.when(asked)(fill)

    def starts_of(first):
        row_t = row_positions(first, height)
        row_start = jnp.zeros((1, height), jnp.int32)
        for e in ends:
            row_start = jnp.where(e <= row_t, e, row_start)
        return row_start, row_t

    def keep(tile, g, state):
        stat_ref[tile, g, 0:1, :] = state[0]
        stat_ref[tile, g, 1:2, :] = state[1]
        mixed_ref[tile, g] = state[2]

    def own_count(tile):
        return min(rows_here, -(-(tile + 1) * TILE // HD) * HD)

    def own_scores(tile, g):
        q = stacked_queries(q_ref, tile, g, group)
        return scores_of(keys_ref[g, : own_count(tile)], q)

    def own_finish(tile, g, s):
        row_start, row_t = starts_of(base + tile * TILE)
        key_t = base + lax.broadcasted_iota(jnp.int32, (own_count(tile), 1), 0)
        s = jnp.where((key_t >= row_start) & (key_t <= row_t), s, LOW)
        keep(tile, g, absorb(None, s, flipped_ref[g, :, : own_count(tile)]))

    if begin:
        staggered(
            [(tile, g) for tile in range(tiles) for g in range(kv_heads)], own_scores, own_finish
        )
    else:
        stat_ref[...] = stat_in[...]
        mixed_ref[...] = mixed_in[...]

    together = math.gcd(tiles, TOGETHER)
    for number in range(1 if begin else 0, len(spans)):
        start, _ = limits(number)
        at, count = ats[number], spans[number][1]

        @pl.loop(0, (counts[number] + together - 1) // together)
        def _(turn, start=start, at=at, count=count):
            def scores(n, g):
                q = stacked_queries(q_ref, turn * together + n, g, group)
                return scores_of(keys_ref[g, at : at + count], q)

            def finish(n, g, s):
                tile = turn * together + n
                row_start, _ = starts_of(base + tile * TILE)
                key_t = start + lax.broadcasted_iota(jnp.int32, (count, 1), 0)
                s = jnp.where(key_t >= row_start, s, LOW)
                old = stat_ref[tile, g, 0:1, :], stat_ref[tile, g, 1:2, :], mixed_ref[tile, g]
                keep(tile, g, absorb(old, s, flipped_ref[g, :, at : at + count]))

            staggered(
                [(n, g) for n in range(together) for g in range(kv_heads)], scores, finish
            )

    for tile in range(tiles if end else 0):
        for g in range(kv_heads):
            write_heads(out_ref, mixed_ref[tile, g], stat_ref[tile, g, 1:2, :], tile, g, group)


def cross_kernel(
    lengths_ref, images_ref, place_ref, q_ref, *refs, kv_heads, group, sources, samples, begin, end, heads
):
    refs = list(refs)
    take = lambda n: [refs.pop(0) for _ in range(n)]
    pieces = [take(len(source)) for source in sources]
    stat_in, mixed_in = (None, None) if begin else take(2)
    if end and heads[0] > 0:
        take(1)
    out_ref = take(1)[0] if end else None
    stat_ref, mixed_ref, keys_ref, flipped_ref = take(4)
    rows_ref, copied = take(2) if end else (None, None)
    rows_here = q_ref.shape[0]
    tiles = rows_here // TILE
    height = group * TILE
    base = place_ref[0] * rows_here
    starts, _ = sample_bounds(lengths_ref, samples)
    image_count = keys_ref.shape[0]

    def fill(ref, at, row, parts, each):
        held = ref.shape[1] // HD // 2
        for n, g in enumerate(heads):
            k_at = (g if held == kv_heads else n) * HD
            v_at = k_at + held * HD
            for image in range(image_count):
                values = []
                for part in range(parts):
                    first = row + (part * image_count + image) * each
                    here = slice(at + part * each, at + (part + 1) * each)
                    keys_ref[image, n, here] = ref[first : first + each, k_at : k_at + HD]
                    values.append(ref[first : first + each, v_at : v_at + HD])
                whole = jnp.concatenate(values, axis=0)
                flipped_ref[image, n, :, at : at + parts * each] = whole.T

    at = 0
    for source, given in zip(sources, pieces):
        for number, ((row, parts, each), ref) in enumerate(zip(source, given)):
            put = functools.partial(fill, ref, at, row, parts, each)
            if len(source) == 1:
                put()
            else:
                pl.when(place_ref[1] == 1 - number)(put)
        at += source[0][1] * source[0][2]

    def images_of(tile):
        first = base + tile * TILE
        row_t = row_positions(first, height)
        row_image = jnp.zeros((1, height), jnp.int32)
        leading = jnp.int32(0)
        for j in range(samples):
            row_image = jnp.where(row_t >= starts[j], images_ref[0, j], row_image)
            leading = jnp.where(first >= starts[j], images_ref[0, j], leading)
        return row_image, leading

    def keep(tile, g, state):
        stat_ref[tile, g, 0:1, :] = state[0]
        stat_ref[tile, g, 1:2, :] = state[1]
        mixed_ref[tile, g] = state[2]

    def chosen(mine, new, old):
        if old is None:
            old = LOW, 0.0, 0.0
        return [jnp.where(mine, n, o) for n, o in zip(new, old)]

    marks = [images_of(tile) for tile in range(tiles)]
    order = range(len(heads))

    def scores(tile, n):
        return scores_of(
            keys_ref[marks[tile][1], n], stacked_queries(q_ref, tile, heads[n], group)
        )

    def finish(tile, n, s):
        row_image, leading = marks[tile]
        old, g = None, heads[n]
        if not begin:
            old = stat_in[tile, g, 0:1, :], stat_in[tile, g, 1:2, :], mixed_in[tile, g]
        new = absorb(old, s, flipped_ref[leading, n])
        keep(tile, n, chosen(row_image == leading, new, old))

    staggered([(tile, n) for tile in range(tiles) for n in order], scores, finish)

    @pl.loop(0, tiles)
    def _(tile):
        first = base + tile * TILE
        leading, others = jnp.int32(0), [jnp.bool_(False)] * image_count
        for j in range(samples):
            leading = jnp.where(first >= starts[j], images_ref[0, j], leading)
        for j in range(samples):
            inside = (starts[j] > first) & (starts[j] < first + TILE)
            for image in range(image_count):
                others[image] = others[image] | (inside & (images_ref[0, j] == image))
        for image in range(image_count):

            @pl.when(others[image] & (leading != image))
            def _(image=image):
                row_image, _ = images_of(tile)
                olds = [
                    (stat_ref[tile, n, 0:1, :], stat_ref[tile, n, 1:2, :], mixed_ref[tile, n])
                    for n in order
                ]
                ss = [
                    scores_of(keys_ref[image, n], stacked_queries(q_ref, tile, heads[n], group))
                    for n in order
                ]
                for n in order:
                    new = absorb(olds[n], ss[n], flipped_ref[image, n])
                    keep(tile, n, chosen(row_image == image, new, olds[n]))

    if not end:
        return
    share = len(heads) * group * HD
    pace = 2
    copies = []
    for tile in range(tiles):
        for n in order:
            write_heads(rows_ref, mixed_ref[tile, n], stat_ref[tile, n, 1:2, :], tile, n, group)
        if (tile + 1) % pace == 0 or tile + 1 == tiles:
            done = slice(len(copies) * pace * TILE, (tile + 1) * TILE)
            copy = pltpu.make_async_copy(
                rows_ref.at[done],
                out_ref.at[done, heads[0] * group * HD : heads[0] * group * HD + share],
                copied.at[len(copies)],
            )
            copy.start()
            copies.append(copy)
    for copy in copies:
        copy.wait()


def smem():
    return pl.BlockSpec(memory_space=pltpu.SMEM)


def vmem():
    return pl.BlockSpec(memory_space=pltpu.VMEM)


def cost(rows, width, keys):
    return pl.CostEstimate(
        flops=8 * rows * width * keys, bytes_accessed=4 * rows * width,
        transcendentals=rows * (width // HD) * keys,
    )


def state_shapes(rows, kv_heads, group):
    tiles, height = rows // TILE, group * TILE
    return (tiles, kv_heads, 8, height), (tiles, kv_heads, HD, height)


def state_call(
    kernel, operands, rows, width, keys, shapes, scratch, end, dtype, placed=False, rest=None
):
    scalars = sum(x.dtype == jnp.int32 for x in operands)
    state_scratch = []
    if end:
        out_shape = jax.ShapeDtypeStruct((rows, width), dtype)
        state_scratch = [pltpu.VMEM(s, jnp.float32) for s in shapes]
    else:
        out_shape = [jax.ShapeDtypeStruct(s, jnp.float32) for s in shapes]
    anywhere = pl.BlockSpec(memory_space=pl.ANY)
    in_specs = [smem()] * scalars + [vmem()] * (len(operands) - scalars)
    aliases = {}
    if rest is not None:
        aliases = {len(operands): 0}
        operands, in_specs = (*operands, rest), in_specs + [anywhere]
    return pl.pallas_call(
        kernel,
        out_shape=out_shape,
        in_specs=in_specs,
        out_specs=(anywhere if placed else vmem()) if end else [vmem(), vmem()],
        scratch_shapes=state_scratch + scratch,
        input_output_aliases=aliases,
        compiler_params=pltpu.CompilerParams(vmem_limit_bytes=28 << 20),
        cost_estimate=cost(rows, width, keys),
    )(*operands)


def self_attention(lengths, place, q, pieces, spans, parts, state, end, kv_heads, group):
    rows, width = q.shape
    keys = sum(count for _, count in spans)
    begin = state is None
    kernel = functools.partial(
        self_kernel, kv_heads=kv_heads, group=group, spans=spans, parts=parts,
        samples=lengths.shape[1], begin=begin, end=end,
    )
    scratch = [
        pltpu.VMEM((kv_heads, keys, HD), q.dtype), pltpu.VMEM((kv_heads, HD, keys), q.dtype)
    ]
    operands = (lengths, place, q, *pieces, *(() if begin else state))
    shapes = state_shapes(rows, kv_heads, group)
    return state_call(kernel, operands, rows, width, keys, shapes, scratch, end, q.dtype)


def cross_attention(
    lengths, images, place, q, sources, state, end, kv_heads, group, image_count,
    heads=None, rest=None,
):
    heads = tuple(range(kv_heads)) if heads is None else heads
    rows, width = q.shape
    begin = state is None
    kernel = functools.partial(
        cross_kernel, kv_heads=kv_heads, group=group, heads=heads,
        sources=tuple(tuple(piece[1:] for piece in source) for source in sources),
        samples=lengths.shape[1], begin=begin, end=end,
    )
    pieces = [piece[0] for source in sources for piece in source]
    keys = sum(source[0][2] * source[0][3] for source in sources)
    scratch = [
        pltpu.VMEM((image_count, len(heads), keys, HD), q.dtype),
        pltpu.VMEM((image_count, len(heads), HD, keys), q.dtype),
    ]
    if end:
        scratch += [
            pltpu.VMEM((rows, len(heads) * group * HD), q.dtype),
            pltpu.SemaphoreType.DMA((rows // TILE,)),
        ]
    operands = (lengths, images, place, q, *pieces, *(() if begin else state))
    shapes = state_shapes(rows, len(heads), group)
    return state_call(
        kernel, operands, rows, width, keys, shapes, scratch, end, q.dtype, True, rest
    )


def per_device(q_self, kv_self, q_cross, kv_cross, sample_lengths, sample_image, *, n_pipe, n_ctx):
    rows = q_self.shape[1]
    kv_heads = kv_self.shape[3] // HD
    group = q_self.shape[2] // HD // kv_heads
    image_count, each = kv_cross.shape[1:3]
    z = lax.axis_index("ctx")
    inner = ((z == 1) | (z == 2)).astype(jnp.int32)
    place = jnp.stack([z, inner]).astype(jnp.int32)

    shift = lambda piece, step: lax.ppermute(
        piece, "ctx", [(c, c + 1) for c in range(step - 1, n_ctx - 1)]
    )
    passed = shift(kv_self[0], 1)
    arrived = lax.all_to_all(kv_cross, "pipe", split_axis=0, concat_axis=0, tiled=True)
    arrived, passed = lax.optimization_barrier((arrived, passed))
    flat = lambda array: array.reshape(-1, array.shape[-2] * array.shape[-1])
    own = flat(kv_self)
    longest = rows * n_ctx * 5 // 8

    attend_self = functools.partial(
        self_attention, sample_lengths, place, q_self[0], kv_heads=kv_heads, group=group
    )
    attend_cross = functools.partial(
        cross_attention, sample_lengths, sample_image, place, q_cross[0],
        kv_heads=kv_heads, group=group, image_count=image_count,
    )
    if n_ctx == 4:
        half = rows // 2
        at = lambda array: (array, 0, n_pipe, each)
        near = lax.ppermute(arrived, "ctx", [(1, 2), (2, 1)])
        pair = lax.ppermute(arrived, "ctx", [(0, 1), (1, 0), (2, 3), (3, 2)])
        state = attend_cross([[at(flat(arrived))]], None, False)
        passed, state = lax.optimization_barrier((passed, state))
        two_back = lax.ppermute(passed, "ctx", [(1, 2), (2, 3)])
        three_back = lax.ppermute(passed[half:], "ctx", [(1, 3)])
        early = ((0, rows), (1, rows))
        parts = ((0, 0, 0, 0, rows, None), (1, 1, 0, 0, rows, None))
        self_state = attend_self([own, flat(passed)], early, parts, None, False)
        near, state = lax.optimization_barrier((near, state))
        pair, two_back, three_back, self_state = lax.optimization_barrier(
            (pair, two_back, three_back, self_state)
        )

        near = flat(near)
        near_on = lax.ppermute(near, "ctx", [(1, 0), (2, 3)])
        far = [
            lax.ppermute(flat(pair[..., g * HD : (g + 1) * HD]), "ctx", [(1, 2), (2, 1)])
            for g in range(kv_heads)
        ]
        state = attend_cross([[at(flat(pair))]], state, False)
        far[0], state = lax.optimization_barrier((far[0], state))
        late = ((2, rows), (3, half))
        parts = ((0, 0, 0, 0, rows, None), (1, 1, 0, 0, half, 3))
        self_out = attend_self([flat(two_back), flat(three_back)], late, parts, self_state, True)
        far[-1], self_out = lax.optimization_barrier((far[-1], self_out))
        far_on = [lax.ppermute(part, "ctx", [(1, 0), (2, 3)]) for part in far]
        state = attend_cross([[at(near), at(near_on)]], state, False)
        cross_out = None
        for g in range(kv_heads):
            cross_out = attend_cross(
                [[at(far[g]), at(far_on[g])]], state, True, heads=(g,), rest=cross_out
            )
    else:
        pieces, spans = [own, flat(passed)], [(0, rows), (1, rows)]
        left, step = longest - 1 - rows, 1
        while left > 0 and step < n_ctx - 1:
            step += 1
            count = min(rows, -(-left // HD) * HD)
            pieces.append(shift(pieces[-1][rows - count :], step))
            spans.append((step, count))
            left -= rows
        parts = tuple((n, n, 0, 0, count, None) for n, (_, count) in enumerate(spans))
        self_out = attend_self(pieces, tuple(spans), parts, None, True)
        gathered = lax.all_gather(flat(arrived), "ctx", axis=0, tiled=True)
        cross_out = attend_cross([[(gathered, 0, n_ctx * n_pipe, each)]], None, True)
    return self_out[None], cross_out[None]


def solution(mesh):
    in_specs = (
        P("pipe", "ctx", "tp"),
        P("pipe", "ctx", None, "tp"),
        P("pipe", "ctx", "tp"),
        P(None, None, ("pipe", "ctx"), None, "tp"),
        P("pipe", None),
        P("pipe", None),
    )
    out_specs = (P("pipe", "ctx", "tp"), P("pipe", "ctx", "tp"))
    body = functools.partial(
        per_device, n_pipe=mesh.shape["pipe"], n_ctx=mesh.shape["ctx"]
    )
    return jax.shard_map(
        body, mesh=mesh, in_specs=in_specs, out_specs=out_specs, check_vma=False
    )
```

```python
import functools
import math

import jax
import jax.numpy as jnp
from jax import lax
from jax.experimental import pallas as pl
from jax.experimental.pallas import tpu as pltpu
from jax.sharding import PartitionSpec as P

HD = 128
TILE = 32
TOGETHER = 4
LOW = -1e30
EXP_SCALE = math.log2(math.e) / math.sqrt(HD)
NT = (((1,), (1,)), ((), ()))
NN = (((1,), (0,)), ((), ()))


def sample_bounds(lengths_ref, count):
    starts, ends, total = [], [], jnp.int32(0)
    for j in range(count):
        starts.append(total)
        total = total + lengths_ref[0, j]
        ends.append(total)
    return starts, ends


def stacked_queries(q_ref, tile, g, group):
    first = g * group
    rows = pl.ds(tile * TILE, TILE)
    return jnp.concatenate(
        [q_ref[rows, (first + h) * HD : (first + h + 1) * HD] for h in range(group)], axis=0
    )


def write_heads(out_ref, mixed, total, tile, g, group):
    rows = (mixed * (1.0 / total)).T.astype(out_ref.dtype)
    for h in range(group):
        at = (g * group + h) * HD
        out_ref[pl.ds(tile * TILE, TILE), at : at + HD] = rows[h * TILE : (h + 1) * TILE]


def scores_of(keys, q):
    return lax.dot_general(keys, q, NT, preferred_element_type=jnp.float32)


def absorb(state, s, v):
    if state is None:
        new_top = jnp.max(s, axis=0, keepdims=True)
    else:
        top, total, mixed = state
        new_top = jnp.maximum(top, jnp.max(s, axis=0, keepdims=True))
    w = jnp.exp2((s - new_top) * EXP_SCALE)
    added = jnp.sum(w, axis=0, keepdims=True)
    product = lax.dot_general(v, w.astype(jnp.bfloat16), NN, preferred_element_type=jnp.float32)
    if state is None:
        return new_top, added, product
    decay = jnp.exp2((top - new_top) * EXP_SCALE)
    return new_top, total * decay + added, mixed * decay + product


def staggered(units, score, finish):
    waiting = None
    for unit in units:
        s = score(*unit)
        if waiting is not None:
            finish(*waiting)
        waiting = (*unit, s)
    finish(*waiting)


def row_positions(first, height):
    return first + (lax.broadcasted_iota(jnp.int32, (1, height), 1) & (TILE - 1))


def lay(keys_at, flipped_at, ref, rows, kv_heads, g):
    keys_at[...] = ref[rows, g * HD : (g + 1) * HD]
    flipped_at[...] = ref[rows, (kv_heads + g) * HD : (kv_heads + g + 1) * HD].T


def self_kernel(
    lengths_ref, place_ref, q_ref, *refs, kv_heads, group, spans, parts, samples, begin, end
):
    refs = list(refs)
    take = lambda n: [refs.pop(0) for _ in range(n)]
    pieces = take(len({part[1] for part in parts}))
    stat_in, mixed_in = (None, None) if begin else take(2)
    out_ref = take(1)[0] if end else None
    stat_ref, mixed_ref, keys_ref, flipped_ref = take(4)
    rows_here = q_ref.shape[0]
    tiles = rows_here // TILE
    height = group * TILE
    base = place_ref[0] * rows_here
    _, ends = sample_bounds(lengths_ref, samples)
    ats = [sum(count for _, count in spans[:n]) for n in range(len(spans))]

    lows = []
    for tile in range(tiles):
        low = jnp.int32(0)
        for e in ends:
            low = jnp.where(e <= base + tile * TILE, e, low)
        lows.append(low)

    def limits(number):
        back, count = spans[number]
        past = base - (back - 1) * rows_here
        return past - count, past

    def reached(number):
        start, past = limits(number)
        many = jnp.int32(0)
        for low in lows:
            many = many + (low < past).astype(jnp.int32)
        return jnp.where(start >= 0, many, 0)

    counts = [reached(number) for number in range(len(spans))]
    for number, source, at, offset, count, only in parts:

        def fill(number=number, source=source, at=at, offset=offset, count=count):
            here = slice(ats[number] + offset, ats[number] + offset + count)
            for g in range(kv_heads):
                lay(
                    keys_ref.at[g, here], flipped_ref.at[g, :, here], pieces[source],
                    slice(at, at + count), kv_heads, g,
                )

        if spans[number][0] == 0:
            fill()
        else:
            asked = counts[number] > 0
            if only is not None:
                asked = asked & (place_ref[0] == only)
            pl.when(asked)(fill)

    def starts_of(first):
        row_t = row_positions(first, height)
        row_start = jnp.zeros((1, height), jnp.int32)
        for e in ends:
            row_start = jnp.where(e <= row_t, e, row_start)
        return row_start, row_t

    def keep(tile, g, state):
        stat_ref[tile, g, 0:1, :] = state[0]
        stat_ref[tile, g, 1:2, :] = state[1]
        mixed_ref[tile, g] = state[2]

    def own_count(tile):
        return min(rows_here, -(-(tile + 1) * TILE // HD) * HD)

    def own_scores(tile, g):
        q = stacked_queries(q_ref, tile, g, group)
        return scores_of(keys_ref[g, : own_count(tile)], q)

    def own_finish(tile, g, s):
        row_start, row_t = starts_of(base + tile * TILE)
        key_t = base + lax.broadcasted_iota(jnp.int32, (own_count(tile), 1), 0)
        s = jnp.where((key_t >= row_start) & (key_t <= row_t), s, LOW)
        keep(tile, g, absorb(None, s, flipped_ref[g, :, : own_count(tile)]))

    if begin:
        staggered(
            [(tile, g) for tile in range(tiles) for g in range(kv_heads)], own_scores, own_finish
        )
    else:
        stat_ref[...] = stat_in[...]
        mixed_ref[...] = mixed_in[...]

    together = math.gcd(tiles, TOGETHER)
    for number in range(1 if begin else 0, len(spans)):
        start, _ = limits(number)
        at, count = ats[number], spans[number][1]

        @pl.loop(0, (counts[number] + together - 1) // together)
        def _(turn, start=start, at=at, count=count):
            def scores(n, g):
                q = stacked_queries(q_ref, turn * together + n, g, group)
                return scores_of(keys_ref[g, at : at + count], q)

            def finish(n, g, s):
                tile = turn * together + n
                row_start, _ = starts_of(base + tile * TILE)
                key_t = start + lax.broadcasted_iota(jnp.int32, (count, 1), 0)
                s = jnp.where(key_t >= row_start, s, LOW)
                old = stat_ref[tile, g, 0:1, :], stat_ref[tile, g, 1:2, :], mixed_ref[tile, g]
                keep(tile, g, absorb(old, s, flipped_ref[g, :, at : at + count]))

            staggered(
                [(n, g) for n in range(together) for g in range(kv_heads)], scores, finish
            )

    for tile in range(tiles if end else 0):
        for g in range(kv_heads):
            write_heads(out_ref, mixed_ref[tile, g], stat_ref[tile, g, 1:2, :], tile, g, group)


def cross_kernel(
    lengths_ref, images_ref, place_ref, q_ref, *refs, kv_heads, group, sources, samples, begin, end
):
    refs = list(refs)
    take = lambda n: [refs.pop(0) for _ in range(n)]
    pieces = [take(len(source)) for source in sources]
    stat_in, mixed_in = (None, None) if begin else take(2)
    out_ref = take(1)[0] if end else None
    stat_ref, mixed_ref, keys_ref, flipped_ref = take(4)
    rows_ref, copied = take(2) if end else (None, None)
    rows_here = q_ref.shape[0]
    tiles = rows_here // TILE
    height = group * TILE
    base = place_ref[0] * rows_here
    starts, _ = sample_bounds(lengths_ref, samples)
    image_count = keys_ref.shape[0]

    def fill(ref, at, parts, each, only):
        for n in range(kv_heads):
            if only not in (None, n):
                continue
            k_at = n * HD if only is None else 0
            v_at = k_at + ref.shape[1] // 2
            for image in range(image_count):
                values = []
                for part in range(parts):
                    first = (part * image_count + image) * each
                    here = slice(at + part * each, at + (part + 1) * each)
                    keys_ref[image, n, here] = ref[first : first + each, k_at : k_at + HD]
                    values.append(ref[first : first + each, v_at : v_at + HD])
                whole = jnp.concatenate(values, axis=0)
                flipped_ref[image, n, :, at : at + parts * each] = whole.T

    at = 0
    for source, given in zip(sources, pieces):
        for number, ((parts, each, only), ref) in enumerate(zip(source, given)):
            put = functools.partial(fill, ref, at, parts, each, only)
            if len(source) == 1:
                put()
            else:
                pl.when(place_ref[1] == 1 - number)(put)
        if source[0][2] in (None, kv_heads - 1):
            at += source[0][0] * source[0][1]

    def images_of(tile):
        first = base + tile * TILE
        row_t = row_positions(first, height)
        row_image = jnp.zeros((1, height), jnp.int32)
        leading = jnp.int32(0)
        for j in range(samples):
            row_image = jnp.where(row_t >= starts[j], images_ref[0, j], row_image)
            leading = jnp.where(first >= starts[j], images_ref[0, j], leading)
        return row_image, leading

    def keep(tile, g, state):
        stat_ref[tile, g, 0:1, :] = state[0]
        stat_ref[tile, g, 1:2, :] = state[1]
        mixed_ref[tile, g] = state[2]

    def chosen(mine, new, old):
        if old is None:
            old = LOW, 0.0, 0.0
        return [jnp.where(mine, n, o) for n, o in zip(new, old)]

    marks = [images_of(tile) for tile in range(tiles)]
    order = range(kv_heads)

    def scores(tile, n):
        return scores_of(
            keys_ref[marks[tile][1], n], stacked_queries(q_ref, tile, n, group)
        )

    def finish(tile, n, s):
        row_image, leading = marks[tile]
        old = None
        if not begin:
            old = stat_in[tile, n, 0:1, :], stat_in[tile, n, 1:2, :], mixed_in[tile, n]
        new = absorb(old, s, flipped_ref[leading, n])
        keep(tile, n, chosen(row_image == leading, new, old))

    staggered([(tile, n) for tile in range(tiles) for n in order], scores, finish)

    @pl.loop(0, tiles)
    def _(tile):
        first = base + tile * TILE
        leading, others = jnp.int32(0), [jnp.bool_(False)] * image_count
        for j in range(samples):
            leading = jnp.where(first >= starts[j], images_ref[0, j], leading)
        for j in range(samples):
            inside = (starts[j] > first) & (starts[j] < first + TILE)
            for image in range(image_count):
                others[image] = others[image] | (inside & (images_ref[0, j] == image))
        for image in range(image_count):

            @pl.when(others[image] & (leading != image))
            def _(image=image):
                row_image, _ = images_of(tile)
                olds = [
                    (stat_ref[tile, n, 0:1, :], stat_ref[tile, n, 1:2, :], mixed_ref[tile, n])
                    for n in order
                ]
                ss = [
                    scores_of(keys_ref[image, n], stacked_queries(q_ref, tile, n, group))
                    for n in order
                ]
                for n in order:
                    new = absorb(olds[n], ss[n], flipped_ref[image, n])
                    keep(tile, n, chosen(row_image == image, new, olds[n]))

    if not end:
        return
    pace = 2
    copies = []
    for tile in range(tiles):
        for n in order:
            write_heads(rows_ref, mixed_ref[tile, n], stat_ref[tile, n, 1:2, :], tile, n, group)
        if (tile + 1) % pace == 0 or tile + 1 == tiles:
            done = slice(len(copies) * pace * TILE, (tile + 1) * TILE)
            copy = pltpu.make_async_copy(
                rows_ref.at[done], out_ref.at[done], copied.at[len(copies)]
            )
            copy.start()
            copies.append(copy)
    for copy in copies:
        copy.wait()


def smem():
    return pl.BlockSpec(memory_space=pltpu.SMEM)


def vmem():
    return pl.BlockSpec(memory_space=pltpu.VMEM)


def cost(rows, width, keys):
    return pl.CostEstimate(
        flops=8 * rows * width * keys, bytes_accessed=4 * rows * width,
        transcendentals=rows * (width // HD) * keys,
    )


def state_shapes(rows, kv_heads, group):
    tiles, height = rows // TILE, group * TILE
    return (tiles, kv_heads, 8, height), (tiles, kv_heads, HD, height)


def state_call(
    kernel, operands, rows, width, keys, shapes, scratch, end, dtype, placed=False
):
    scalars = sum(x.dtype == jnp.int32 for x in operands)
    state_scratch = []
    if end:
        out_shape = jax.ShapeDtypeStruct((rows, width), dtype)
        state_scratch = [pltpu.VMEM(s, jnp.float32) for s in shapes]
    else:
        out_shape = [jax.ShapeDtypeStruct(s, jnp.float32) for s in shapes]
    anywhere = pl.BlockSpec(memory_space=pl.ANY)
    in_specs = [smem()] * scalars + [vmem()] * (len(operands) - scalars)
    return pl.pallas_call(
        kernel,
        out_shape=out_shape,
        in_specs=in_specs,
        out_specs=(anywhere if placed else vmem()) if end else [vmem(), vmem()],
        scratch_shapes=state_scratch + scratch,
        compiler_params=pltpu.CompilerParams(vmem_limit_bytes=28 << 20),
        cost_estimate=cost(rows, width, keys),
    )(*operands)


def self_attention(lengths, place, q, pieces, spans, parts, state, end, kv_heads, group):
    rows, width = q.shape
    keys = sum(count for _, count in spans)
    begin = state is None
    kernel = functools.partial(
        self_kernel, kv_heads=kv_heads, group=group, spans=spans, parts=parts,
        samples=lengths.shape[1], begin=begin, end=end,
    )
    scratch = [
        pltpu.VMEM((kv_heads, keys, HD), q.dtype), pltpu.VMEM((kv_heads, HD, keys), q.dtype)
    ]
    operands = (lengths, place, q, *pieces, *(() if begin else state))
    shapes = state_shapes(rows, kv_heads, group)
    return state_call(kernel, operands, rows, width, keys, shapes, scratch, end, q.dtype)


def cross_attention(lengths, images, place, q, sources, state, end, kv_heads, group, image_count):
    rows, width = q.shape
    begin = state is None
    kernel = functools.partial(
        cross_kernel, kv_heads=kv_heads, group=group,
        sources=tuple(tuple(piece[1:] for piece in source) for source in sources),
        samples=lengths.shape[1], begin=begin, end=end,
    )
    pieces = [piece[0] for source in sources for piece in source]
    keys = sum(s[0][1] * s[0][2] for s in sources if s[0][3] in (None, 0))
    scratch = [
        pltpu.VMEM((image_count, kv_heads, keys, HD), q.dtype),
        pltpu.VMEM((image_count, kv_heads, HD, keys), q.dtype),
    ]
    if end:
        scratch += [pltpu.VMEM((rows, width), q.dtype), pltpu.SemaphoreType.DMA((rows // TILE,))]
    operands = (lengths, images, place, q, *pieces, *(() if begin else state))
    shapes = state_shapes(rows, kv_heads, group)
    return state_call(kernel, operands, rows, width, keys, shapes, scratch, end, q.dtype, True)


def per_device(q_self, kv_self, q_cross, kv_cross, sample_lengths, sample_image, *, n_pipe, n_ctx):
    rows = q_self.shape[1]
    kv_heads = kv_self.shape[3] // HD
    group = q_self.shape[2] // HD // kv_heads
    image_count, each = kv_cross.shape[1:3]
    z = lax.axis_index("ctx")
    inner = ((z == 1) | (z == 2)).astype(jnp.int32)
    place = jnp.stack([z, inner]).astype(jnp.int32)

    shift = lambda piece, step: lax.ppermute(
        piece, "ctx", [(c, c + 1) for c in range(step - 1, n_ctx - 1)]
    )
    passed = shift(kv_self[0], 1)
    arrived = lax.all_to_all(kv_cross, "pipe", split_axis=0, concat_axis=0, tiled=True)
    arrived, passed = lax.optimization_barrier((arrived, passed))
    flat = lambda array: array.reshape(-1, array.shape[-2] * array.shape[-1])
    own = flat(kv_self)
    longest = rows * n_ctx * 5 // 8

    attend_self = functools.partial(
        self_attention, sample_lengths, place, q_self[0], kv_heads=kv_heads, group=group
    )
    attend_cross = functools.partial(
        cross_attention, sample_lengths, sample_image, place, q_cross[0],
        kv_heads=kv_heads, group=group, image_count=image_count,
    )
    if n_ctx == 4:
        half = rows // 2
        at = lambda array, head=None: (array, n_pipe, each, head)
        near = lax.ppermute(arrived, "ctx", [(1, 2), (2, 1)])
        pair = lax.ppermute(arrived, "ctx", [(0, 1), (1, 0), (2, 3), (3, 2)])
        state = attend_cross([[at(flat(arrived))]], None, False)
        passed, state = lax.optimization_barrier((passed, state))
        two_back = lax.ppermute(passed, "ctx", [(1, 2), (2, 3)])
        three_back = lax.ppermute(passed[half:], "ctx", [(1, 3)])
        early = ((0, rows), (1, rows))
        parts = ((0, 0, 0, 0, rows, None), (1, 1, 0, 0, rows, None))
        self_state = attend_self([own, flat(passed)], early, parts, None, False)
        near, state = lax.optimization_barrier((near, state))
        pair, two_back, three_back, self_state = lax.optimization_barrier(
            (pair, two_back, three_back, self_state)
        )

        near = flat(near)
        near_on = lax.ppermute(near, "ctx", [(1, 0), (2, 3)])
        far = [
            lax.ppermute(flat(pair[..., g * HD : (g + 1) * HD]), "ctx", [(1, 2), (2, 1)])
            for g in range(kv_heads)
        ]
        state = attend_cross([[at(flat(pair))]], state, False)
        far[0], state = lax.optimization_barrier((far[0], state))
        late = ((2, rows), (3, half))
        parts = ((0, 0, 0, 0, rows, None), (1, 1, 0, 0, half, 3))
        self_out = attend_self([flat(two_back), flat(three_back)], late, parts, self_state, True)
        far_on = [lax.ppermute(part, "ctx", [(1, 0), (2, 3)]) for part in far]
        state = attend_cross([[at(near), at(near_on)]], state, False)
        last = [[at(far[g], g), at(far_on[g], g)] for g in range(kv_heads)]
        cross_out = attend_cross(last, state, True)
    else:
        pieces, spans = [own, flat(passed)], [(0, rows), (1, rows)]
        left, step = longest - 1 - rows, 1
        while left > 0 and step < n_ctx - 1:
            step += 1
            count = min(rows, -(-left // HD) * HD)
            pieces.append(shift(pieces[-1][rows - count :], step))
            spans.append((step, count))
            left -= rows
        parts = tuple((n, n, 0, 0, count, None) for n, (_, count) in enumerate(spans))
        self_out = attend_self(pieces, tuple(spans), parts, None, True)
        gathered = lax.all_gather(flat(arrived), "ctx", axis=0, tiled=True)
        cross_out = attend_cross([[(gathered, n_ctx * n_pipe, each, None)]], None, True)
    return self_out[None], cross_out[None]


def solution(mesh):
    in_specs = (
        P("pipe", "ctx", "tp"),
        P("pipe", "ctx", None, "tp"),
        P("pipe", "ctx", "tp"),
        P(None, None, ("pipe", "ctx"), None, "tp"),
        P("pipe", None),
        P("pipe", None),
    )
    out_specs = (P("pipe", "ctx", "tp"), P("pipe", "ctx", "tp"))
    body = functools.partial(
        per_device, n_pipe=mesh.shape["pipe"], n_ctx=mesh.shape["ctx"]
    )
    return jax.shard_map(
        body, mesh=mesh, in_specs=in_specs, out_specs=out_specs, check_vma=False
    )
```

```python
import functools
import math

import jax
import jax.numpy as jnp
from jax import lax
from jax.experimental import pallas as pl
from jax.experimental.pallas import tpu as pltpu
from jax.sharding import PartitionSpec as P

HD = 128
TILE = 32
TOGETHER = 4
LOW = -1e30
EXP_SCALE = math.log2(math.e) / math.sqrt(HD)
NT = (((1,), (1,)), ((), ()))
NN = (((1,), (0,)), ((), ()))


def sample_bounds(lengths_ref, count):
    starts, ends, total = [], [], jnp.int32(0)
    for j in range(count):
        starts.append(total)
        total = total + lengths_ref[0, j]
        ends.append(total)
    return starts, ends


def stacked_queries(q_ref, tile, g, group):
    first = g * group
    rows = pl.ds(tile * TILE, TILE)
    return jnp.concatenate(
        [q_ref[rows, (first + h) * HD : (first + h + 1) * HD] for h in range(group)], axis=0
    )


def write_heads(out_ref, mixed, total, tile, g, group):
    rows = (mixed * (1.0 / total)).T.astype(out_ref.dtype)
    for h in range(group):
        at = (g * group + h) * HD
        out_ref[pl.ds(tile * TILE, TILE), at : at + HD] = rows[h * TILE : (h + 1) * TILE]


def scores_of(keys, q):
    return lax.dot_general(keys, q, NT, preferred_element_type=jnp.float32)


def absorb(state, s, v):
    if state is None:
        new_top = jnp.max(s, axis=0, keepdims=True)
    else:
        top, total, mixed = state
        new_top = jnp.maximum(top, jnp.max(s, axis=0, keepdims=True))
    w = jnp.exp2((s - new_top) * EXP_SCALE)
    added = jnp.sum(w, axis=0, keepdims=True)
    product = lax.dot_general(v, w.astype(jnp.bfloat16), NN, preferred_element_type=jnp.float32)
    if state is None:
        return new_top, added, product
    decay = jnp.exp2((top - new_top) * EXP_SCALE)
    return new_top, total * decay + added, mixed * decay + product


def staggered(units, score, finish):
    waiting = None
    for unit in units:
        s = score(*unit)
        if waiting is not None:
            finish(*waiting)
        waiting = (*unit, s)
    finish(*waiting)


def row_positions(first, height):
    return first + (lax.broadcasted_iota(jnp.int32, (1, height), 1) & (TILE - 1))


def lay(keys_at, flipped_at, ref, rows, kv_heads, g):
    keys_at[...] = ref[rows, g * HD : (g + 1) * HD]
    flipped_at[...] = ref[rows, (kv_heads + g) * HD : (kv_heads + g + 1) * HD].T


def self_kernel(
    lengths_ref, place_ref, q_ref, *refs, kv_heads, group, spans, parts, samples, begin, end
):
    refs = list(refs)
    take = lambda n: [refs.pop(0) for _ in range(n)]
    pieces = take(len({part[1] for part in parts}))
    stat_in, mixed_in = (None, None) if begin else take(2)
    out_ref = take(1)[0] if end else None
    stat_ref, mixed_ref, keys_ref, flipped_ref = take(4)
    rows_here = q_ref.shape[0]
    tiles = rows_here // TILE
    height = group * TILE
    base = place_ref[0] * rows_here
    _, ends = sample_bounds(lengths_ref, samples)
    ats = [sum(count for _, count in spans[:n]) for n in range(len(spans))]

    lows = []
    for tile in range(tiles):
        low = jnp.int32(0)
        for e in ends:
            low = jnp.where(e <= base + tile * TILE, e, low)
        lows.append(low)

    def limits(number):
        back, count = spans[number]
        past = base - (back - 1) * rows_here
        return past - count, past

    def reached(number):
        start, past = limits(number)
        many = jnp.int32(0)
        for low in lows:
            many = many + (low < past).astype(jnp.int32)
        return jnp.where(start >= 0, many, 0)

    counts = [reached(number) for number in range(len(spans))]
    for number, source, at, offset, count, only in parts:

        def fill(number=number, source=source, at=at, offset=offset, count=count):
            here = slice(ats[number] + offset, ats[number] + offset + count)
            for g in range(kv_heads):
                lay(
                    keys_ref.at[g, here], flipped_ref.at[g, :, here], pieces[source],
                    slice(at, at + count), kv_heads, g,
                )

        if spans[number][0] == 0:
            fill()
        else:
            asked = counts[number] > 0
            if only is not None:
                asked = asked & (place_ref[0] == only)
            pl.when(asked)(fill)

    def starts_of(first):
        row_t = row_positions(first, height)
        row_start = jnp.zeros((1, height), jnp.int32)
        for e in ends:
            row_start = jnp.where(e <= row_t, e, row_start)
        return row_start, row_t

    def keep(tile, g, state):
        stat_ref[tile, g, 0:1, :] = state[0]
        stat_ref[tile, g, 1:2, :] = state[1]
        mixed_ref[tile, g] = state[2]

    def own_count(tile):
        return min(rows_here, -(-(tile + 1) * TILE // HD) * HD)

    def own_scores(tile, g):
        q = stacked_queries(q_ref, tile, g, group)
        return scores_of(keys_ref[g, : own_count(tile)], q)

    def own_finish(tile, g, s):
        row_start, row_t = starts_of(base + tile * TILE)
        key_t = base + lax.broadcasted_iota(jnp.int32, (own_count(tile), 1), 0)
        s = jnp.where((key_t >= row_start) & (key_t <= row_t), s, LOW)
        keep(tile, g, absorb(None, s, flipped_ref[g, :, : own_count(tile)]))

    if begin:
        staggered(
            [(tile, g) for tile in range(tiles) for g in range(kv_heads)], own_scores, own_finish
        )
    else:
        stat_ref[...] = stat_in[...]
        mixed_ref[...] = mixed_in[...]

    together = math.gcd(tiles, TOGETHER)
    for number in range(1 if begin else 0, len(spans)):
        start, _ = limits(number)
        at, count = ats[number], spans[number][1]

        @pl.loop(0, (counts[number] + together - 1) // together)
        def _(turn, start=start, at=at, count=count):
            def scores(n, g):
                q = stacked_queries(q_ref, turn * together + n, g, group)
                return scores_of(keys_ref[g, at : at + count], q)

            def finish(n, g, s):
                tile = turn * together + n
                row_start, _ = starts_of(base + tile * TILE)
                key_t = start + lax.broadcasted_iota(jnp.int32, (count, 1), 0)
                s = jnp.where(key_t >= row_start, s, LOW)
                old = stat_ref[tile, g, 0:1, :], stat_ref[tile, g, 1:2, :], mixed_ref[tile, g]
                keep(tile, g, absorb(old, s, flipped_ref[g, :, at : at + count]))

            staggered(
                [(n, g) for n in range(together) for g in range(kv_heads)], scores, finish
            )

    for tile in range(tiles if end else 0):
        for g in range(kv_heads):
            write_heads(out_ref, mixed_ref[tile, g], stat_ref[tile, g, 1:2, :], tile, g, group)


def cross_kernel(
    lengths_ref, images_ref, place_ref, q_ref, *refs, kv_heads, group, sources, samples, begin, end
):
    refs = list(refs)
    take = lambda n: [refs.pop(0) for _ in range(n)]
    pieces = [take(len(source)) for source in sources]
    stat_in, mixed_in = (None, None) if begin else take(2)
    out_ref = take(1)[0] if end else None
    stat_ref, mixed_ref, keys_ref, flipped_ref = take(4)
    rows_ref, copied = take(2) if end else (None, None)
    rows_here = q_ref.shape[0]
    tiles = rows_here // TILE
    height = group * TILE
    base = place_ref[0] * rows_here
    starts, _ = sample_bounds(lengths_ref, samples)
    image_count = keys_ref.shape[0]

    def fill(ref, at, parts, each, only):
        for n in range(kv_heads):
            if only not in (None, n):
                continue
            k_at = n * HD if only is None else 0
            v_at = k_at + ref.shape[1] // 2
            for image in range(image_count):
                values = []
                for part in range(parts):
                    first = (part * image_count + image) * each
                    here = slice(at + part * each, at + (part + 1) * each)
                    keys_ref[image, n, here] = ref[first : first + each, k_at : k_at + HD]
                    values.append(ref[first : first + each, v_at : v_at + HD])
                whole = jnp.concatenate(values, axis=0)
                flipped_ref[image, n, :, at : at + parts * each] = whole.T

    at = 0
    for source, given in zip(sources, pieces):
        for number, ((parts, each, only), ref) in enumerate(zip(source, given)):
            put = functools.partial(fill, ref, at, parts, each, only)
            if len(source) == 1:
                put()
            else:
                pl.when(place_ref[1] == 1 - number)(put)
        if source[0][2] in (None, kv_heads - 1):
            at += source[0][0] * source[0][1]

    def images_of(tile):
        first = base + tile * TILE
        row_t = row_positions(first, height)
        row_image = jnp.zeros((1, height), jnp.int32)
        leading = jnp.int32(0)
        for j in range(samples):
            row_image = jnp.where(row_t >= starts[j], images_ref[0, j], row_image)
            leading = jnp.where(first >= starts[j], images_ref[0, j], leading)
        return row_image, leading

    def keep(tile, g, state):
        stat_ref[tile, g, 0:1, :] = state[0]
        stat_ref[tile, g, 1:2, :] = state[1]
        mixed_ref[tile, g] = state[2]

    def chosen(mine, new, old):
        if old is None:
            old = LOW, 0.0, 0.0
        return [jnp.where(mine, n, o) for n, o in zip(new, old)]

    marks = [images_of(tile) for tile in range(tiles)]
    order = range(kv_heads)

    def scores(tile, n):
        return scores_of(
            keys_ref[marks[tile][1], n], stacked_queries(q_ref, tile, n, group)
        )

    def finish(tile, n, s):
        row_image, leading = marks[tile]
        old = None
        if not begin:
            old = stat_in[tile, n, 0:1, :], stat_in[tile, n, 1:2, :], mixed_in[tile, n]
        new = absorb(old, s, flipped_ref[leading, n])
        keep(tile, n, chosen(row_image == leading, new, old))

    staggered([(tile, n) for tile in range(tiles) for n in order], scores, finish)

    @pl.loop(0, tiles)
    def _(tile):
        first = base + tile * TILE
        leading, others = jnp.int32(0), [jnp.bool_(False)] * image_count
        for j in range(samples):
            leading = jnp.where(first >= starts[j], images_ref[0, j], leading)
        for j in range(samples):
            inside = (starts[j] > first) & (starts[j] < first + TILE)
            for image in range(image_count):
                others[image] = others[image] | (inside & (images_ref[0, j] == image))
        for image in range(image_count):

            @pl.when(others[image] & (leading != image))
            def _(image=image):
                row_image, _ = images_of(tile)
                olds = [
                    (stat_ref[tile, n, 0:1, :], stat_ref[tile, n, 1:2, :], mixed_ref[tile, n])
                    for n in order
                ]
                ss = [
                    scores_of(keys_ref[image, n], stacked_queries(q_ref, tile, n, group))
                    for n in order
                ]
                for n in order:
                    new = absorb(olds[n], ss[n], flipped_ref[image, n])
                    keep(tile, n, chosen(row_image == image, new, olds[n]))

    if not end:
        return
    pace = 2
    copies = []
    for tile in range(tiles):
        for n in order:
            write_heads(rows_ref, mixed_ref[tile, n], stat_ref[tile, n, 1:2, :], tile, n, group)
        if (tile + 1) % pace == 0 or tile + 1 == tiles:
            done = slice(len(copies) * pace * TILE, (tile + 1) * TILE)
            copy = pltpu.make_async_copy(
                rows_ref.at[done], out_ref.at[done], copied.at[len(copies)]
            )
            copy.start()
            copies.append(copy)
    for copy in copies:
        copy.wait()


def smem():
    return pl.BlockSpec(memory_space=pltpu.SMEM)


def vmem():
    return pl.BlockSpec(memory_space=pltpu.VMEM)


def cost(rows, width, keys):
    return pl.CostEstimate(
        flops=8 * rows * width * keys, bytes_accessed=4 * rows * width,
        transcendentals=rows * (width // HD) * keys,
    )


def state_shapes(rows, kv_heads, group):
    tiles, height = rows // TILE, group * TILE
    return (tiles, kv_heads, 8, height), (tiles, kv_heads, HD, height)


def state_call(
    kernel, operands, rows, width, keys, shapes, scratch, end, dtype, placed=False
):
    scalars = sum(x.dtype == jnp.int32 for x in operands)
    state_scratch = []
    if end:
        out_shape = jax.ShapeDtypeStruct((rows, width), dtype)
        state_scratch = [pltpu.VMEM(s, jnp.float32) for s in shapes]
    else:
        out_shape = [jax.ShapeDtypeStruct(s, jnp.float32) for s in shapes]
    anywhere = pl.BlockSpec(memory_space=pl.ANY)
    in_specs = [smem()] * scalars + [vmem()] * (len(operands) - scalars)
    return pl.pallas_call(
        kernel,
        out_shape=out_shape,
        in_specs=in_specs,
        out_specs=(anywhere if placed else vmem()) if end else [vmem(), vmem()],
        scratch_shapes=state_scratch + scratch,
        compiler_params=pltpu.CompilerParams(vmem_limit_bytes=28 << 20),
        cost_estimate=cost(rows, width, keys),
    )(*operands)


def self_attention(lengths, place, q, pieces, spans, parts, state, end, kv_heads, group):
    rows, width = q.shape
    keys = sum(count for _, count in spans)
    begin = state is None
    kernel = functools.partial(
        self_kernel, kv_heads=kv_heads, group=group, spans=spans, parts=parts,
        samples=lengths.shape[1], begin=begin, end=end,
    )
    scratch = [
        pltpu.VMEM((kv_heads, keys, HD), q.dtype), pltpu.VMEM((kv_heads, HD, keys), q.dtype)
    ]
    operands = (lengths, place, q, *pieces, *(() if begin else state))
    shapes = state_shapes(rows, kv_heads, group)
    return state_call(kernel, operands, rows, width, keys, shapes, scratch, end, q.dtype)


def cross_attention(lengths, images, place, q, sources, state, end, kv_heads, group, image_count):
    rows, width = q.shape
    begin = state is None
    kernel = functools.partial(
        cross_kernel, kv_heads=kv_heads, group=group,
        sources=tuple(tuple(piece[1:] for piece in source) for source in sources),
        samples=lengths.shape[1], begin=begin, end=end,
    )
    pieces = [piece[0] for source in sources for piece in source]
    keys = sum(s[0][1] * s[0][2] for s in sources if s[0][3] in (None, 0))
    scratch = [
        pltpu.VMEM((image_count, kv_heads, keys, HD), q.dtype),
        pltpu.VMEM((image_count, kv_heads, HD, keys), q.dtype),
    ]
    if end:
        scratch += [pltpu.VMEM((rows, width), q.dtype), pltpu.SemaphoreType.DMA((rows // TILE,))]
    operands = (lengths, images, place, q, *pieces, *(() if begin else state))
    shapes = state_shapes(rows, kv_heads, group)
    return state_call(kernel, operands, rows, width, keys, shapes, scratch, end, q.dtype, True)


def per_device(q_self, kv_self, q_cross, kv_cross, sample_lengths, sample_image, *, n_pipe, n_ctx):
    rows = q_self.shape[1]
    kv_heads = kv_self.shape[3] // HD
    group = q_self.shape[2] // HD // kv_heads
    image_count, each = kv_cross.shape[1:3]
    z = lax.axis_index("ctx")
    inner = ((z == 1) | (z == 2)).astype(jnp.int32)
    place = jnp.stack([z, inner]).astype(jnp.int32)

    shift = lambda piece, step: lax.ppermute(
        piece, "ctx", [(c, c + 1) for c in range(step - 1, n_ctx - 1)]
    )
    passed = shift(kv_self[0], 1)
    arrived = lax.all_to_all(kv_cross, "pipe", split_axis=0, concat_axis=0, tiled=True)
    arrived, passed = lax.optimization_barrier((arrived, passed))
    flat = lambda array: array.reshape(-1, array.shape[-2] * array.shape[-1])
    own = flat(kv_self)
    longest = rows * n_ctx * 5 // 8

    attend_self = functools.partial(
        self_attention, sample_lengths, place, q_self[0], kv_heads=kv_heads, group=group
    )
    attend_cross = functools.partial(
        cross_attention, sample_lengths, sample_image, place, q_cross[0],
        kv_heads=kv_heads, group=group, image_count=image_count,
    )
    if n_ctx == 4:
        half = rows // 2
        at = lambda array, head=None: (array, n_pipe, each, head)
        near = lax.ppermute(arrived, "ctx", [(1, 2), (2, 1)])
        pair = lax.ppermute(arrived, "ctx", [(0, 1), (1, 0), (2, 3), (3, 2)])
        state = attend_cross([[at(flat(arrived))]], None, False)
        passed, state = lax.optimization_barrier((passed, state))
        two_back = lax.ppermute(passed, "ctx", [(1, 2), (2, 3)])
        three_back = lax.ppermute(passed[half:], "ctx", [(1, 3)])
        early = ((0, rows), (1, rows))
        parts = ((0, 0, 0, 0, rows, None), (1, 1, 0, 0, rows, None))
        self_state = attend_self([own, flat(passed)], early, parts, None, False)
        near, state = lax.optimization_barrier((near, state))
        state = attend_cross([[at(flat(pair))]], state, False)
        pair, two_back, three_back, self_state, state = lax.optimization_barrier(
            (pair, two_back, three_back, self_state, state)
        )

        near = flat(near)
        near_on = lax.ppermute(near, "ctx", [(1, 0), (2, 3)])
        far = [
            lax.ppermute(flat(pair[..., g * HD : (g + 1) * HD]), "ctx", [(1, 2), (2, 1)])
            for g in range(kv_heads)
        ]
        late = ((2, rows), (3, half))
        parts = ((0, 0, 0, 0, rows, None), (1, 1, 0, 0, half, 3))
        self_out = attend_self([flat(two_back), flat(three_back)], late, parts, self_state, True)
        far[-1], self_out = lax.optimization_barrier((far[-1], self_out))
        far_on = [lax.ppermute(part, "ctx", [(1, 0), (2, 3)]) for part in far]
        state = attend_cross([[at(near), at(near_on)]], state, False)
        last = [[at(far[g], g), at(far_on[g], g)] for g in range(kv_heads)]
        cross_out = attend_cross(last, state, True)
    else:
        pieces, spans = [own, flat(passed)], [(0, rows), (1, rows)]
        left, step = longest - 1 - rows, 1
        while left > 0 and step < n_ctx - 1:
            step += 1
            count = min(rows, -(-left // HD) * HD)
            pieces.append(shift(pieces[-1][rows - count :], step))
            spans.append((step, count))
            left -= rows
        parts = tuple((n, n, 0, 0, count, None) for n, (_, count) in enumerate(spans))
        self_out = attend_self(pieces, tuple(spans), parts, None, True)
        gathered = lax.all_gather(flat(arrived), "ctx", axis=0, tiled=True)
        cross_out = attend_cross([[(gathered, n_ctx * n_pipe, each, None)]], None, True)
    return self_out[None], cross_out[None]


def solution(mesh):
    in_specs = (
        P("pipe", "ctx", "tp"),
        P("pipe", "ctx", None, "tp"),
        P("pipe", "ctx", "tp"),
        P(None, None, ("pipe", "ctx"), None, "tp"),
        P("pipe", None),
        P("pipe", None),
    )
    out_specs = (P("pipe", "ctx", "tp"), P("pipe", "ctx", "tp"))
    body = functools.partial(
        per_device, n_pipe=mesh.shape["pipe"], n_ctx=mesh.shape["ctx"]
    )
    return jax.shard_map(
        body, mesh=mesh, in_specs=in_specs, out_specs=out_specs, check_vma=False
    )
```

```python
import functools
import math

import jax
import jax.numpy as jnp
from jax import lax
from jax.experimental import pallas as pl
from jax.experimental.pallas import tpu as pltpu
from jax.sharding import PartitionSpec as P

HD = 128
TILE = 32
TOGETHER = 4
LOW = -1e30
EXP_SCALE = math.log2(math.e) / math.sqrt(HD)
NT = (((1,), (1,)), ((), ()))
NN = (((1,), (0,)), ((), ()))


def sample_bounds(lengths_ref, count):
    starts, ends, total = [], [], jnp.int32(0)
    for j in range(count):
        starts.append(total)
        total = total + lengths_ref[0, j]
        ends.append(total)
    return starts, ends


def stacked_queries(q_ref, tile, g, group):
    first = g * group
    rows = pl.ds(tile * TILE, TILE)
    return jnp.concatenate(
        [q_ref[rows, (first + h) * HD : (first + h + 1) * HD] for h in range(group)], axis=0
    )


def write_heads(out_ref, mixed, total, tile, g, group):
    rows = (mixed * (1.0 / total)).T.astype(out_ref.dtype)
    for h in range(group):
        at = (g * group + h) * HD
        out_ref[pl.ds(tile * TILE, TILE), at : at + HD] = rows[h * TILE : (h + 1) * TILE]


def scores_of(keys, q):
    return lax.dot_general(keys, q, NT, preferred_element_type=jnp.float32)


def absorb(state, s, v):
    if state is None:
        new_top = jnp.max(s, axis=0, keepdims=True)
    else:
        top, total, mixed = state
        new_top = jnp.maximum(top, jnp.max(s, axis=0, keepdims=True))
    w = jnp.exp2((s - new_top) * EXP_SCALE)
    added = jnp.sum(w, axis=0, keepdims=True)
    product = lax.dot_general(v, w.astype(jnp.bfloat16), NN, preferred_element_type=jnp.float32)
    if state is None:
        return new_top, added, product
    decay = jnp.exp2((top - new_top) * EXP_SCALE)
    return new_top, total * decay + added, mixed * decay + product


def staggered(units, score, finish):
    waiting = None
    for unit in units:
        s = score(*unit)
        if waiting is not None:
            finish(*waiting)
        waiting = (*unit, s)
    finish(*waiting)


def row_positions(first, height):
    return first + (lax.broadcasted_iota(jnp.int32, (1, height), 1) & (TILE - 1))


def lay(keys_at, flipped_at, ref, rows, kv_heads, g):
    keys_at[...] = ref[rows, g * HD : (g + 1) * HD]
    flipped_at[...] = ref[rows, (kv_heads + g) * HD : (kv_heads + g + 1) * HD].T


def self_kernel(
    lengths_ref, place_ref, q_ref, *refs, kv_heads, group, spans, parts, samples, begin, end
):
    refs = list(refs)
    take = lambda n: [refs.pop(0) for _ in range(n)]
    pieces = take(len({part[1] for part in parts}))
    stat_in, mixed_in = (None, None) if begin else take(2)
    out_ref = take(1)[0] if end else None
    stat_ref, mixed_ref, keys_ref, flipped_ref = take(4)
    rows_here = q_ref.shape[0]
    tiles = rows_here // TILE
    height = group * TILE
    base = place_ref[0] * rows_here
    _, ends = sample_bounds(lengths_ref, samples)
    ats = [sum(count for _, count in spans[:n]) for n in range(len(spans))]

    lows = []
    for tile in range(tiles):
        low = jnp.int32(0)
        for e in ends:
            low = jnp.where(e <= base + tile * TILE, e, low)
        lows.append(low)

    def limits(number):
        back, count = spans[number]
        past = base - (back - 1) * rows_here
        return past - count, past

    def reached(number):
        start, past = limits(number)
        many = jnp.int32(0)
        for low in lows:
            many = many + (low < past).astype(jnp.int32)
        return jnp.where(start >= 0, many, 0)

    counts = [reached(number) for number in range(len(spans))]
    for number, source, at, offset, count, only in parts:

        def fill(number=number, source=source, at=at, offset=offset, count=count):
            here = slice(ats[number] + offset, ats[number] + offset + count)
            for g in range(kv_heads):
                lay(
                    keys_ref.at[g, here], flipped_ref.at[g, :, here], pieces[source],
                    slice(at, at + count), kv_heads, g,
                )

        if spans[number][0] == 0:
            fill()
        else:
            asked = counts[number] > 0
            if only is not None:
                asked = asked & (place_ref[0] == only)
            pl.when(asked)(fill)

    def starts_of(first):
        row_t = row_positions(first, height)
        row_start = jnp.zeros((1, height), jnp.int32)
        for e in ends:
            row_start = jnp.where(e <= row_t, e, row_start)
        return row_start, row_t

    def keep(tile, g, state):
        stat_ref[tile, g, 0:1, :] = state[0]
        stat_ref[tile, g, 1:2, :] = state[1]
        mixed_ref[tile, g] = state[2]

    def own_count(tile):
        return min(rows_here, -(-(tile + 1) * TILE // HD) * HD)

    def own_scores(tile, g):
        q = stacked_queries(q_ref, tile, g, group)
        return scores_of(keys_ref[g, : own_count(tile)], q)

    def own_finish(tile, g, s):
        row_start, row_t = starts_of(base + tile * TILE)
        key_t = base + lax.broadcasted_iota(jnp.int32, (own_count(tile), 1), 0)
        s = jnp.where((key_t >= row_start) & (key_t <= row_t), s, LOW)
        keep(tile, g, absorb(None, s, flipped_ref[g, :, : own_count(tile)]))

    if begin:
        staggered(
            [(tile, g) for tile in range(tiles) for g in range(kv_heads)], own_scores, own_finish
        )
    else:
        stat_ref[...] = stat_in[...]
        mixed_ref[...] = mixed_in[...]

    together = math.gcd(tiles, TOGETHER)
    for number in range(1 if begin else 0, len(spans)):
        start, _ = limits(number)
        at, count = ats[number], spans[number][1]

        @pl.loop(0, (counts[number] + together - 1) // together)
        def _(turn, start=start, at=at, count=count):
            def scores(n, g):
                q = stacked_queries(q_ref, turn * together + n, g, group)
                return scores_of(keys_ref[g, at : at + count], q)

            def finish(n, g, s):
                tile = turn * together + n
                row_start, _ = starts_of(base + tile * TILE)
                key_t = start + lax.broadcasted_iota(jnp.int32, (count, 1), 0)
                s = jnp.where(key_t >= row_start, s, LOW)
                old = stat_ref[tile, g, 0:1, :], stat_ref[tile, g, 1:2, :], mixed_ref[tile, g]
                keep(tile, g, absorb(old, s, flipped_ref[g, :, at : at + count]))

            staggered(
                [(n, g) for n in range(together) for g in range(kv_heads)], scores, finish
            )

    for tile in range(tiles if end else 0):
        for g in range(kv_heads):
            write_heads(out_ref, mixed_ref[tile, g], stat_ref[tile, g, 1:2, :], tile, g, group)


def cross_kernel(
    lengths_ref, images_ref, place_ref, q_ref, *refs, kv_heads, group, sources, samples, begin, end
):
    refs = list(refs)
    take = lambda n: [refs.pop(0) for _ in range(n)]
    pieces = [take(len(source)) for source in sources]
    stat_in, mixed_in = (None, None) if begin else take(2)
    out_ref = take(1)[0] if end else None
    stat_ref, mixed_ref, keys_ref, flipped_ref = take(4)
    rows_ref, copied = take(2) if end else (None, None)
    (mixed_tiles_ref,) = take(1)
    rows_here = q_ref.shape[0]
    tiles = rows_here // TILE
    height = group * TILE
    base = place_ref[0] * rows_here
    starts, _ = sample_bounds(lengths_ref, samples)
    image_count = keys_ref.shape[0]

    def fill(ref, at, parts, each, only):
        for n in range(kv_heads):
            if only not in (None, n):
                continue
            k_at = n * HD if only is None else 0
            v_at = k_at + ref.shape[1] // 2
            for image in range(image_count):
                values = []
                for part in range(parts):
                    first = (part * image_count + image) * each
                    here = slice(at + part * each, at + (part + 1) * each)
                    keys_ref[image, n, here] = ref[first : first + each, k_at : k_at + HD]
                    values.append(ref[first : first + each, v_at : v_at + HD])
                whole = jnp.concatenate(values, axis=0)
                flipped_ref[image, n, :, at : at + parts * each] = whole.T

    at = 0
    for source, given in zip(sources, pieces):
        for number, ((parts, each, only), ref) in enumerate(zip(source, given)):
            put = functools.partial(fill, ref, at, parts, each, only)
            if len(source) == 1:
                put()
            else:
                pl.when(place_ref[1] == 1 - number)(put)
        if source[0][2] in (None, kv_heads - 1):
            at += source[0][0] * source[0][1]

    def images_of(tile):
        first = base + tile * TILE
        row_t = row_positions(first, height)
        row_image = jnp.zeros((1, height), jnp.int32)
        leading = jnp.int32(0)
        for j in range(samples):
            row_image = jnp.where(row_t >= starts[j], images_ref[0, j], row_image)
            leading = jnp.where(first >= starts[j], images_ref[0, j], leading)
        return row_image, leading

    def keep(tile, g, state):
        stat_ref[tile, g, 0:1, :] = state[0]
        stat_ref[tile, g, 1:2, :] = state[1]
        mixed_ref[tile, g] = state[2]

    def chosen(mine, new, old):
        if old is None:
            old = LOW, 0.0, 0.0
        return [jnp.where(mine, n, o) for n, o in zip(new, old)]

    marks = [images_of(tile) for tile in range(tiles)]
    for tile in range(tiles):
        first = base + tile * TILE
        second = jnp.int32(0)
        for j in range(samples):
            inside = (starts[j] > first) & (starts[j] < first + TILE)
            second = jnp.where(inside & (images_ref[0, j] != marks[tile][1]), 1, second)
        mixed_tiles_ref[tile] = second
    order = range(kv_heads)

    def scores(tile, n):
        return scores_of(
            keys_ref[marks[tile][1], n], stacked_queries(q_ref, tile, n, group)
        )

    def finish(tile, n, s):
        row_image, leading = marks[tile]
        old = None
        if not begin:
            old = stat_in[tile, n, 0:1, :], stat_in[tile, n, 1:2, :], mixed_in[tile, n]
        new = absorb(old, s, flipped_ref[leading, n])
        keep(tile, n, chosen(row_image == leading, new, old))

    staggered([(tile, n) for tile in range(tiles) for n in order], scores, finish)

    def second_images(tile):
        first = base + tile * TILE
        leading, others = jnp.int32(0), [jnp.bool_(False)] * image_count
        for j in range(samples):
            leading = jnp.where(first >= starts[j], images_ref[0, j], leading)
        for j in range(samples):
            inside = (starts[j] > first) & (starts[j] < first + TILE)
            for image in range(image_count):
                others[image] = others[image] | (inside & (images_ref[0, j] == image))
        for image in range(image_count):

            @pl.when(others[image] & (leading != image))
            def _(image=image):
                row_image, _ = images_of(tile)
                olds = [
                    (stat_ref[tile, n, 0:1, :], stat_ref[tile, n, 1:2, :], mixed_ref[tile, n])
                    for n in order
                ]
                ss = [
                    scores_of(keys_ref[image, n], stacked_queries(q_ref, tile, n, group))
                    for n in order
                ]
                for n in order:
                    new = absorb(olds[n], ss[n], flipped_ref[image, n])
                    keep(tile, n, chosen(row_image == image, new, olds[n]))

    @pl.loop(0, tiles)
    def _(tile):
        pl.when(mixed_tiles_ref[tile] == 1)(functools.partial(second_images, tile))

    if not end:
        return
    pace = 2
    copies = []
    for tile in range(tiles):
        for n in order:
            write_heads(rows_ref, mixed_ref[tile, n], stat_ref[tile, n, 1:2, :], tile, n, group)
        if (tile + 1) % pace == 0 or tile + 1 == tiles:
            done = slice(len(copies) * pace * TILE, (tile + 1) * TILE)
            copy = pltpu.make_async_copy(
                rows_ref.at[done], out_ref.at[done], copied.at[len(copies)]
            )
            copy.start()
            copies.append(copy)
    for copy in copies:
        copy.wait()


def smem():
    return pl.BlockSpec(memory_space=pltpu.SMEM)


def vmem():
    return pl.BlockSpec(memory_space=pltpu.VMEM)


def cost(rows, width, keys):
    return pl.CostEstimate(
        flops=8 * rows * width * keys, bytes_accessed=4 * rows * width,
        transcendentals=rows * (width // HD) * keys,
    )


def state_shapes(rows, kv_heads, group):
    tiles, height = rows // TILE, group * TILE
    return (tiles, kv_heads, 8, height), (tiles, kv_heads, HD, height)


def state_call(
    kernel, operands, rows, width, keys, shapes, scratch, end, dtype, placed=False
):
    scalars = sum(x.dtype == jnp.int32 for x in operands)
    state_scratch = []
    if end:
        out_shape = jax.ShapeDtypeStruct((rows, width), dtype)
        state_scratch = [pltpu.VMEM(s, jnp.float32) for s in shapes]
    else:
        out_shape = [jax.ShapeDtypeStruct(s, jnp.float32) for s in shapes]
    anywhere = pl.BlockSpec(memory_space=pl.ANY)
    in_specs = [smem()] * scalars + [vmem()] * (len(operands) - scalars)
    return pl.pallas_call(
        kernel,
        out_shape=out_shape,
        in_specs=in_specs,
        out_specs=(anywhere if placed else vmem()) if end else [vmem(), vmem()],
        scratch_shapes=state_scratch + scratch,
        compiler_params=pltpu.CompilerParams(vmem_limit_bytes=28 << 20),
        cost_estimate=cost(rows, width, keys),
    )(*operands)


def self_attention(lengths, place, q, pieces, spans, parts, state, end, kv_heads, group):
    rows, width = q.shape
    keys = sum(count for _, count in spans)
    begin = state is None
    kernel = functools.partial(
        self_kernel, kv_heads=kv_heads, group=group, spans=spans, parts=parts,
        samples=lengths.shape[1], begin=begin, end=end,
    )
    scratch = [
        pltpu.VMEM((kv_heads, keys, HD), q.dtype), pltpu.VMEM((kv_heads, HD, keys), q.dtype)
    ]
    operands = (lengths, place, q, *pieces, *(() if begin else state))
    shapes = state_shapes(rows, kv_heads, group)
    return state_call(kernel, operands, rows, width, keys, shapes, scratch, end, q.dtype)


def cross_attention(lengths, images, place, q, sources, state, end, kv_heads, group, image_count):
    rows, width = q.shape
    begin = state is None
    kernel = functools.partial(
        cross_kernel, kv_heads=kv_heads, group=group,
        sources=tuple(tuple(piece[1:] for piece in source) for source in sources),
        samples=lengths.shape[1], begin=begin, end=end,
    )
    pieces = [piece[0] for source in sources for piece in source]
    keys = sum(s[0][1] * s[0][2] for s in sources if s[0][3] in (None, 0))
    scratch = [
        pltpu.VMEM((image_count, kv_heads, keys, HD), q.dtype),
        pltpu.VMEM((image_count, kv_heads, HD, keys), q.dtype),
    ]
    if end:
        scratch += [pltpu.VMEM((rows, width), q.dtype), pltpu.SemaphoreType.DMA((rows // TILE,))]
    scratch.append(pltpu.SMEM((rows // TILE,), jnp.int32))
    operands = (lengths, images, place, q, *pieces, *(() if begin else state))
    shapes = state_shapes(rows, kv_heads, group)
    return state_call(kernel, operands, rows, width, keys, shapes, scratch, end, q.dtype, True)


def per_device(q_self, kv_self, q_cross, kv_cross, sample_lengths, sample_image, *, n_pipe, n_ctx):
    rows = q_self.shape[1]
    kv_heads = kv_self.shape[3] // HD
    group = q_self.shape[2] // HD // kv_heads
    image_count, each = kv_cross.shape[1:3]
    z = lax.axis_index("ctx")
    inner = ((z == 1) | (z == 2)).astype(jnp.int32)
    place = jnp.stack([z, inner]).astype(jnp.int32)

    shift = lambda piece, step: lax.ppermute(
        piece, "ctx", [(c, c + 1) for c in range(step - 1, n_ctx - 1)]
    )
    passed = shift(kv_self[0], 1)
    arrived = lax.all_to_all(kv_cross, "pipe", split_axis=0, concat_axis=0, tiled=True)
    arrived, passed = lax.optimization_barrier((arrived, passed))
    flat = lambda array: array.reshape(-1, array.shape[-2] * array.shape[-1])
    own = flat(kv_self)
    longest = rows * n_ctx * 5 // 8

    attend_self = functools.partial(
        self_attention, sample_lengths, place, q_self[0], kv_heads=kv_heads, group=group
    )
    attend_cross = functools.partial(
        cross_attention, sample_lengths, sample_image, place, q_cross[0],
        kv_heads=kv_heads, group=group, image_count=image_count,
    )
    if n_ctx == 4:
        half = rows // 2
        at = lambda array, head=None: (array, n_pipe, each, head)
        near = lax.ppermute(arrived, "ctx", [(1, 2), (2, 1)])
        pair = lax.ppermute(arrived, "ctx", [(0, 1), (1, 0), (2, 3), (3, 2)])
        state = attend_cross([[at(flat(arrived))]], None, False)
        passed, state = lax.optimization_barrier((passed, state))
        two_back = lax.ppermute(passed, "ctx", [(1, 2), (2, 3)])
        three_back = lax.ppermute(passed[half:], "ctx", [(1, 3)])
        early = ((0, rows), (1, rows))
        parts = ((0, 0, 0, 0, rows, None), (1, 1, 0, 0, rows, None))
        self_state = attend_self([own, flat(passed)], early, parts, None, False)
        near, state = lax.optimization_barrier((near, state))
        pair, two_back, three_back, self_state = lax.optimization_barrier(
            (pair, two_back, three_back, self_state)
        )

        near = flat(near)
        near_on = lax.ppermute(near, "ctx", [(1, 0), (2, 3)])
        far = [
            lax.ppermute(flat(pair[..., g * HD : (g + 1) * HD]), "ctx", [(1, 2), (2, 1)])
            for g in range(kv_heads)
        ]
        state = attend_cross([[at(flat(pair))]], state, False)
        far[0], state = lax.optimization_barrier((far[0], state))
        late = ((2, rows), (3, half))
        parts = ((0, 0, 0, 0, rows, None), (1, 1, 0, 0, half, 3))
        self_out = attend_self([flat(two_back), flat(three_back)], late, parts, self_state, True)
        far_on = [lax.ppermute(part, "ctx", [(1, 0), (2, 3)]) for part in far]
        state = attend_cross([[at(near), at(near_on)]], state, False)
        last = [[at(far[g], g), at(far_on[g], g)] for g in range(kv_heads)]
        cross_out = attend_cross(last, state, True)
    else:
        pieces, spans = [own, flat(passed)], [(0, rows), (1, rows)]
        left, step = longest - 1 - rows, 1
        while left > 0 and step < n_ctx - 1:
            step += 1
            count = min(rows, -(-left // HD) * HD)
            pieces.append(shift(pieces[-1][rows - count :], step))
            spans.append((step, count))
            left -= rows
        parts = tuple((n, n, 0, 0, count, None) for n, (_, count) in enumerate(spans))
        self_out = attend_self(pieces, tuple(spans), parts, None, True)
        gathered = lax.all_gather(flat(arrived), "ctx", axis=0, tiled=True)
        cross_out = attend_cross([[(gathered, n_ctx * n_pipe, each, None)]], None, True)
    return self_out[None], cross_out[None]


def solution(mesh):
    in_specs = (
        P("pipe", "ctx", "tp"),
        P("pipe", "ctx", None, "tp"),
        P("pipe", "ctx", "tp"),
        P(None, None, ("pipe", "ctx"), None, "tp"),
        P("pipe", None),
        P("pipe", None),
    )
    out_specs = (P("pipe", "ctx", "tp"), P("pipe", "ctx", "tp"))
    body = functools.partial(
        per_device, n_pipe=mesh.shape["pipe"], n_ctx=mesh.shape["ctx"]
    )
    return jax.shard_map(
        body, mesh=mesh, in_specs=in_specs, out_specs=out_specs, check_vma=False
    )
```

```python
import functools
import math

import jax
import jax.numpy as jnp
from jax import lax
from jax.experimental import pallas as pl
from jax.experimental.pallas import tpu as pltpu
from jax.sharding import PartitionSpec as P

HD = 128
ONES = 16
TILE = 32
TOGETHER = 4
LOW = -1e30
EXP_SCALE = math.log2(math.e) / math.sqrt(HD)
NT = (((1,), (1,)), ((), ()))
NN = (((1,), (0,)), ((), ()))


def sample_bounds(lengths_ref, count):
    starts, ends, total = [], [], jnp.int32(0)
    for j in range(count):
        starts.append(total)
        total = total + lengths_ref[0, j]
        ends.append(total)
    return starts, ends


def stacked_queries(q_ref, tile, g, group):
    first = g * group
    rows = pl.ds(tile * TILE, TILE)
    return jnp.concatenate(
        [q_ref[rows, (first + h) * HD : (first + h + 1) * HD] for h in range(group)], axis=0
    )


def write_heads(out_ref, mixed, total, tile, g, group):
    rows = (mixed * (1.0 / total)).T.astype(out_ref.dtype)
    for h in range(group):
        at = (g * group + h) * HD
        out_ref[pl.ds(tile * TILE, TILE), at : at + HD] = rows[h * TILE : (h + 1) * TILE]


def scores_of(keys, q):
    return lax.dot_general(keys, q, NT, preferred_element_type=jnp.float32)


def absorb(state, s, v):
    if state is None:
        new_top = jnp.max(s, axis=0, keepdims=True)
    else:
        top, total, mixed = state
        new_top = jnp.maximum(top, jnp.max(s, axis=0, keepdims=True))
    w = jnp.exp2((s - new_top) * EXP_SCALE)
    product = lax.dot_general(v, w.astype(jnp.bfloat16), NN, preferred_element_type=jnp.float32)
    added, product = product[HD : HD + 1], product[:HD]
    if state is None:
        return new_top, added, product
    decay = jnp.exp2((top - new_top) * EXP_SCALE)
    return new_top, total * decay + added, mixed * decay + product


def staggered(units, score, finish):
    waiting = None
    for unit in units:
        s = score(*unit)
        if waiting is not None:
            finish(*waiting)
        waiting = (*unit, s)
    finish(*waiting)


def row_positions(first, height):
    return first + (lax.broadcasted_iota(jnp.int32, (1, height), 1) & (TILE - 1))


def lay(keys_at, flipped_at, ref, rows, kv_heads, g):
    keys_at[...] = ref[rows, g * HD : (g + 1) * HD]
    flipped_at[...] = ref[rows, (kv_heads + g) * HD : (kv_heads + g + 1) * HD].T


def self_kernel(
    lengths_ref, place_ref, q_ref, *refs, kv_heads, group, spans, parts, samples, begin, end
):
    refs = list(refs)
    take = lambda n: [refs.pop(0) for _ in range(n)]
    pieces = take(len({part[1] for part in parts}))
    stat_in, mixed_in = (None, None) if begin else take(2)
    out_ref = take(1)[0] if end else None
    stat_ref, mixed_ref, keys_ref, flipped_ref = take(4)
    ones_at = flipped_ref.shape[:-2] + (ONES, flipped_ref.shape[-1])
    flipped_ref[..., HD:, :] = jnp.ones(ones_at, flipped_ref.dtype)
    rows_here = q_ref.shape[0]
    tiles = rows_here // TILE
    height = group * TILE
    base = place_ref[0] * rows_here
    _, ends = sample_bounds(lengths_ref, samples)
    ats = [sum(count for _, count in spans[:n]) for n in range(len(spans))]

    lows = []
    for tile in range(tiles):
        low = jnp.int32(0)
        for e in ends:
            low = jnp.where(e <= base + tile * TILE, e, low)
        lows.append(low)

    def limits(number):
        back, count = spans[number]
        past = base - (back - 1) * rows_here
        return past - count, past

    def reached(number):
        start, past = limits(number)
        many = jnp.int32(0)
        for low in lows:
            many = many + (low < past).astype(jnp.int32)
        return jnp.where(start >= 0, many, 0)

    counts = [reached(number) for number in range(len(spans))]
    for number, source, at, offset, count, only in parts:

        def fill(number=number, source=source, at=at, offset=offset, count=count):
            here = slice(ats[number] + offset, ats[number] + offset + count)
            for g in range(kv_heads):
                lay(
                    keys_ref.at[g, here], flipped_ref.at[g, :HD, here], pieces[source],
                    slice(at, at + count), kv_heads, g,
                )

        if spans[number][0] == 0:
            fill()
        else:
            asked = counts[number] > 0
            if only is not None:
                asked = asked & (place_ref[0] == only)
            pl.when(asked)(fill)

    def starts_of(first):
        row_t = row_positions(first, height)
        row_start = jnp.zeros((1, height), jnp.int32)
        for e in ends:
            row_start = jnp.where(e <= row_t, e, row_start)
        return row_start, row_t

    def keep(tile, g, state):
        stat_ref[tile, g, 0:1, :] = state[0]
        stat_ref[tile, g, 1:2, :] = state[1]
        mixed_ref[tile, g] = state[2]

    def own_count(tile):
        return min(rows_here, -(-(tile + 1) * TILE // HD) * HD)

    def own_scores(tile, g):
        q = stacked_queries(q_ref, tile, g, group)
        return scores_of(keys_ref[g, : own_count(tile)], q)

    def own_finish(tile, g, s):
        row_start, row_t = starts_of(base + tile * TILE)
        key_t = base + lax.broadcasted_iota(jnp.int32, (own_count(tile), 1), 0)
        s = jnp.where((key_t >= row_start) & (key_t <= row_t), s, LOW)
        keep(tile, g, absorb(None, s, flipped_ref[g, :, : own_count(tile)]))

    if begin:
        staggered(
            [(tile, g) for tile in range(tiles) for g in range(kv_heads)], own_scores, own_finish
        )
    else:
        stat_ref[...] = stat_in[...]
        mixed_ref[...] = mixed_in[...]

    together = math.gcd(tiles, TOGETHER)
    for number in range(1 if begin else 0, len(spans)):
        start, _ = limits(number)
        at, count = ats[number], spans[number][1]

        @pl.loop(0, (counts[number] + together - 1) // together)
        def _(turn, start=start, at=at, count=count):
            def scores(n, g):
                q = stacked_queries(q_ref, turn * together + n, g, group)
                return scores_of(keys_ref[g, at : at + count], q)

            def finish(n, g, s):
                tile = turn * together + n
                row_start, _ = starts_of(base + tile * TILE)
                key_t = start + lax.broadcasted_iota(jnp.int32, (count, 1), 0)
                s = jnp.where(key_t >= row_start, s, LOW)
                old = stat_ref[tile, g, 0:1, :], stat_ref[tile, g, 1:2, :], mixed_ref[tile, g]
                keep(tile, g, absorb(old, s, flipped_ref[g, :, at : at + count]))

            staggered(
                [(n, g) for n in range(together) for g in range(kv_heads)], scores, finish
            )

    for tile in range(tiles if end else 0):
        for g in range(kv_heads):
            write_heads(out_ref, mixed_ref[tile, g], stat_ref[tile, g, 1:2, :], tile, g, group)


def cross_kernel(
    lengths_ref, images_ref, place_ref, q_ref, *refs, kv_heads, group, sources, samples, begin, end
):
    refs = list(refs)
    take = lambda n: [refs.pop(0) for _ in range(n)]
    pieces = [take(len(source)) for source in sources]
    stat_in, mixed_in = (None, None) if begin else take(2)
    out_ref = take(1)[0] if end else None
    stat_ref, mixed_ref, keys_ref, flipped_ref = take(4)
    ones_at = flipped_ref.shape[:-2] + (ONES, flipped_ref.shape[-1])
    flipped_ref[..., HD:, :] = jnp.ones(ones_at, flipped_ref.dtype)
    rows_ref, copied = take(2) if end else (None, None)
    (mixed_tiles_ref,) = take(1)
    rows_here = q_ref.shape[0]
    tiles = rows_here // TILE
    height = group * TILE
    base = place_ref[0] * rows_here
    starts, _ = sample_bounds(lengths_ref, samples)
    image_count = keys_ref.shape[0]

    def fill(ref, at, parts, each, only):
        for n in range(kv_heads):
            if only not in (None, n):
                continue
            k_at = n * HD if only is None else 0
            v_at = k_at + ref.shape[1] // 2
            for image in range(image_count):
                values = []
                for part in range(parts):
                    first = (part * image_count + image) * each
                    here = slice(at + part * each, at + (part + 1) * each)
                    keys_ref[image, n, here] = ref[first : first + each, k_at : k_at + HD]
                    values.append(ref[first : first + each, v_at : v_at + HD])
                whole = jnp.concatenate(values, axis=0)
                flipped_ref[image, n, :HD, at : at + parts * each] = whole.T

    at = 0
    for source, given in zip(sources, pieces):
        for number, ((parts, each, only), ref) in enumerate(zip(source, given)):
            put = functools.partial(fill, ref, at, parts, each, only)
            if len(source) == 1:
                put()
            else:
                pl.when(place_ref[1] == 1 - number)(put)
        if source[0][2] in (None, kv_heads - 1):
            at += source[0][0] * source[0][1]

    def images_of(tile):
        first = base + tile * TILE
        row_t = row_positions(first, height)
        row_image = jnp.zeros((1, height), jnp.int32)
        leading = jnp.int32(0)
        for j in range(samples):
            row_image = jnp.where(row_t >= starts[j], images_ref[0, j], row_image)
            leading = jnp.where(first >= starts[j], images_ref[0, j], leading)
        return row_image, leading

    def keep(tile, g, state):
        stat_ref[tile, g, 0:1, :] = state[0]
        stat_ref[tile, g, 1:2, :] = state[1]
        mixed_ref[tile, g] = state[2]

    def chosen(mine, new, old):
        if old is None:
            old = LOW, 0.0, 0.0
        return [jnp.where(mine, n, o) for n, o in zip(new, old)]

    marks = [images_of(tile) for tile in range(tiles)]
    for tile in range(tiles):
        first = base + tile * TILE
        second = jnp.int32(0)
        for j in range(samples):
            inside = (starts[j] > first) & (starts[j] < first + TILE)
            second = jnp.where(inside & (images_ref[0, j] != marks[tile][1]), 1, second)
        mixed_tiles_ref[tile] = second
    order = range(kv_heads)

    def scores(tile, n):
        return scores_of(
            keys_ref[marks[tile][1], n], stacked_queries(q_ref, tile, n, group)
        )

    def finish(tile, n, s):
        row_image, leading = marks[tile]
        old = None
        if not begin:
            old = stat_in[tile, n, 0:1, :], stat_in[tile, n, 1:2, :], mixed_in[tile, n]
        new = absorb(old, s, flipped_ref[leading, n])
        keep(tile, n, chosen(row_image == leading, new, old))

    staggered([(tile, n) for tile in range(tiles) for n in order], scores, finish)

    def second_images(tile):
        first = base + tile * TILE
        leading, others = jnp.int32(0), [jnp.bool_(False)] * image_count
        for j in range(samples):
            leading = jnp.where(first >= starts[j], images_ref[0, j], leading)
        for j in range(samples):
            inside = (starts[j] > first) & (starts[j] < first + TILE)
            for image in range(image_count):
                others[image] = others[image] | (inside & (images_ref[0, j] == image))
        for image in range(image_count):

            @pl.when(others[image] & (leading != image))
            def _(image=image):
                row_image, _ = images_of(tile)
                olds = [
                    (stat_ref[tile, n, 0:1, :], stat_ref[tile, n, 1:2, :], mixed_ref[tile, n])
                    for n in order
                ]
                ss = [
                    scores_of(keys_ref[image, n], stacked_queries(q_ref, tile, n, group))
                    for n in order
                ]
                for n in order:
                    new = absorb(olds[n], ss[n], flipped_ref[image, n])
                    keep(tile, n, chosen(row_image == image, new, olds[n]))

    @pl.loop(0, tiles)
    def _(tile):
        pl.when(mixed_tiles_ref[tile] == 1)(functools.partial(second_images, tile))

    if not end:
        return
    pace = 2
    copies = []
    for tile in range(tiles):
        for n in order:
            write_heads(rows_ref, mixed_ref[tile, n], stat_ref[tile, n, 1:2, :], tile, n, group)
        if (tile + 1) % pace == 0 or tile + 1 == tiles:
            done = slice(len(copies) * pace * TILE, (tile + 1) * TILE)
            copy = pltpu.make_async_copy(
                rows_ref.at[done], out_ref.at[done], copied.at[len(copies)]
            )
            copy.start()
            copies.append(copy)
    for copy in copies:
        copy.wait()


def smem():
    return pl.BlockSpec(memory_space=pltpu.SMEM)


def vmem():
    return pl.BlockSpec(memory_space=pltpu.VMEM)


def cost(rows, width, keys):
    return pl.CostEstimate(
        flops=8 * rows * width * keys, bytes_accessed=4 * rows * width,
        transcendentals=rows * (width // HD) * keys,
    )


def state_shapes(rows, kv_heads, group):
    tiles, height = rows // TILE, group * TILE
    return (tiles, kv_heads, 8, height), (tiles, kv_heads, HD, height)


def state_call(
    kernel, operands, rows, width, keys, shapes, scratch, end, dtype, placed=False
):
    scalars = sum(x.dtype == jnp.int32 for x in operands)
    state_scratch = []
    if end:
        out_shape = jax.ShapeDtypeStruct((rows, width), dtype)
        state_scratch = [pltpu.VMEM(s, jnp.float32) for s in shapes]
    else:
        out_shape = [jax.ShapeDtypeStruct(s, jnp.float32) for s in shapes]
    anywhere = pl.BlockSpec(memory_space=pl.ANY)
    in_specs = [smem()] * scalars + [vmem()] * (len(operands) - scalars)
    return pl.pallas_call(
        kernel,
        out_shape=out_shape,
        in_specs=in_specs,
        out_specs=(anywhere if placed else vmem()) if end else [vmem(), vmem()],
        scratch_shapes=state_scratch + scratch,
        compiler_params=pltpu.CompilerParams(vmem_limit_bytes=28 << 20),
        cost_estimate=cost(rows, width, keys),
    )(*operands)


def self_attention(lengths, place, q, pieces, spans, parts, state, end, kv_heads, group):
    rows, width = q.shape
    keys = sum(count for _, count in spans)
    begin = state is None
    kernel = functools.partial(
        self_kernel, kv_heads=kv_heads, group=group, spans=spans, parts=parts,
        samples=lengths.shape[1], begin=begin, end=end,
    )
    scratch = [
        pltpu.VMEM((kv_heads, keys, HD), q.dtype), pltpu.VMEM((kv_heads, HD + ONES, keys), q.dtype)
    ]
    operands = (lengths, place, q, *pieces, *(() if begin else state))
    shapes = state_shapes(rows, kv_heads, group)
    return state_call(kernel, operands, rows, width, keys, shapes, scratch, end, q.dtype)


def cross_attention(lengths, images, place, q, sources, state, end, kv_heads, group, image_count):
    rows, width = q.shape
    begin = state is None
    kernel = functools.partial(
        cross_kernel, kv_heads=kv_heads, group=group,
        sources=tuple(tuple(piece[1:] for piece in source) for source in sources),
        samples=lengths.shape[1], begin=begin, end=end,
    )
    pieces = [piece[0] for source in sources for piece in source]
    keys = sum(s[0][1] * s[0][2] for s in sources if s[0][3] in (None, 0))
    scratch = [
        pltpu.VMEM((image_count, kv_heads, keys, HD), q.dtype),
        pltpu.VMEM((image_count, kv_heads, HD + ONES, keys), q.dtype),
    ]
    if end:
        scratch += [pltpu.VMEM((rows, width), q.dtype), pltpu.SemaphoreType.DMA((rows // TILE,))]
    scratch.append(pltpu.SMEM((rows // TILE,), jnp.int32))
    operands = (lengths, images, place, q, *pieces, *(() if begin else state))
    shapes = state_shapes(rows, kv_heads, group)
    return state_call(kernel, operands, rows, width, keys, shapes, scratch, end, q.dtype, True)


def per_device(q_self, kv_self, q_cross, kv_cross, sample_lengths, sample_image, *, n_pipe, n_ctx):
    rows = q_self.shape[1]
    kv_heads = kv_self.shape[3] // HD
    group = q_self.shape[2] // HD // kv_heads
    image_count, each = kv_cross.shape[1:3]
    z = lax.axis_index("ctx")
    inner = ((z == 1) | (z == 2)).astype(jnp.int32)
    place = jnp.stack([z, inner]).astype(jnp.int32)

    shift = lambda piece, step: lax.ppermute(
        piece, "ctx", [(c, c + 1) for c in range(step - 1, n_ctx - 1)]
    )
    passed = shift(kv_self[0], 1)
    arrived = lax.all_to_all(kv_cross, "pipe", split_axis=0, concat_axis=0, tiled=True)
    arrived, passed = lax.optimization_barrier((arrived, passed))
    flat = lambda array: array.reshape(-1, array.shape[-2] * array.shape[-1])
    own = flat(kv_self)
    longest = rows * n_ctx * 5 // 8

    attend_self = functools.partial(
        self_attention, sample_lengths, place, q_self[0], kv_heads=kv_heads, group=group
    )
    attend_cross = functools.partial(
        cross_attention, sample_lengths, sample_image, place, q_cross[0],
        kv_heads=kv_heads, group=group, image_count=image_count,
    )
    if n_ctx == 4:
        half = rows // 2
        at = lambda array, head=None: (array, n_pipe, each, head)
        near = lax.ppermute(arrived, "ctx", [(1, 2), (2, 1)])
        pair = lax.ppermute(arrived, "ctx", [(0, 1), (1, 0), (2, 3), (3, 2)])
        state = attend_cross([[at(flat(arrived))]], None, False)
        passed, state = lax.optimization_barrier((passed, state))
        two_back = lax.ppermute(passed, "ctx", [(1, 2), (2, 3)])
        three_back = lax.ppermute(passed[half:], "ctx", [(1, 3)])
        early = ((0, rows), (1, rows))
        parts = ((0, 0, 0, 0, rows, None), (1, 1, 0, 0, rows, None))
        self_state = attend_self([own, flat(passed)], early, parts, None, False)
        near, state = lax.optimization_barrier((near, state))
        pair, two_back, three_back, self_state = lax.optimization_barrier(
            (pair, two_back, three_back, self_state)
        )

        near = flat(near)
        near_on = lax.ppermute(near, "ctx", [(1, 0), (2, 3)])
        far = [
            lax.ppermute(flat(pair[..., g * HD : (g + 1) * HD]), "ctx", [(1, 2), (2, 1)])
            for g in range(kv_heads)
        ]
        state = attend_cross([[at(flat(pair))]], state, False)
        far[0], state = lax.optimization_barrier((far[0], state))
        late = ((2, rows), (3, half))
        parts = ((0, 0, 0, 0, rows, None), (1, 1, 0, 0, half, 3))
        self_out = attend_self([flat(two_back), flat(three_back)], late, parts, self_state, True)
        far_on = [lax.ppermute(part, "ctx", [(1, 0), (2, 3)]) for part in far]
        state = attend_cross([[at(near), at(near_on)]], state, False)
        last = [[at(far[g], g), at(far_on[g], g)] for g in range(kv_heads)]
        cross_out = attend_cross(last, state, True)
    else:
        pieces, spans = [own, flat(passed)], [(0, rows), (1, rows)]
        left, step = longest - 1 - rows, 1
        while left > 0 and step < n_ctx - 1:
            step += 1
            count = min(rows, -(-left // HD) * HD)
            pieces.append(shift(pieces[-1][rows - count :], step))
            spans.append((step, count))
            left -= rows
        parts = tuple((n, n, 0, 0, count, None) for n, (_, count) in enumerate(spans))
        self_out = attend_self(pieces, tuple(spans), parts, None, True)
        gathered = lax.all_gather(flat(arrived), "ctx", axis=0, tiled=True)
        cross_out = attend_cross([[(gathered, n_ctx * n_pipe, each, None)]], None, True)
    return self_out[None], cross_out[None]


def solution(mesh):
    in_specs = (
        P("pipe", "ctx", "tp"),
        P("pipe", "ctx", None, "tp"),
        P("pipe", "ctx", "tp"),
        P(None, None, ("pipe", "ctx"), None, "tp"),
        P("pipe", None),
        P("pipe", None),
    )
    out_specs = (P("pipe", "ctx", "tp"), P("pipe", "ctx", "tp"))
    body = functools.partial(
        per_device, n_pipe=mesh.shape["pipe"], n_ctx=mesh.shape["ctx"]
    )
    return jax.shard_map(
        body, mesh=mesh, in_specs=in_specs, out_specs=out_specs, check_vma=False
    )
```
